768 devices in a mesh: gx: 12 (over z_lo, core), gy: 64 (over y, z_hi, x).
Axes of the slice: x: 4, y: 8, z: 12 (z_hi: 2, z_lo: 6; z = z_hi * 6 + z_lo), core: 2. Of those that a mesh axis runs over, the one named last changes fastest.
Arguments:
- fluid_state: float32 [6, 3, 192, 8192], P(None, None, 'gx', 'gy'), may hold values from -1.875 to 10.7, as said below
- switch: int32 [3, 192, 8192], P(None, 'gx', 'gy'), may hold values 0 or 1
- z_edges: float32 [2, 6, 3, 192, 8192], P(None, None, None, 'gx', 'gy'), may hold values from -1.875 to 10.7, as said below
- forcing: float32 [3, 3, 192, 8192], P(None, None, 'gx', 'gy'), may hold values from -3 to 3
Outputs:
- updated: float32 [6, 3, 192, 8192], P(None, None, 'gx', 'gy')
The draws below stay inside these ranges and needn't reach their ends.
Inputs may be any that keep to these rules, and one draw needn't show every extreme that they name: `fluid_state`: density lies in 0.7 to 1.4; total energy minus kinetic energy lies in 1 to 3 in every cell, and so does the internal-energy field. `z_edges`: the same law as the window state.
All inputs are finite; a program needn't handle non-finite values. No bound on the sum of `switch` on one device may be relied on, other than what follows from the above.
Results may differ from the reference program's by a relative error of at most 0.0003.
Values sent between devices are 32-bit elements; how exact they have to be, the bound alone decides.
No kernel may reach another device: no remote copies, remote signals or barrier semaphores. Data moves between devices by JAX's collectives and lax.ppermute only.
A program may use at most 32 MiB of HBM per device.

```python
import jax
import jax.numpy as jnp
from jax import lax

CY = 128
NX = 192
NY = 8192
N_GY = 64


def fluid_law(key, noise_field, planes):
    key_density, key_heat, key_inner = jax.random.split(key, 3)
    grid_shape = (planes, NX, NY)
    x_frac = jnp.arange(NX, dtype=jnp.float32)[:, None] / NX
    y_frac = jnp.arange(NY, dtype=jnp.float32)[None, :] / NY
    ramp_field = jnp.power(3.0, 0.5 * (x_frac + y_frac))
    density = jnp.exp(jax.random.uniform(key_density, grid_shape, jnp.float32, jnp.log(0.7), jnp.log(1.4)))
    momenta = 0.25 * ramp_field * noise_field
    heat_draw = jnp.exp(jax.random.uniform(key_heat, grid_shape, jnp.float32, 0.0, jnp.log(3.0)))
    inner_heat = jnp.exp(jax.random.uniform(key_inner, grid_shape, jnp.float32, 0.0, jnp.log(3.0)))
    total_energy = heat_draw + 0.5 * (momenta[0] ** 2 + momenta[1] ** 2 + momenta[2] ** 2) / density
    return jnp.stack([density, momenta[0], momenta[1], momenta[2], total_energy, inner_heat])


def draw_fluid_state(key, part):
    key = jax.random.fold_in(key, 11)
    key_noise, key_rest = jax.random.split(key, 2)
    noise_field = jnp.clip(jax.random.normal(key_noise, (3, 3, NX, NY), jnp.float32), -2.5, 2.5)
    return fluid_law(key_rest, noise_field, 3)


def draw_z_edges(key, part):
    key = jax.random.fold_in(key, 23)
    key_noise, key_rest = jax.random.split(key, 2)
    noise_field = jnp.clip(jax.random.normal(key_noise, (3, 6, NX, NY), jnp.float32), -2.5, 2.5)
    stacked = fluid_law(key_rest, noise_field, 6)
    return stacked.reshape(6, 2, 3, NX, NY).transpose(1, 0, 2, 3, 4)


def draw_forcing(key, part):
    key = jax.random.fold_in(key, 37)
    x_frac = jnp.arange(NX, dtype=jnp.float32)[:, None] / NX
    y_frac = jnp.arange(NY, dtype=jnp.float32)[None, :] / NY
    ramp_field = jnp.power(10.0, x_frac + y_frac - 2.0)
    noise_field = jnp.clip(jax.random.normal(key, (3, 3, NX, NY), jnp.float32), -3.0, 3.0)
    return noise_field * ramp_field


def set_ends(array, key, low, top_value):
    longest = array.shape.index(max(array.shape))
    spots = []
    for shift in (0, 1):
        where = [jax.random.randint(jax.random.fold_in(key, axis), (), 0, length) for axis, length in enumerate(array.shape)]
        where[longest] = (where[longest] + shift) % array.shape[longest]
        spots.append(tuple(where))
    return array.at[spots[0]].set(low).at[spots[1]].set(top_value)


def setup_inputs(seed: int = 0) -> dict:
    arg_keys = jax.random.split(jax.random.key(seed), 5)
    fluid_state = draw_fluid_state(jax.random.fold_in(arg_keys[4], 71), 0)
    switch = set_ends((jax.random.randint(arg_keys[1], (3, NX, NY), 0, 3) < 1).astype(jnp.int32), jax.random.fold_in(arg_keys[1], 1), 0, 1)
    z_edges = draw_z_edges(jax.random.fold_in(arg_keys[4], 71), 0)
    forcing = draw_forcing(jax.random.fold_in(arg_keys[4], 71), 0)
    return {"fluid_state": fluid_state, "switch": switch, "z_edges": z_edges, "forcing": forcing}


ADIABATIC = 5.0 / 3.0
CFL_NUMBER = 0.4
INJECTION = 0.04

def kinetic(conserved):
    return 0.5 * (conserved[1] ** 2 + conserved[2] ** 2 + conserved[3] ** 2) / conserved[0]

def thermal(conserved, switch):
    return jnp.where(switch == 1, conserved[5], conserved[4] - kinetic(conserved))

def primitives(conserved, heat_field):
    density = conserved[0]
    return jnp.stack([density, conserved[1] / density, conserved[2] / density, conserved[3] / density, (ADIABATIC - 1.0) * heat_field, conserved[5] / density])

def signal_speed(conserved, heat_field):
    density = conserved[0]
    sound_speed = jnp.sqrt(ADIABATIC * (ADIABATIC - 1.0) * heat_field / density)
    return jnp.abs(conserved[1] / density) + jnp.abs(conserved[2] / density) + jnp.abs(conserved[3] / density) + 3.0 * sound_speed

def slab_of(values, begin, length, axis_dim):
    return lax.slice_in_dim(values, begin, begin + length, axis=axis_dim)

def edge_states(values, axis_dim):
    cell_count = values.shape[axis_dim] - 6
    face_value = (7.0 * (slab_of(values, 1, cell_count + 3, axis_dim) + slab_of(values, 2, cell_count + 3, axis_dim)) - (slab_of(values, 0, cell_count + 3, axis_dim) + slab_of(values, 3, cell_count + 3, axis_dim))) / 12.0
    bound_low = jnp.minimum(slab_of(values, 1, cell_count + 3, axis_dim), slab_of(values, 2, cell_count + 3, axis_dim))
    bound_high = jnp.maximum(slab_of(values, 1, cell_count + 3, axis_dim), slab_of(values, 2, cell_count + 3, axis_dim))
    face_value = jnp.minimum(jnp.maximum(face_value, bound_low), bound_high)
    center = slab_of(values, 2, cell_count + 2, axis_dim)
    below_dev = slab_of(face_value, 0, cell_count + 2, axis_dim) - center
    above_dev = slab_of(face_value, 1, cell_count + 2, axis_dim) - center
    opposite = below_dev * above_dev < 0.0
    left_dev = jnp.where(opposite, jnp.clip(below_dev, -2.0 * jnp.abs(above_dev), 2.0 * jnp.abs(above_dev)), 0.0)
    right_dev = jnp.where(opposite, jnp.clip(above_dev, -2.0 * jnp.abs(below_dev), 2.0 * jnp.abs(below_dev)), 0.0)
    left_edge = center + left_dev
    right_edge = center + right_dev
    return (slab_of(right_edge, 0, cell_count + 1, axis_dim), slab_of(left_edge, 1, cell_count + 1, axis_dim))

def physical(primitive, normal):
    density = primitive[0]
    pressure = primitive[4]
    normal_speed = primitive[1 + normal]
    energy = pressure / (ADIABATIC - 1.0) + 0.5 * density * (primitive[1] ** 2 + primitive[2] ** 2 + primitive[3] ** 2)
    conserved = jnp.stack([density, density * primitive[1], density * primitive[2], density * primitive[3], energy, density * primitive[5]])
    flux_value = conserved * normal_speed
    flux_value = flux_value.at[1 + normal].add(pressure)
    flux_value = flux_value.at[4].add(pressure * normal_speed)
    sound_speed = jnp.sqrt(ADIABATIC * pressure / density)
    return (conserved, flux_value, normal_speed, sound_speed)

def riemann_flux(left_state, right_state, normal):
    left_cons, left_flux, left_speed, left_sound = physical(left_state, normal)
    right_cons, right_flux, right_speed, right_sound = physical(right_state, normal)
    speed_low = jnp.minimum(jnp.minimum(left_speed - left_sound, right_speed - right_sound), 0.0)
    speed_high = jnp.maximum(jnp.maximum(left_speed + left_sound, right_speed + right_sound), 0.0)
    return (speed_high * left_flux - speed_low * right_flux + speed_low * speed_high * (right_cons - left_cons)) / (speed_high - speed_low)

def directional(primitive, axis_dim, normal):
    left_state, right_state = edge_states(primitive, axis_dim)
    flux_value = riemann_flux(left_state, right_state, normal)
    cell_count = primitive.shape[axis_dim] - 6
    difference = slab_of(flux_value, 1, cell_count, axis_dim) - slab_of(flux_value, 0, cell_count, axis_dim)
    velocity = primitive[1 + normal]
    spread = 0.5 * (slab_of(velocity, 4, cell_count, axis_dim - 1) - slab_of(velocity, 2, cell_count, axis_dim - 1))
    return (difference, spread)

def tendency(cons_pad, heat_pad, edge_below, edge_above, forcing, force_scale):
    row_strip = primitives(cons_pad[:, :, :, 3:-3], heat_pad[:, :, 3:-3])
    core_prim = row_strip[:, :, 3:-3, :]
    rim_low = primitives(cons_pad[:, :, 3:-3, :3], heat_pad[:, 3:-3, :3])
    rim_high = primitives(cons_pad[:, :, 3:-3, -3:], heat_pad[:, 3:-3, -3:])
    column_strip = jnp.concatenate([rim_low, core_prim, rim_high], axis=3)
    lower_prim = primitives(edge_below, edge_below[4] - kinetic(edge_below))
    upper_prim = primitives(edge_above, edge_above[4] - kinetic(edge_above))
    z_column = jnp.concatenate([lower_prim, core_prim, upper_prim], axis=1)
    flux_rows, spread_rows = directional(row_strip, 2, 0)
    flux_cols, spread_cols = directional(column_strip, 3, 1)
    flux_planes, spread_planes = directional(z_column, 1, 2)
    conserved = cons_pad[:, :, 3:-3, 3:-3]
    density = conserved[0]
    divergence = spread_rows + spread_cols + spread_planes
    momentum_push = force_scale * density * forcing
    power_term = force_scale * (conserved[1] * forcing[0] + conserved[2] * forcing[1] + conserved[3] * forcing[2])
    blank_field = jnp.zeros_like(density)
    source = jnp.stack([blank_field, momentum_push[0], momentum_push[1], momentum_push[2], power_term, -core_prim[4] * divergence])
    return source - (flux_rows + flux_cols + flux_planes)

def settle(conserved, switch):
    return conserved.at[5].set(jnp.where(switch == 0, conserved[4] - kinetic(conserved), conserved[5]))

def wrap_pad(values):
    widths = [(0, 0)] * (values.ndim - 2) + [(3, 3), (3, 3)]
    return jnp.pad(values, widths, mode='wrap')

def whole_tendency(conserved, heat_field, z_edges, forcing, force_scale):
    cons_pad = wrap_pad(conserved)
    heat_pad = wrap_pad(heat_field)

    def one_block(block_index):
        block_start = (block_index * CY).astype(jnp.int32)
        return tendency(lax.dynamic_slice_in_dim(cons_pad, block_start, CY + 6, 3), lax.dynamic_slice_in_dim(heat_pad, block_start, CY + 6, 2), lax.dynamic_slice_in_dim(z_edges[0], block_start, CY, 3), lax.dynamic_slice_in_dim(z_edges[1], block_start, CY, 3), lax.dynamic_slice_in_dim(forcing, block_start, CY, 3), force_scale)
    block_list = lax.map(one_block, jnp.arange(N_GY, dtype=jnp.int32))
    return jnp.moveaxis(block_list, 0, 3).reshape(6, 3, NX, NY)

def reference(fluid_state, switch, z_edges, forcing):
    heat_field = thermal(fluid_state, switch)
    peak_speed = jnp.max(signal_speed(fluid_state, heat_field))
    power_total = jnp.sum(fluid_state[0] * (forcing[0] ** 2 + forcing[1] ** 2 + forcing[2] ** 2))
    time_step = CFL_NUMBER / peak_speed
    force_scale = jnp.sqrt(INJECTION / (0.5 * time_step * (power_total / (3.0 * NX * NY) + 1e-06)))
    section_one = settle(fluid_state + time_step * whole_tendency(fluid_state, heat_field, z_edges, forcing, force_scale), switch)
    section_two = whole_tendency(section_one, thermal(section_one, switch), z_edges, forcing, force_scale)
    return settle(0.5 * fluid_state + 0.5 * (section_one + time_step * section_two), switch)
```

```python
import functools

import jax
import jax.numpy as jnp
from jax import lax
from jax.experimental import pallas as pl
from jax.experimental.pallas import tpu as pltpu
from jax.sharding import Mesh
from jax.sharding import PartitionSpec as P

ADIABATIC = 5.0 / 3.0
CFL_NUMBER = 0.4
INJECTION = 0.04
LANES = 128
ROWS = 16
EXT = 32
FIELDS = 21
EDGES = 36
FORCES = 9
X_TILES = FIELDS + EDGES + FORCES
VMEM_LIMIT = 16 * 1024 * 1024
F32 = jnp.float32


def lane_index(shape):
    return lax.broadcasted_iota(jnp.int32, shape, len(shape) - 1)


def roll(values, shift, axis):
    size = values.shape[axis]
    shift = shift % size
    return values if shift == 0 else pltpu.roll(values, shift, axis)


def source_tile(refs, index):
    state, switch, edges, forcing = refs
    if index < 18:
        return lambda rows: state[index // 3, index % 3, rows, :]
    index -= 18
    if index < 3:
        return lambda rows: switch[index, rows, :].astype(F32)
    index -= 3
    if index < EDGES:
        side, rest = divmod(index, 18)
        return lambda rows: edges[side, rest // 3, rest % 3, rows, :]
    index -= EDGES
    return lambda rows: forcing[index // 3, index % 3, rows, :]


def first_kernel(place, state, switch, edges, forcing, pair_out, odd_out):
    odd = place[0]
    near = pl.multiple_of(8 * (1 - odd), 8)
    far = pl.multiple_of(8 * odd, 8)
    refs = (state, switch, edges, forcing)
    peak = None
    total = None
    for plane in range(3):
        density = state[0, plane]
        inverse = 1.0 / density
        momenta = [state[1 + k, plane] for k in range(3)]
        kinetic = 0.5 * inverse * (momenta[0] ** 2 + momenta[1] ** 2 + momenta[2] ** 2)
        heat = jnp.where(switch[plane] == 1, state[5, plane], state[4, plane] - kinetic)
        sound = jnp.sqrt(ADIABATIC * (ADIABATIC - 1.0) * heat * inverse)
        speed = (
            jnp.abs(momenta[0]) + jnp.abs(momenta[1]) + jnp.abs(momenta[2])
        ) * inverse + 3.0 * sound
        power = density * (forcing[0, plane] ** 2 + forcing[1, plane] ** 2 + forcing[2, plane] ** 2)
        peak = speed if peak is None else jnp.maximum(peak, speed)
        total = power if total is None else total + power
    for index in range(X_TILES):
        tile = source_tile(refs, index)
        pair_out[index] = tile(pl.ds(near, 8))
        odd_out[index] = tile(pl.ds(far, 8))
    row = lax.broadcasted_iota(jnp.int32, (8, LANES), 0)
    pair_out[X_TILES] = jnp.where(row == 0, jnp.max(peak), jnp.sum(total))


def second_kernel(place, state, switch, edges, forcing, pair_in, odd_in, even_out, odd_out):
    odd_x = place[0]
    odd_y = place[1]
    refs = (state, switch, edges, forcing)
    lane = lane_index((EXT, LANES))
    high = jnp.zeros((EXT, LANES), F32)
    low = jnp.zeros((EXT, LANES), F32)
    for index in range(FIELDS):
        from_pair = pair_in[1 - odd_x, index]
        from_odd = odd_in[index]
        below = jnp.where(odd_x == 0, from_odd, from_pair)
        above = jnp.where(odd_x == 0, from_pair, from_odd)
        block = source_tile(refs, index)(slice(0, ROWS))
        column = jnp.concatenate([below, block, above], axis=0)
        mine = (lane >= 6 * index) & (lane < 6 * index + 6)
        high = jnp.where(mine, roll(column, 6 * index - 122, 1), high)
        low = jnp.where(mine, roll(column, 6 * index, 1), low)
    even_out[0:EXT] = jnp.where(odd_y == 0, high, low)
    odd_out[0:EXT] = jnp.where(odd_y == 0, low, high)
    lane = lane_index((ROWS, LANES))
    for begin, count, row in ((FIELDS, EDGES, EXT), (FIELDS + EDGES, FORCES, EXT + ROWS)):
        high = jnp.zeros((ROWS, LANES), F32)
        low = jnp.zeros((ROWS, LANES), F32)
        for index in range(count):
            block = source_tile(refs, begin + index)(slice(0, ROWS))
            mine = (lane >= 3 * index) & (lane < 3 * index + 3)
            high = jnp.where(mine, roll(block, 3 * index - 125, 1), high)
            low = jnp.where(mine, roll(block, 3 * index, 1), low)
        even_out[row : row + ROWS] = jnp.where(odd_y == 0, high, low)
        odd_out[row : row + ROWS] = jnp.where(odd_y == 0, low, high)


def face_above(before, here, after, beyond):
    value = (7.0 / 12.0) * (here + after) - (1.0 / 12.0) * (before + beyond)
    return jnp.minimum(
        jnp.maximum(value, jnp.minimum(here, after)), jnp.maximum(here, after)
    )


def limited(here, face_low, face_high):
    low_dev = face_low - here
    high_dev = face_high - here
    opposite = low_dev * high_dev < 0.0
    low_span = 2.0 * jnp.abs(low_dev)
    high_span = 2.0 * jnp.abs(high_dev)
    low_dev = jnp.minimum(jnp.maximum(low_dev, -high_span), high_span)
    high_dev = jnp.minimum(jnp.maximum(high_dev, -low_span), low_span)
    return jnp.where(opposite, here + low_dev, here), jnp.where(opposite, here + high_dev, here)


def face_flux(left, right, normal):
    left_u, right_u = left[1 + normal], right[1 + normal]
    left_sound = jnp.sqrt(ADIABATIC * left[4] / left[0])
    right_sound = jnp.sqrt(ADIABATIC * right[4] / right[0])
    slow = jnp.minimum(jnp.minimum(left_u - left_sound, right_u - right_sound), 0.0)
    fast = jnp.maximum(jnp.maximum(left_u + left_sound, right_u + right_sound), 0.0)
    share = 1.0 / (fast - slow)
    left_part = fast * share
    right_part = -slow * share
    left_rate = left_part * (left_u - slow)
    right_rate = right_part * (right_u - fast)
    left_mass = left_rate * left[0]
    right_mass = right_rate * right[0]
    left_square = left[1] * left[1] + left[2] * left[2] + left[3] * left[3]
    right_square = right[1] * right[1] + right[2] * right[2] + right[3] * right[3]
    flux = [left_mass + right_mass]
    for k in (1, 2, 3):
        flux.append(left_mass * left[k] + right_mass * right[k])
    left_push = left_part * left[4]
    right_push = right_part * right[4]
    flux[1 + normal] = flux[1 + normal] + (left_push + right_push)
    flux.append(
        0.5 * (left_mass * left_square + right_mass * right_square)
        + left[4] * (1.5 * left_rate)
        + right[4] * (1.5 * right_rate)
        + left_push * left_u
        + right_push * right_u
    )
    flux.append(left_mass * left[5] + right_mass * right[5])
    return flux


def z_fluxes(planes):
    lower, upper = [], []
    for k in range(6):
        column = [planes[j][k] for j in range(9)]
        faces = [face_above(*column[j : j + 4]) for j in range(6)]
        cells = [limited(column[j + 2], faces[j], faces[j + 1]) for j in range(5)]
        lower.append([cells[j][1] for j in range(4)])
        upper.append([cells[j + 1][0] for j in range(4)])
    return [
        face_flux([lower[k][j] for k in range(6)], [upper[k][j] for k in range(6)], 2)
        for j in range(4)
    ]


def edge_primitives(fields):
    density = fields[0]
    inverse = 1.0 / density
    kinetic = 0.5 * inverse * (fields[1] ** 2 + fields[2] ** 2 + fields[3] ** 2)
    return [
        density,
        fields[1] * inverse,
        fields[2] * inverse,
        fields[3] * inverse,
        (ADIABATIC - 1.0) * (fields[4] - kinetic),
        fields[5] * inverse,
    ]


def shift_pair(main, rim, step):
    lane = lane_index(main.shape)
    main_rolled = roll(main, -step, 1)
    rim_rolled = roll(rim, -step, 1)
    inside = lane < LANES - step if step > 0 else lane >= -step
    return (
        jnp.where(inside, main_rolled, rim_rolled),
        jnp.where(inside, rim_rolled, main_rolled),
    )


def y_differences(main, rim):
    lows, highs = ([], []), ([], [])
    spread = None
    for k in range(6):
        here = (main[k], rim[k])
        before = shift_pair(*here, -1)
        after = shift_pair(*here, 1)
        beyond = shift_pair(*here, 2)
        faces = [face_above(before[j], here[j], after[j], beyond[j]) for j in range(2)]
        below = shift_pair(*faces, -1)
        cells = [limited(here[j], below[j], faces[j]) for j in range(2)]
        nexts = shift_pair(cells[0][0], cells[1][0], 1)
        for j in range(2):
            lows[j].append(cells[j][1])
            highs[j].append(nexts[j])
        if k == 2:
            spread = [0.5 * (after[j] - before[j]) for j in range(2)]
    fluxes = [face_flux(lows[j], highs[j], 1) for j in range(2)]
    differences = ([], [])
    for k in range(6):
        below = shift_pair(fluxes[0][k], fluxes[1][k], -1)
        for j in range(2):
            differences[j].append(fluxes[j][k] - below[j])
    return differences, spread


CHUNKS = (4, 12, 20)


def x_sweep(prims, plane, chunks, low_ref, high_ref, flux_ref):
    for row in chunks:
        for k in range(6):
            rows = [prims[k, plane, pl.ds(row + s, 8), :] for s in (-2, -1, 0, 1, 2)]
            below = face_above(*rows[0:4])
            above = face_above(*rows[1:5])
            low_ref[k, pl.ds(row, 8), :], high_ref[k, pl.ds(row, 8), :] = limited(
                rows[2], below, above
            )
    for row in chunks:
        left = [high_ref[k, pl.ds(row, 8), :] for k in range(6)]
        right = [low_ref[k, pl.ds(row + 1, 8), :] for k in range(6)]
        flux = face_flux(left, right, 0)
        for k in range(6):
            flux_ref[k, pl.ds(row, 8), :] = flux[k]


def third_kernel(
    place, state, switch, edges, forcing, pair_in, odd_in, even_in, odd_y_in,
    fields, force, tend, prims, planes, low_ref, high_ref, flux_ref,
):
    odd_x = place[0]
    odd_y = place[1]
    refs = (state, switch, edges, forcing)
    lane = lane_index((EXT, LANES))
    above_strip = jnp.where(odd_y == 0, even_in[...], odd_y_in[...])
    below_strip = jnp.where(odd_y == 0, odd_y_in[...], even_in[...])

    def with_rows(index):
        from_pair = pair_in[1 - odd_x, index]
        from_odd = odd_in[index]
        below = jnp.where(odd_x == 0, from_odd, from_pair)
        above = jnp.where(odd_x == 0, from_pair, from_odd)
        block = source_tile(refs, index)(slice(0, ROWS))
        return jnp.concatenate([below, block, above], axis=0)

    for index in range(FIELDS):
        fields[0, index] = with_rows(index)
        fields[1, index] = jnp.where(
            lane < 64,
            roll(above_strip[0:EXT], -6 * index, 1),
            roll(below_strip[0:EXT], 122 - 6 * index, 1),
        )
    lane = lane_index((ROWS, LANES))
    rim_edges = []
    for begin, count, row in ((FIELDS, EDGES, EXT), (FIELDS + EDGES, FORCES, EXT + ROWS)):
        for index in range(count):
            rim = jnp.where(
                lane < 64,
                roll(above_strip[row : row + ROWS], -3 * index, 1),
                roll(below_strip[row : row + ROWS], 125 - 3 * index, 1),
            )
            if begin == FIELDS:
                rim_edges.append(rim)
            else:
                force[0, index] = with_rows(begin + index)
                force[1, index, 0:8] = jnp.zeros((8, LANES), F32)
                force[1, index, 8:24] = rim
                force[1, index, 24:32] = jnp.zeros((8, LANES), F32)

    for plane in range(3):
        for tile in range(2):
            values = [fields[tile, 3 * k + plane] for k in range(7)]
            density = values[0]
            inverse = 1.0 / density
            kinetic = 0.5 * inverse * (values[1] ** 2 + values[2] ** 2 + values[3] ** 2)
            heat = jnp.where(values[6] == 1.0, values[5], values[4] - kinetic)
            prims[tile, 0, plane] = density
            for k in (1, 2, 3):
                prims[tile, k, plane] = values[k] * inverse
            prims[tile, 4, plane] = (ADIABATIC - 1.0) * heat
            prims[tile, 5, plane] = values[5] * inverse
    for side in range(2):
        for plane in range(3):
            index = 18 * side + plane
            values = edge_primitives([with_rows(FIELDS + index + 3 * k) for k in range(6)])
            for k in range(6):
                planes[0, side, k, plane] = values[k]
            values = edge_primitives([rim_edges[index + 3 * k] for k in range(6)])
            for k in range(6):
                planes[1, side, k, plane, 0:8] = jnp.ones((8, LANES), F32)
                planes[1, side, k, plane, 8:24] = values[k]
                planes[1, side, k, plane, 24:32] = jnp.ones((8, LANES), F32)

    for plane in range(3):
        spreads = {}
        for row in CHUNKS:
            both = [
                [prims[tile, k, plane, pl.ds(row, 8), :] for k in range(6)] for tile in range(2)
            ]
            differences, spread = y_differences(*both)
            for tile in range(2):
                spreads[tile, row] = spread[tile]
                for k in range(6):
                    tend[tile, 3 * k + plane, pl.ds(row, 8), :] = -differences[tile][k]
        for tile in range(2):
            for k in range(6):
                low_ref[k, pl.ds(28, 4), :] = jnp.ones((4, LANES), F32)
                flux_ref[k, pl.ds(0, 4), :] = jnp.zeros((4, LANES), F32)
            x_sweep(prims.at[tile], plane, CHUNKS, low_ref, high_ref, flux_ref)
            for row in CHUNKS:
                for k in range(6):
                    difference = (
                        flux_ref[k, pl.ds(row, 8), :] - flux_ref[k, pl.ds(row - 1, 8), :]
                    )
                    tend[tile, 3 * k + plane, pl.ds(row, 8), :] -= difference
                before = prims[tile, 1, plane, pl.ds(row - 1, 8), :]
                after = prims[tile, 1, plane, pl.ds(row + 1, 8), :]
                spread = spreads[tile, row] + 0.5 * (after - before)
                below = prims[tile, 3, plane - 1, pl.ds(row, 8), :] if plane > 0 else (
                    planes[tile, 0, 3, 2, pl.ds(row, 8), :]
                )
                above = prims[tile, 3, plane + 1, pl.ds(row, 8), :] if plane < 2 else (
                    planes[tile, 1, 3, 0, pl.ds(row, 8), :]
                )
                spread = spread + 0.5 * (above - below)
                pressure = prims[tile, 4, plane, pl.ds(row, 8), :]
                tend[tile, 15 + plane, pl.ds(row, 8), :] -= pressure * spread
    for tile in range(2):
        for row in CHUNKS:
            rows = pl.ds(row, 8)
            column = (
                [[planes[tile, 0, k, p, rows, :] for k in range(6)] for p in range(3)]
                + [[prims[tile, k, p, rows, :] for k in range(6)] for p in range(3)]
                + [[planes[tile, 1, k, p, rows, :] for k in range(6)] for p in range(3)]
            )
            flux = z_fluxes(column)
            for plane in range(3):
                for k in range(6):
                    tend[tile, 3 * k + plane, rows, :] -= flux[plane + 1][k] - flux[plane][k]


def settled(values, switch):
    kinetic = 0.5 / values[0] * (values[1] ** 2 + values[2] ** 2 + values[3] ** 2)
    return jnp.where(switch == 0.0, values[4] - kinetic, values[5])


def fourth_kernel(
    cells, totals, fields, force, tend, edges, updated,
    section, prims, low_ref, high_ref, flux_ref,
):
    peak = jnp.max(totals[:, 0, :], axis=0, keepdims=True)
    power = jnp.sum(totals[:, 1, :], axis=0, keepdims=True)
    time_step = CFL_NUMBER / peak
    scale = jnp.sqrt(INJECTION / (0.5 * time_step * (power / cells + 1e-06)))

    def forced(values, force_values, tendency):
        result = list(tendency)
        for k in (1, 2, 3):
            result[k] = result[k] + scale * values[0] * force_values[k - 1]
        result[4] = result[4] + scale * (
            values[1] * force_values[0] + values[2] * force_values[1] + values[3] * force_values[2]
        )
        return result

    for plane in range(3):
        for tile in range(2):
            for row in CHUNKS:
                rows = pl.ds(row, 8)
                values = [fields[tile, 3 * k + plane, rows, :] for k in range(7)]
                drive = [force[tile, 3 * k + plane, rows, :] for k in range(3)]
                rate = forced(values, drive, [tend[tile, 3 * k + plane, rows, :] for k in range(6)])
                stage = [values[k] + time_step * rate[k] for k in range(6)]
                stage[5] = settled(stage, values[6])
                inverse = 1.0 / stage[0]
                if tile == 0:
                    for k in range(6):
                        section[k, plane, rows, :] = stage[k]
                prims[tile, 0, plane, rows, :] = stage[0]
                for k in (1, 2, 3):
                    prims[tile, k, plane, rows, :] = stage[k] * inverse
                prims[tile, 4, plane, rows, :] = (ADIABATIC - 1.0) * stage[5]
                prims[tile, 5, plane, rows, :] = stage[5] * inverse

    z_flux = []
    outer = {}
    for row in (8, 16):
        rows = pl.ds(row, 8)
        for side in range(2):
            for plane in range(3):
                outer[side, plane] = edge_primitives(
                    [edges[side, k, plane, pl.ds(row - 8, 8), :] for k in range(6)]
                )
        column = (
            [outer[0, p] for p in range(3)]
            + [[prims[0, k, p, rows, :] for k in range(6)] for p in range(3)]
            + [outer[1, p] for p in range(3)]
        )
        flux = z_fluxes(column)
        for plane in range(3):
            below = outer[0, 2][3] if plane == 0 else prims[0, 3, plane - 1, rows, :]
            above = outer[1, 0][3] if plane == 2 else prims[0, 3, plane + 1, rows, :]
            spread = 0.5 * (above - below)
            for k in range(6):
                updated[k, plane, pl.ds(row - 8, 8), :] = flux[plane][k] - flux[plane + 1][k]
            pressure = prims[0, 4, plane, rows, :]
            updated[5, plane, pl.ds(row - 8, 8), :] -= pressure * spread
    for plane in range(3):
        for k in range(6):
            low_ref[k, pl.ds(28, 4), :] = jnp.ones((4, LANES), F32)
        x_sweep(prims.at[0], plane, CHUNKS, low_ref, high_ref, flux_ref)
        for row in (8, 16):
            rows = pl.ds(row, 8)
            inner = pl.ds(row - 8, 8)
            both = [
                [prims[tile, k, plane, rows, :] for k in range(6)] for tile in range(2)
            ]
            differences, spread = y_differences(*both)
            before = prims[0, 1, plane, pl.ds(row - 1, 8), :]
            after = prims[0, 1, plane, pl.ds(row + 1, 8), :]
            spread = spread[0] + 0.5 * (after - before)
            rate = []
            for k in range(6):
                across = flux_ref[k, rows, :] - flux_ref[k, pl.ds(row - 1, 8), :]
                rate.append(updated[k, plane, inner, :] - differences[0][k] - across)
            rate[5] = rate[5] - both[0][4] * spread
            stage = [section[k, plane, rows, :] for k in range(6)]
            drive = [force[0, 3 * k + plane, rows, :] for k in range(3)]
            rate = forced(stage, drive, rate)
            values = [fields[0, 3 * k + plane, rows, :] for k in range(7)]
            result = [
                0.5 * values[k] + 0.5 * (stage[k] + time_step * rate[k]) for k in range(6)
            ]
            result[5] = settled(result, values[6])
            for k in range(6):
                updated[k, plane, inner, :] = result[k]


def shape(*sizes):
    return jax.ShapeDtypeStruct(sizes, F32)


def vmem_specs(count):
    return [pl.BlockSpec(memory_space=pltpu.VMEM)] * count


def call(kernel, name, outs, scalars, arrays, scratch=(), flops=0):
    single = not isinstance(outs, tuple)
    return pl.pallas_call(
        kernel,
        out_shape=outs,
        in_specs=[pl.BlockSpec(memory_space=pltpu.SMEM)] * len(scalars) + vmem_specs(len(arrays)),
        out_specs=vmem_specs(1)[0] if single else tuple(vmem_specs(len(outs))),
        scratch_shapes=list(scratch),
        compiler_params=pltpu.CompilerParams(vmem_limit_bytes=VMEM_LIMIT),
        cost_estimate=pl.CostEstimate(flops=flops, bytes_accessed=1000000, transcendentals=0),
        name=name,
    )(*scalars, *arrays)


def pairs(count, begin):
    table = []
    for first in range(begin, begin + count, 2):
        low, high = first % count, (first + 1) % count
        table += [(low, high), (high, low)]
    return table


def join(rows):
    return jnp.stack([jnp.max(rows[:, 0], axis=0), jnp.sum(rows[:, 1], axis=0)])


def exchanged(row, axes):
    count = lax.axis_size(axes)
    spread = jnp.broadcast_to(row[None], (count,) + row.shape)
    return lax.all_to_all(spread, axes, 0, 0, tiled=True)


GX = ("zl", "core")
GY = ("y", "zh", "x")


def local(fluid_state, switch, z_edges, forcing):
    count_x = lax.axis_size(GX)
    count_y = lax.axis_size(GY)
    cells = 3.0 * ROWS * LANES * count_x * count_y
    place = jnp.stack([lax.axis_index(GX) % 2, lax.axis_index(GY) % 2]).astype(jnp.int32)
    arrays = (fluid_state, switch, z_edges, forcing)
    tile = (8, LANES)
    pair_out, odd_out = call(
        first_kernel,
        "first",
        (shape(X_TILES + 1, *tile), shape(X_TILES, *tile)),
        (place,),
        arrays,
    )
    pair_in = lax.all_gather(pair_out, "core")
    odd_in = lax.ppermute(odd_out, GX, pairs(count_x, 1))
    totals = exchanged(join(pair_in[:, X_TILES, 0:2]), ("y", "x"))
    strips = call(
        second_kernel,
        "second",
        (shape(EXT + 2 * ROWS, LANES), shape(EXT + 2 * ROWS, LANES)),
        (place,),
        (*arrays, pair_in, odd_in),
    )
    even_in = lax.ppermute(strips[0], GY, pairs(count_y, 0))
    odd_y_in = lax.ppermute(strips[1], GY, pairs(count_y, 1))
    totals = exchanged(join(totals), ("zh", "zl"))
    extended = (EXT, LANES)
    work = [pltpu.VMEM((6, *extended), F32) for _ in range(3)]
    fields, force, tend = call(
        third_kernel,
        "third",
        (shape(2, FIELDS, *extended), shape(2, FORCES, *extended), shape(2, 18, *extended)),
        (place,),
        (*arrays, pair_in, odd_in, even_in, odd_y_in),
        [pltpu.VMEM((2, 6, 3, *extended), F32), pltpu.VMEM((2, 2, 6, 3, *extended), F32), *work],
        flops=10_000_000,
    )
    return call(
        functools.partial(fourth_kernel, cells),
        "fourth",
        shape(6, 3, ROWS, LANES),
        (),
        (totals, fields, force, tend, z_edges),
        [pltpu.VMEM((6, 3, *extended), F32), pltpu.VMEM((2, 6, 3, *extended), F32), *work],
        flops=10_000_000,
    )


def solution(mesh):
    count_x, count_y = mesh.devices.shape
    count_z = 2 if count_y % 8 == 0 else 1
    parts = (count_x // 2, 2, count_y // (4 * count_z), count_z, 4)
    split = Mesh(mesh.devices.reshape(parts), (*GX, *GY))
    return jax.shard_map(
        local,
        mesh=split,
        in_specs=(
            P(None, None, GX, GY),
            P(None, GX, GY),
            P(None, None, None, GX, GY),
            P(None, None, GX, GY),
        ),
        out_specs=P(None, None, GX, GY),
        check_vma=False,
    )
```

```python
import functools

import jax
import jax.numpy as jnp
from jax import lax
from jax.experimental import pallas as pl
from jax.experimental.pallas import tpu as pltpu
from jax.sharding import Mesh
from jax.sharding import PartitionSpec as P

ADIABATIC = 5.0 / 3.0
CFL_NUMBER = 0.4
INJECTION = 0.04
LANES = 128
ROWS = 16
EXT = 32
FIELDS = 21
EDGES = 36
FORCES = 9
X_TILES = FIELDS + EDGES + FORCES
VMEM_LIMIT = 16 * 1024 * 1024
F32 = jnp.float32


def lane_index(shape):
    return lax.broadcasted_iota(jnp.int32, shape, len(shape) - 1)


def roll(values, shift, axis):
    size = values.shape[axis]
    shift = shift % size
    return values if shift == 0 else pltpu.roll(values, shift, axis)


def source_tile(refs, index):
    state, switch, edges, forcing = refs
    if index < 18:
        return lambda rows: state[index // 3, index % 3, rows, :]
    index -= 18
    if index < 3:
        return lambda rows: switch[index, rows, :].astype(F32)
    index -= 3
    if index < EDGES:
        side, rest = divmod(index, 18)
        return lambda rows: edges[side, rest // 3, rest % 3, rows, :]
    index -= EDGES
    return lambda rows: forcing[index // 3, index % 3, rows, :]


def first_kernel(
    place, state_in, switch_in, edges_in, forcing_in,
    pair_out, odd_out, state, switch, edges, forcing, arrived,
):
    refs = (state, switch, edges, forcing)
    copies = [
        pltpu.make_async_copy(source, target, arrived.at[k])
        for k, (source, target) in enumerate(
            zip((state_in, switch_in, edges_in, forcing_in), refs, strict=True)
        )
    ]
    for copy in copies:
        copy.start()
    odd = place[0]
    near = pl.multiple_of(8 * (1 - odd), 8)
    far = pl.multiple_of(8 * odd, 8)
    for copy in copies:
        copy.wait()
    peak = None
    total = None
    for plane in range(3):
        density = state[0, plane]
        inverse = 1.0 / density
        momenta = [state[1 + k, plane] for k in range(3)]
        kinetic = 0.5 * inverse * (momenta[0] ** 2 + momenta[1] ** 2 + momenta[2] ** 2)
        heat = jnp.where(switch[plane] == 1, state[5, plane], state[4, plane] - kinetic)
        sound = jnp.sqrt(ADIABATIC * (ADIABATIC - 1.0) * heat * inverse)
        speed = (
            jnp.abs(momenta[0]) + jnp.abs(momenta[1]) + jnp.abs(momenta[2])
        ) * inverse + 3.0 * sound
        power = density * (forcing[0, plane] ** 2 + forcing[1, plane] ** 2 + forcing[2, plane] ** 2)
        peak = speed if peak is None else jnp.maximum(peak, speed)
        total = power if total is None else total + power
    for index in range(X_TILES):
        tile = source_tile(refs, index)
        pair_out[index] = tile(pl.ds(near, 8))
        odd_out[index] = tile(pl.ds(far, 8))
    row = lax.broadcasted_iota(jnp.int32, (8, LANES), 0)
    pair_out[X_TILES] = jnp.where(row == 0, jnp.max(peak), jnp.sum(total))


def spread_kernel(rows, after, out):
    peak = jnp.max(rows[:, 0, :], axis=0, keepdims=True)
    total = jnp.sum(rows[:, 1, :], axis=0, keepdims=True)
    joined = jnp.concatenate([peak, total], axis=0)
    out[...] = jnp.broadcast_to(joined[None], out.shape)


def second_kernel(place, state, switch, edges, forcing, pair_in, odd_in, even_out, odd_out):
    odd_x = place[0]
    odd_y = place[1]
    refs = (state, switch, edges, forcing)
    lane = lane_index((EXT, LANES))
    high = jnp.zeros((EXT, LANES), F32)
    low = jnp.zeros((EXT, LANES), F32)
    for index in range(FIELDS):
        from_pair = pair_in[1 - odd_x, index]
        from_odd = odd_in[index]
        below = jnp.where(odd_x == 0, from_odd, from_pair)
        above = jnp.where(odd_x == 0, from_pair, from_odd)
        block = source_tile(refs, index)(slice(0, ROWS))
        column = jnp.concatenate([below, block, above], axis=0)
        mine = (lane >= 6 * index) & (lane < 6 * index + 6)
        high = jnp.where(mine, roll(column, 6 * index - 122, 1), high)
        low = jnp.where(mine, roll(column, 6 * index, 1), low)
    even_out[0:EXT] = jnp.where(odd_y == 0, high, low)
    odd_out[0:EXT] = jnp.where(odd_y == 0, low, high)
    lane = lane_index((ROWS, LANES))
    for begin, count, row in ((FIELDS, EDGES, EXT), (FIELDS + EDGES, FORCES, EXT + ROWS)):
        high = jnp.zeros((ROWS, LANES), F32)
        low = jnp.zeros((ROWS, LANES), F32)
        for index in range(count):
            block = source_tile(refs, begin + index)(slice(0, ROWS))
            mine = (lane >= 3 * index) & (lane < 3 * index + 3)
            high = jnp.where(mine, roll(block, 3 * index - 125, 1), high)
            low = jnp.where(mine, roll(block, 3 * index, 1), low)
        even_out[row : row + ROWS] = jnp.where(odd_y == 0, high, low)
        odd_out[row : row + ROWS] = jnp.where(odd_y == 0, low, high)


def face_above(before, here, after, beyond):
    value = (7.0 / 12.0) * (here + after) - (1.0 / 12.0) * (before + beyond)
    return jnp.minimum(
        jnp.maximum(value, jnp.minimum(here, after)), jnp.maximum(here, after)
    )


def limited(here, face_low, face_high):
    low_dev = face_low - here
    high_dev = face_high - here
    opposite = low_dev * high_dev < 0.0
    low_span = 2.0 * jnp.abs(low_dev)
    high_span = 2.0 * jnp.abs(high_dev)
    low_dev = jnp.minimum(jnp.maximum(low_dev, -high_span), high_span)
    high_dev = jnp.minimum(jnp.maximum(high_dev, -low_span), low_span)
    return jnp.where(opposite, here + low_dev, here), jnp.where(opposite, here + high_dev, here)


def face_flux(left, right, normal):
    left_u, right_u = left[1 + normal], right[1 + normal]
    left_sound = jnp.sqrt(ADIABATIC * left[4] / left[0])
    right_sound = jnp.sqrt(ADIABATIC * right[4] / right[0])
    slow = jnp.minimum(jnp.minimum(left_u - left_sound, right_u - right_sound), 0.0)
    fast = jnp.maximum(jnp.maximum(left_u + left_sound, right_u + right_sound), 0.0)
    share = 1.0 / (fast - slow)
    left_part = fast * share
    right_part = -slow * share
    left_rate = left_part * (left_u - slow)
    right_rate = right_part * (right_u - fast)
    left_mass = left_rate * left[0]
    right_mass = right_rate * right[0]
    left_square = left[1] * left[1] + left[2] * left[2] + left[3] * left[3]
    right_square = right[1] * right[1] + right[2] * right[2] + right[3] * right[3]
    flux = [left_mass + right_mass]
    for k in (1, 2, 3):
        flux.append(left_mass * left[k] + right_mass * right[k])
    left_push = left_part * left[4]
    right_push = right_part * right[4]
    flux[1 + normal] = flux[1 + normal] + (left_push + right_push)
    flux.append(
        0.5 * (left_mass * left_square + right_mass * right_square)
        + left[4] * (1.5 * left_rate)
        + right[4] * (1.5 * right_rate)
        + left_push * left_u
        + right_push * right_u
    )
    flux.append(left_mass * left[5] + right_mass * right[5])
    return flux


def z_fluxes(planes):
    lower, upper = [], []
    for k in range(6):
        column = [planes[j][k] for j in range(9)]
        faces = [face_above(*column[j : j + 4]) for j in range(6)]
        cells = [limited(column[j + 2], faces[j], faces[j + 1]) for j in range(5)]
        lower.append([cells[j][1] for j in range(4)])
        upper.append([cells[j + 1][0] for j in range(4)])
    return [
        face_flux([lower[k][j] for k in range(6)], [upper[k][j] for k in range(6)], 2)
        for j in range(4)
    ]


def edge_primitives(fields):
    density = fields[0]
    inverse = 1.0 / density
    kinetic = 0.5 * inverse * (fields[1] ** 2 + fields[2] ** 2 + fields[3] ** 2)
    return [
        density,
        fields[1] * inverse,
        fields[2] * inverse,
        fields[3] * inverse,
        (ADIABATIC - 1.0) * (fields[4] - kinetic),
        fields[5] * inverse,
    ]


def shift_pair(main, rim, step):
    lane = lane_index(main.shape)
    main_rolled = roll(main, -step, 1)
    rim_rolled = roll(rim, -step, 1)
    inside = lane < LANES - step if step > 0 else lane >= -step
    return (
        jnp.where(inside, main_rolled, rim_rolled),
        jnp.where(inside, rim_rolled, main_rolled),
    )


def y_differences(main, rim):
    lows, highs = ([], []), ([], [])
    spread = None
    for k in range(6):
        here = (main[k], rim[k])
        before = shift_pair(*here, -1)
        after = shift_pair(*here, 1)
        beyond = shift_pair(*here, 2)
        faces = [face_above(before[j], here[j], after[j], beyond[j]) for j in range(2)]
        below = shift_pair(*faces, -1)
        cells = [limited(here[j], below[j], faces[j]) for j in range(2)]
        nexts = shift_pair(cells[0][0], cells[1][0], 1)
        for j in range(2):
            lows[j].append(cells[j][1])
            highs[j].append(nexts[j])
        if k == 2:
            spread = [0.5 * (after[j] - before[j]) for j in range(2)]
    fluxes = [face_flux(lows[j], highs[j], 1) for j in range(2)]
    differences = ([], [])
    for k in range(6):
        below = shift_pair(fluxes[0][k], fluxes[1][k], -1)
        for j in range(2):
            differences[j].append(fluxes[j][k] - below[j])
    return differences, spread


CHUNKS = (4, 12, 20)


def x_sweep(prims, plane, chunks, low_ref, high_ref, flux_ref):
    for row in chunks:
        for k in range(6):
            rows = [prims[k, plane, pl.ds(row + s, 8), :] for s in (-2, -1, 0, 1, 2)]
            below = face_above(*rows[0:4])
            above = face_above(*rows[1:5])
            low_ref[k, pl.ds(row, 8), :], high_ref[k, pl.ds(row, 8), :] = limited(
                rows[2], below, above
            )
    for row in chunks:
        left = [high_ref[k, pl.ds(row, 8), :] for k in range(6)]
        right = [low_ref[k, pl.ds(row + 1, 8), :] for k in range(6)]
        flux = face_flux(left, right, 0)
        for k in range(6):
            flux_ref[k, pl.ds(row, 8), :] = flux[k]


def third_kernel(
    place, state, switch, edges, forcing, pair_in, odd_in, even_in, odd_y_in,
    fields, force, tend, prims, planes, low_ref, high_ref, flux_ref,
):
    odd_x = place[0]
    odd_y = place[1]
    refs = (state, switch, edges, forcing)
    lane = lane_index((EXT, LANES))
    above_strip = jnp.where(odd_y == 0, even_in[...], odd_y_in[...])
    below_strip = jnp.where(odd_y == 0, odd_y_in[...], even_in[...])

    def with_rows(index):
        from_pair = pair_in[1 - odd_x, index]
        from_odd = odd_in[index]
        below = jnp.where(odd_x == 0, from_odd, from_pair)
        above = jnp.where(odd_x == 0, from_pair, from_odd)
        block = source_tile(refs, index)(slice(0, ROWS))
        return jnp.concatenate([below, block, above], axis=0)

    for index in range(FIELDS):
        fields[0, index] = with_rows(index)
        fields[1, index] = jnp.where(
            lane < 64,
            roll(above_strip[0:EXT], -6 * index, 1),
            roll(below_strip[0:EXT], 122 - 6 * index, 1),
        )
    lane = lane_index((ROWS, LANES))
    rim_edges = []
    for begin, count, row in ((FIELDS, EDGES, EXT), (FIELDS + EDGES, FORCES, EXT + ROWS)):
        for index in range(count):
            rim = jnp.where(
                lane < 64,
                roll(above_strip[row : row + ROWS], -3 * index, 1),
                roll(below_strip[row : row + ROWS], 125 - 3 * index, 1),
            )
            if begin == FIELDS:
                rim_edges.append(rim)
            else:
                force[0, index] = with_rows(begin + index)
                force[1, index, 0:8] = jnp.zeros((8, LANES), F32)
                force[1, index, 8:24] = rim
                force[1, index, 24:32] = jnp.zeros((8, LANES), F32)

    for plane in range(3):
        for tile in range(2):
            values = [fields[tile, 3 * k + plane] for k in range(7)]
            density = values[0]
            inverse = 1.0 / density
            kinetic = 0.5 * inverse * (values[1] ** 2 + values[2] ** 2 + values[3] ** 2)
            heat = jnp.where(values[6] == 1.0, values[5], values[4] - kinetic)
            prims[tile, 0, plane] = density
            for k in (1, 2, 3):
                prims[tile, k, plane] = values[k] * inverse
            prims[tile, 4, plane] = (ADIABATIC - 1.0) * heat
            prims[tile, 5, plane] = values[5] * inverse
    for side in range(2):
        for plane in range(3):
            index = 18 * side + plane
            values = edge_primitives([with_rows(FIELDS + index + 3 * k) for k in range(6)])
            for k in range(6):
                planes[0, side, k, plane] = values[k]
            values = edge_primitives([rim_edges[index + 3 * k] for k in range(6)])
            for k in range(6):
                planes[1, side, k, plane, 0:8] = jnp.ones((8, LANES), F32)
                planes[1, side, k, plane, 8:24] = values[k]
                planes[1, side, k, plane, 24:32] = jnp.ones((8, LANES), F32)

    for plane in range(3):
        spreads = {}
        for row in CHUNKS:
            both = [
                [prims[tile, k, plane, pl.ds(row, 8), :] for k in range(6)] for tile in range(2)
            ]
            differences, spread = y_differences(*both)
            for tile in range(2):
                spreads[tile, row] = spread[tile]
                for k in range(6):
                    tend[tile, 3 * k + plane, pl.ds(row, 8), :] = -differences[tile][k]
        for tile in range(2):
            for k in range(6):
                low_ref[k, pl.ds(28, 4), :] = jnp.ones((4, LANES), F32)
                flux_ref[k, pl.ds(0, 4), :] = jnp.zeros((4, LANES), F32)
            x_sweep(prims.at[tile], plane, CHUNKS, low_ref, high_ref, flux_ref)
            for row in CHUNKS:
                for k in range(6):
                    difference = (
                        flux_ref[k, pl.ds(row, 8), :] - flux_ref[k, pl.ds(row - 1, 8), :]
                    )
                    tend[tile, 3 * k + plane, pl.ds(row, 8), :] -= difference
                before = prims[tile, 1, plane, pl.ds(row - 1, 8), :]
                after = prims[tile, 1, plane, pl.ds(row + 1, 8), :]
                spread = spreads[tile, row] + 0.5 * (after - before)
                below = prims[tile, 3, plane - 1, pl.ds(row, 8), :] if plane > 0 else (
                    planes[tile, 0, 3, 2, pl.ds(row, 8), :]
                )
                above = prims[tile, 3, plane + 1, pl.ds(row, 8), :] if plane < 2 else (
                    planes[tile, 1, 3, 0, pl.ds(row, 8), :]
                )
                spread = spread + 0.5 * (above - below)
                pressure = prims[tile, 4, plane, pl.ds(row, 8), :]
                tend[tile, 15 + plane, pl.ds(row, 8), :] -= pressure * spread
    for tile in range(2):
        for row in CHUNKS:
            rows = pl.ds(row, 8)
            column = (
                [[planes[tile, 0, k, p, rows, :] for k in range(6)] for p in range(3)]
                + [[prims[tile, k, p, rows, :] for k in range(6)] for p in range(3)]
                + [[planes[tile, 1, k, p, rows, :] for k in range(6)] for p in range(3)]
            )
            flux = z_fluxes(column)
            for plane in range(3):
                for k in range(6):
                    tend[tile, 3 * k + plane, rows, :] -= flux[plane + 1][k] - flux[plane][k]


def settled(values, switch):
    kinetic = 0.5 / values[0] * (values[1] ** 2 + values[2] ** 2 + values[3] ** 2)
    return jnp.where(switch == 0.0, values[4] - kinetic, values[5])


def fourth_kernel(
    cells, totals, fields, force, tend, edges, updated,
    section, prims, low_ref, high_ref, flux_ref,
):
    peak = jnp.max(totals[:, 0, :], axis=0, keepdims=True)
    power = jnp.sum(totals[:, 1, :], axis=0, keepdims=True)
    time_step = CFL_NUMBER / peak
    scale = jnp.sqrt(INJECTION / (0.5 * time_step * (power / cells + 1e-06)))

    def forced(values, force_values, tendency):
        result = list(tendency)
        for k in (1, 2, 3):
            result[k] = result[k] + scale * values[0] * force_values[k - 1]
        result[4] = result[4] + scale * (
            values[1] * force_values[0] + values[2] * force_values[1] + values[3] * force_values[2]
        )
        return result

    for plane in range(3):
        for tile in range(2):
            for row in CHUNKS:
                rows = pl.ds(row, 8)
                values = [fields[tile, 3 * k + plane, rows, :] for k in range(7)]
                drive = [force[tile, 3 * k + plane, rows, :] for k in range(3)]
                rate = forced(values, drive, [tend[tile, 3 * k + plane, rows, :] for k in range(6)])
                stage = [values[k] + time_step * rate[k] for k in range(6)]
                stage[5] = settled(stage, values[6])
                inverse = 1.0 / stage[0]
                if tile == 0:
                    for k in range(6):
                        section[k, plane, rows, :] = stage[k]
                prims[tile, 0, plane, rows, :] = stage[0]
                for k in (1, 2, 3):
                    prims[tile, k, plane, rows, :] = stage[k] * inverse
                prims[tile, 4, plane, rows, :] = (ADIABATIC - 1.0) * stage[5]
                prims[tile, 5, plane, rows, :] = stage[5] * inverse

    z_flux = []
    outer = {}
    for row in (8, 16):
        rows = pl.ds(row, 8)
        for side in range(2):
            for plane in range(3):
                outer[side, plane] = edge_primitives(
                    [edges[side, k, plane, pl.ds(row - 8, 8), :] for k in range(6)]
                )
        column = (
            [outer[0, p] for p in range(3)]
            + [[prims[0, k, p, rows, :] for k in range(6)] for p in range(3)]
            + [outer[1, p] for p in range(3)]
        )
        flux = z_fluxes(column)
        for plane in range(3):
            below = outer[0, 2][3] if plane == 0 else prims[0, 3, plane - 1, rows, :]
            above = outer[1, 0][3] if plane == 2 else prims[0, 3, plane + 1, rows, :]
            spread = 0.5 * (above - below)
            for k in range(6):
                updated[k, plane, pl.ds(row - 8, 8), :] = flux[plane][k] - flux[plane + 1][k]
            pressure = prims[0, 4, plane, rows, :]
            updated[5, plane, pl.ds(row - 8, 8), :] -= pressure * spread
    for plane in range(3):
        for k in range(6):
            low_ref[k, pl.ds(28, 4), :] = jnp.ones((4, LANES), F32)
        x_sweep(prims.at[0], plane, CHUNKS, low_ref, high_ref, flux_ref)
        for row in (8, 16):
            rows = pl.ds(row, 8)
            inner = pl.ds(row - 8, 8)
            both = [
                [prims[tile, k, plane, rows, :] for k in range(6)] for tile in range(2)
            ]
            differences, spread = y_differences(*both)
            before = prims[0, 1, plane, pl.ds(row - 1, 8), :]
            after = prims[0, 1, plane, pl.ds(row + 1, 8), :]
            spread = spread[0] + 0.5 * (after - before)
            rate = []
            for k in range(6):
                across = flux_ref[k, rows, :] - flux_ref[k, pl.ds(row - 1, 8), :]
                rate.append(updated[k, plane, inner, :] - differences[0][k] - across)
            rate[5] = rate[5] - both[0][4] * spread
            stage = [section[k, plane, rows, :] for k in range(6)]
            drive = [force[0, 3 * k + plane, rows, :] for k in range(3)]
            rate = forced(stage, drive, rate)
            values = [fields[0, 3 * k + plane, rows, :] for k in range(7)]
            result = [
                0.5 * values[k] + 0.5 * (stage[k] + time_step * rate[k]) for k in range(6)
            ]
            result[5] = settled(result, values[6])
            for k in range(6):
                updated[k, plane, inner, :] = result[k]


def shape(*sizes):
    return jax.ShapeDtypeStruct(sizes, F32)


def vmem_specs(count):
    return [pl.BlockSpec(memory_space=pltpu.VMEM)] * count


def call(kernel, name, outs, scalars, arrays, scratch=(), cost=0):
    single = not isinstance(outs, tuple)
    return pl.pallas_call(
        kernel,
        out_shape=outs,
        in_specs=[pl.BlockSpec(memory_space=pltpu.SMEM)] * len(scalars) + vmem_specs(len(arrays)),
        out_specs=vmem_specs(1)[0] if single else tuple(vmem_specs(len(outs))),
        scratch_shapes=list(scratch),
        compiler_params=pltpu.CompilerParams(vmem_limit_bytes=VMEM_LIMIT),
        cost_estimate=pl.CostEstimate(flops=cost, bytes_accessed=cost, transcendentals=0),
        name=name,
    )(*scalars, *arrays)


def pairs(count, begin):
    table = []
    for first in range(begin, begin + count, 2):
        low, high = first % count, (first + 1) % count
        table += [(low, high), (high, low)]
    return table


def exchanged(rows, after, axes):
    count = lax.axis_size(axes)
    spread = pl.pallas_call(
        spread_kernel,
        out_shape=shape(count, 2, LANES),
        in_specs=[*vmem_specs(1), pl.BlockSpec(memory_space=pl.ANY)],
        out_specs=vmem_specs(1)[0],
        compiler_params=pltpu.CompilerParams(vmem_limit_bytes=VMEM_LIMIT),
        name="spread",
    )(rows, after)
    return lax.all_to_all(spread, axes, 0, 0, tiled=True)


GX = ("zl", "core")
GY = ("y", "zh", "x")


def local(fluid_state, switch, z_edges, forcing):
    count_x = lax.axis_size(GX)
    count_y = lax.axis_size(GY)
    cells = 3.0 * ROWS * LANES * count_x * count_y
    place = jnp.stack([lax.axis_index(GX) % 2, lax.axis_index(GY) % 2]).astype(jnp.int32)
    tile = (8, LANES)
    inputs = (fluid_state, switch, z_edges, forcing)
    pair_out, odd_out, *arrays = pl.pallas_call(
        first_kernel,
        out_shape=(
            shape(X_TILES + 1, *tile),
            shape(X_TILES, *tile),
            *(jax.ShapeDtypeStruct(values.shape, values.dtype) for values in inputs),
        ),
        in_specs=[
            pl.BlockSpec(memory_space=pltpu.SMEM),
            *([pl.BlockSpec(memory_space=pltpu.HBM)] * 4),
        ],
        out_specs=tuple(vmem_specs(6)),
        scratch_shapes=[pltpu.SemaphoreType.DMA((4,))],
        compiler_params=pltpu.CompilerParams(vmem_limit_bytes=VMEM_LIMIT),
        name="first",
    )(place, *(pltpu.with_memory_space_constraint(values, pltpu.HBM) for values in inputs))
    pair_in = lax.all_gather(pair_out, "core")
    odd_in = lax.ppermute(odd_out, GX, pairs(count_x, 1))
    totals = exchanged(pair_in[:, X_TILES, 0:2], place, ("y", "x"))
    strips = call(
        second_kernel,
        "second",
        (shape(EXT + 2 * ROWS, LANES), shape(EXT + 2 * ROWS, LANES)),
        (place,),
        (*arrays, pair_in, odd_in),
        cost=4_000_000,
    )
    even_in = lax.ppermute(strips[0], GY, pairs(count_y, 0))
    odd_y_in = lax.ppermute(strips[1], GY, pairs(count_y, 1))
    totals = exchanged(totals, even_in, ("zh", "zl"))
    extended = (EXT, LANES)
    work = [pltpu.VMEM((6, *extended), F32) for _ in range(3)]
    fields, force, tend = call(
        third_kernel,
        "third",
        (shape(2, FIELDS, *extended), shape(2, FORCES, *extended), shape(2, 18, *extended)),
        (place,),
        (*arrays, pair_in, odd_in, even_in, odd_y_in),
        [pltpu.VMEM((2, 6, 3, *extended), F32), pltpu.VMEM((2, 2, 6, 3, *extended), F32), *work],
        cost=60_000_000,
    )
    return call(
        functools.partial(fourth_kernel, cells),
        "fourth",
        shape(6, 3, ROWS, LANES),
        (),
        (totals, fields, force, tend, arrays[2]),
        [pltpu.VMEM((6, 3, *extended), F32), pltpu.VMEM((2, 6, 3, *extended), F32), *work],
        cost=8_000_000,
    )


def solution(mesh):
    count_x, count_y = mesh.devices.shape
    count_z = 2 if count_y % 8 == 0 else 1
    parts = (count_x // 2, 2, count_y // (4 * count_z), count_z, 4)
    split = Mesh(mesh.devices.reshape(parts), (*GX, *GY))
    return jax.shard_map(
        local,
        mesh=split,
        in_specs=(
            P(None, None, GX, GY),
            P(None, GX, GY),
            P(None, None, None, GX, GY),
            P(None, None, GX, GY),
        ),
        out_specs=P(None, None, GX, GY),
        check_vma=False,
    )
```

```python
import functools

import jax
import jax.numpy as jnp
from jax import lax
from jax.experimental import pallas as pl
from jax.experimental.pallas import tpu as pltpu
from jax.sharding import Mesh
from jax.sharding import PartitionSpec as P

ADIABATIC = 5.0 / 3.0
CFL_NUMBER = 0.4
INJECTION = 0.04
LANES = 128
ROWS = 16
EXT = 32
FIELDS = 21
EDGES = 36
FORCES = 9
X_TILES = FIELDS + EDGES + FORCES
VMEM_LIMIT = 16 * 1024 * 1024
F32 = jnp.float32


def lane_index(shape):
    return lax.broadcasted_iota(jnp.int32, shape, len(shape) - 1)


def roll(values, shift, axis):
    size = values.shape[axis]
    shift = shift % size
    return values if shift == 0 else pltpu.roll(values, shift, axis)


def each(count, body):
    def step(index, carry):
        body(index)
        return carry

    lax.fori_loop(0, count, step, 0)


def x_place(refs, index):
    state, switch, edges, forcing = refs
    if index < 18:
        return lambda rows: state[index, rows, :]
    index -= 18
    if index < 3:
        return lambda rows: switch[index, rows, :].astype(F32)
    index -= 3
    if index < EDGES:
        return lambda rows: edges[index, rows, :]
    index -= EDGES
    return lambda rows: forcing[index, rows, :]


def first_kernel(
    place, state_in, switch_in, edges_in, forcing_in,
    pair_out, odd_out, state, switch, edges, forcing, arrived,
):
    refs = (state, switch, edges, forcing)
    copies = [
        pltpu.make_async_copy(source, target, arrived.at[k])
        for k, (source, target) in enumerate(
            zip((state_in, switch_in, edges_in, forcing_in), refs, strict=True)
        )
    ]
    for copy in copies:
        copy.start()
    odd = place[0]
    near = pl.multiple_of(8 * (1 - odd), 8)
    far = pl.multiple_of(8 * odd, 8)
    for copy in copies:
        copy.wait()
    peak = None
    total = None
    for plane in range(3):
        fields = [state[3 * k + plane] for k in range(6)]
        density = fields[0]
        inverse = 1.0 / density
        kinetic = 0.5 * inverse * (fields[1] ** 2 + fields[2] ** 2 + fields[3] ** 2)
        heat = jnp.where(switch[plane] == 1, fields[5], fields[4] - kinetic)
        sound = jnp.sqrt(ADIABATIC * (ADIABATIC - 1.0) * heat * inverse)
        speed = (
            jnp.abs(fields[1]) + jnp.abs(fields[2]) + jnp.abs(fields[3])
        ) * inverse + 3.0 * sound
        drive = [forcing[3 * k + plane] for k in range(3)]
        power = density * (drive[0] ** 2 + drive[1] ** 2 + drive[2] ** 2)
        peak = speed if peak is None else jnp.maximum(peak, speed)
        total = power if total is None else total + power
    for index in range(X_TILES):
        tile = x_place(refs, index)
        pair_out[index] = tile(pl.ds(near, 8))
        odd_out[index] = tile(pl.ds(far, 8))
    row = lax.broadcasted_iota(jnp.int32, (8, LANES), 0)
    pair_out[X_TILES] = jnp.where(row == 0, jnp.max(peak), jnp.sum(total))


def spread_kernel(rows, after, out):
    peak = jnp.max(rows[:, 0, :], axis=0, keepdims=True)
    total = jnp.sum(rows[:, 1, :], axis=0, keepdims=True)
    joined = jnp.concatenate([peak, total], axis=0)
    out[...] = jnp.broadcast_to(joined[None], out.shape)


def rows_around(odd_x, pair_in, odd_in, index, block):
    from_pair = pair_in[1 - odd_x, index]
    from_odd = odd_in[index]
    below = jnp.where(odd_x == 0, from_odd, from_pair)
    above = jnp.where(odd_x == 0, from_pair, from_odd)
    return jnp.concatenate([below, block, above], axis=0)


def turned(values, shift):
    return pltpu.roll(values, lax.rem(shift + LANES, LANES), 1)


def second_kernel(place, state, switch, edges, forcing, pair_in, odd_in, even_out, odd_out):
    odd_x = place[0]
    odd_y = place[1]
    lane = lane_index((EXT, LANES))

    def columns(index, block, sums):
        column = rows_around(odd_x, pair_in, odd_in, index, block)
        mine = (lane >= 6 * index) & (lane < 6 * index + 6)
        return (
            jnp.where(mine, turned(column, 6 * index - 122), sums[0]),
            jnp.where(mine, turned(column, 6 * index), sums[1]),
        )

    def state_columns(field, sums):
        for plane in range(3):
            index = 3 * field + plane
            sums = columns(index, state[index], sums)
        return sums

    blank = jnp.zeros((EXT, LANES), F32)
    sums = lax.fori_loop(0, 6, state_columns, (blank, blank))
    for plane in range(3):
        sums = columns(18 + plane, switch[plane].astype(F32), sums)
    high, low = sums
    even_out[0:EXT] = jnp.where(odd_y == 0, high, low)
    odd_out[0:EXT] = jnp.where(odd_y == 0, low, high)

    lane = lane[0:ROWS]
    blank = blank[0:ROWS]
    for source, count, row in ((edges, EDGES, EXT), (forcing, FORCES, EXT + ROWS)):

        def three(step, sums, source=source):
            for k in range(3):
                index = 3 * step + k
                block = source[index]
                mine = (lane >= 3 * index) & (lane < 3 * index + 3)
                sums = (
                    jnp.where(mine, turned(block, 3 * index - 125), sums[0]),
                    jnp.where(mine, turned(block, 3 * index), sums[1]),
                )
            return sums

        high, low = lax.fori_loop(0, count // 3, three, (blank, blank))
        even_out[row : row + ROWS] = jnp.where(odd_y == 0, high, low)
        odd_out[row : row + ROWS] = jnp.where(odd_y == 0, low, high)


def face_above(before, here, after, beyond):
    value = (7.0 / 12.0) * (here + after) - (1.0 / 12.0) * (before + beyond)
    return jnp.minimum(
        jnp.maximum(value, jnp.minimum(here, after)), jnp.maximum(here, after)
    )


def limited(here, face_low, face_high):
    low_dev = face_low - here
    high_dev = face_high - here
    opposite = low_dev * high_dev < 0.0
    low_span = 2.0 * jnp.abs(low_dev)
    high_span = 2.0 * jnp.abs(high_dev)
    low_dev = jnp.minimum(jnp.maximum(low_dev, -high_span), high_span)
    high_dev = jnp.minimum(jnp.maximum(high_dev, -low_span), low_span)
    return jnp.where(opposite, here + low_dev, here), jnp.where(opposite, here + high_dev, here)


def face_flux(left, right, normal):
    left_u, right_u = left[1 + normal], right[1 + normal]
    left_sound = jnp.sqrt(ADIABATIC * left[4] / left[0])
    right_sound = jnp.sqrt(ADIABATIC * right[4] / right[0])
    slow = jnp.minimum(jnp.minimum(left_u - left_sound, right_u - right_sound), 0.0)
    fast = jnp.maximum(jnp.maximum(left_u + left_sound, right_u + right_sound), 0.0)
    share = 1.0 / (fast - slow)
    left_part = fast * share
    right_part = -slow * share
    left_rate = left_part * (left_u - slow)
    right_rate = right_part * (right_u - fast)
    left_mass = left_rate * left[0]
    right_mass = right_rate * right[0]
    left_square = left[1] * left[1] + left[2] * left[2] + left[3] * left[3]
    right_square = right[1] * right[1] + right[2] * right[2] + right[3] * right[3]
    flux = [left_mass + right_mass]
    for k in (1, 2, 3):
        flux.append(left_mass * left[k] + right_mass * right[k])
    left_push = left_part * left[4]
    right_push = right_part * right[4]
    flux[1 + normal] = flux[1 + normal] + (left_push + right_push)
    flux.append(
        0.5 * (left_mass * left_square + right_mass * right_square)
        + left[4] * (1.5 * left_rate)
        + right[4] * (1.5 * right_rate)
        + left_push * left_u
        + right_push * right_u
    )
    flux.append(left_mass * left[5] + right_mass * right[5])
    return flux


def z_fluxes(planes):
    lower, upper = [], []
    for k in range(6):
        column = [planes[j][k] for j in range(9)]
        faces = [face_above(*column[j : j + 4]) for j in range(6)]
        cells = [limited(column[j + 2], faces[j], faces[j + 1]) for j in range(5)]
        lower.append([cells[j][1] for j in range(4)])
        upper.append([cells[j + 1][0] for j in range(4)])
    return [
        face_flux([lower[k][j] for k in range(6)], [upper[k][j] for k in range(6)], 2)
        for j in range(4)
    ]


def edge_primitives(fields):
    density = fields[0]
    inverse = 1.0 / density
    kinetic = 0.5 * inverse * (fields[1] ** 2 + fields[2] ** 2 + fields[3] ** 2)
    return [
        density,
        fields[1] * inverse,
        fields[2] * inverse,
        fields[3] * inverse,
        (ADIABATIC - 1.0) * (fields[4] - kinetic),
        fields[5] * inverse,
    ]


def shift_pair(main, rim, step):
    lane = lane_index(main.shape)
    main_rolled = roll(main, -step, 1)
    rim_rolled = roll(rim, -step, 1)
    inside = lane < LANES - step if step > 0 else lane >= -step
    return (
        jnp.where(inside, main_rolled, rim_rolled),
        jnp.where(inside, rim_rolled, main_rolled),
    )


def y_differences(main, rim):
    lows, highs = ([], []), ([], [])
    spread = None
    for k in range(6):
        here = (main[k], rim[k])
        before = shift_pair(*here, -1)
        after = shift_pair(*here, 1)
        beyond = shift_pair(*here, 2)
        faces = [face_above(before[j], here[j], after[j], beyond[j]) for j in range(2)]
        below = shift_pair(*faces, -1)
        cells = [limited(here[j], below[j], faces[j]) for j in range(2)]
        nexts = shift_pair(cells[0][0], cells[1][0], 1)
        for j in range(2):
            lows[j].append(cells[j][1])
            highs[j].append(nexts[j])
        if k == 2:
            spread = [0.5 * (after[j] - before[j]) for j in range(2)]
    fluxes = [face_flux(lows[j], highs[j], 1) for j in range(2)]
    differences = ([], [])
    for k in range(6):
        below = shift_pair(fluxes[0][k], fluxes[1][k], -1)
        for j in range(2):
            differences[j].append(fluxes[j][k] - below[j])
    return differences, spread


CHUNKS = (4, 12, 20)


def x_sweep(prims, low_ref, high_ref, face_ref, flux_ref):
    for row in CHUNKS:
        for k in range(6):
            before, here, after, beyond = [
                prims[k, pl.ds(row + s, 8), :] for s in (-1, 0, 1, 2)
            ]
            if row == CHUNKS[0]:
                below = face_above(prims[k, pl.ds(row - 2, 8), :], before, here, after)
            above = face_above(before, here, after, beyond)
            face_ref[k, pl.ds(row, 8), :] = above
            if row != CHUNKS[0]:
                below = face_ref[k, pl.ds(row - 1, 8), :]
            low_ref[k, pl.ds(row, 8), :], high_ref[k, pl.ds(row, 8), :] = limited(
                here, below, above
            )
    for row in CHUNKS:
        left = [high_ref[k, pl.ds(row, 8), :] for k in range(6)]
        right = [low_ref[k, pl.ds(row + 1, 8), :] for k in range(6)]
        flux = face_flux(left, right, 0)
        for k in range(6):
            flux_ref[k, pl.ds(row, 8), :] = flux[k]


def clear_ends(low_ref, flux_ref):
    for k in range(6):
        low_ref[k, pl.ds(28, 4), :] = jnp.ones((4, LANES), F32)
        flux_ref[k, pl.ds(0, 4), :] = jnp.zeros((4, LANES), F32)


def third_kernel(
    place, state, switch, edges, forcing, pair_in, odd_in, even_in, odd_y_in,
    fields, force, tend, prims, planes, low_ref, high_ref, face_ref, flux_ref, strip_ref,
):
    odd_x = place[0]
    odd_y = place[1]
    strip_ref[0] = jnp.where(odd_y == 0, even_in[...], odd_y_in[...])
    strip_ref[1] = jnp.where(odd_y == 0, odd_y_in[...], even_in[...])
    clear_ends(low_ref, flux_ref)
    lane = lane_index((EXT, LANES))
    edge_lane = lane[0:ROWS]

    def field_tiles(index, block):
        fields[0, index] = rows_around(odd_x, pair_in, odd_in, index, block)
        fields[1, index] = jnp.where(
            lane < 64,
            turned(strip_ref[0, 0:EXT], -6 * index),
            turned(strip_ref[1, 0:EXT], 122 - 6 * index),
        )

    def rim_tile(row, index):
        return jnp.where(
            edge_lane < 64,
            turned(strip_ref[0, row : row + ROWS], -3 * index),
            turned(strip_ref[1, row : row + ROWS], 125 - 3 * index),
        )

    @functools.partial(each, 6)
    def _(field):
        for plane in range(3):
            index = 3 * field + plane
            field_tiles(index, state[index])

    for plane in range(3):
        field_tiles(18 + plane, switch[plane].astype(F32))

    @functools.partial(each, 3)
    def _(part):
        for k in range(3):
            index = 3 * part + k
            force[0, index] = rows_around(
                odd_x, pair_in, odd_in, FIELDS + EDGES + index, forcing[index]
            )
            force[1, index, 0:8] = jnp.zeros((8, LANES), F32)
            force[1, index, 8:24] = rim_tile(EXT + ROWS, index)
            force[1, index, 24:32] = jnp.zeros((8, LANES), F32)

    @functools.partial(each, 6)
    def _(step):
        tile, plane = step // 3, step % 3
        values = [fields[tile, 3 * k + plane] for k in range(7)]
        density = values[0]
        inverse = 1.0 / density
        kinetic = 0.5 * inverse * (values[1] ** 2 + values[2] ** 2 + values[3] ** 2)
        heat = jnp.where(values[6] == 1.0, values[5], values[4] - kinetic)
        prims[tile, plane, 0] = density
        for k in (1, 2, 3):
            prims[tile, plane, k] = values[k] * inverse
        prims[tile, plane, 4] = (ADIABATIC - 1.0) * heat
        prims[tile, plane, 5] = values[5] * inverse

    @functools.partial(each, 6)
    def _(step):
        first = 18 * (step // 3) + step % 3
        places = [first + 3 * k for k in range(6)]
        values = edge_primitives(
            [rows_around(odd_x, pair_in, odd_in, FIELDS + k, edges[k]) for k in places]
        )
        for k in range(6):
            planes[0, step, k] = values[k]
        values = edge_primitives([rim_tile(EXT, k) for k in places])
        for k in range(6):
            planes[1, step, k, 0:8] = jnp.ones((8, LANES), F32)
            planes[1, step, k, 8:24] = values[k]
            planes[1, step, k, 24:32] = jnp.ones((8, LANES), F32)

    @functools.partial(each, 3)
    def _(plane):
        for row in CHUNKS:
            rows = pl.ds(row, 8)
            both = [[prims[tile, plane, k, rows, :] for k in range(6)] for tile in range(2)]
            differences, spread = y_differences(*both)
            for tile in range(2):
                for k in range(5):
                    tend[tile, 3 * k + plane, rows, :] = -differences[tile][k]
                tend[tile, 15 + plane, rows, :] = (
                    -differences[tile][5] - both[tile][4] * spread[tile]
                )

    @functools.partial(each, 6)
    def _(step):
        tile, plane = step // 3, step % 3
        x_sweep(prims.at[tile, plane], low_ref, high_ref, face_ref, flux_ref)
        for row in CHUNKS:
            rows = pl.ds(row, 8)
            for k in range(6):
                difference = flux_ref[k, rows, :] - flux_ref[k, pl.ds(row - 1, 8), :]
                if k == 5:
                    before = prims[tile, plane, 1, pl.ds(row - 1, 8), :]
                    after = prims[tile, plane, 1, pl.ds(row + 1, 8), :]
                    spread = 0.5 * (after - before)
                    difference = difference + prims[tile, plane, 4, rows, :] * spread
                tend[tile, 3 * k + plane, rows, :] -= difference

    @functools.partial(each, 2)
    def _(tile):
        for row in CHUNKS:
            rows = pl.ds(row, 8)
            column = (
                [[planes[tile, p, k, rows, :] for k in range(6)] for p in range(3)]
                + [[prims[tile, p, k, rows, :] for k in range(6)] for p in range(3)]
                + [[planes[tile, 3 + p, k, rows, :] for k in range(6)] for p in range(3)]
            )
            flux = z_fluxes(column)
            for plane in range(3):
                for k in range(6):
                    difference = flux[plane + 1][k] - flux[plane][k]
                    if k == 5:
                        spread = 0.5 * (column[plane + 4][3] - column[plane + 2][3])
                        difference = difference + column[plane + 3][4] * spread
                    tend[tile, 3 * k + plane, rows, :] -= difference


def fourth_kernel(
    cells, totals, fields, force, tend, edges, updated,
    section, prims, low_ref, high_ref, face_ref, flux_ref,
):
    peak = jnp.max(totals[:, 0, :], axis=0, keepdims=True)
    power = jnp.sum(totals[:, 1, :], axis=0, keepdims=True)
    time_step = CFL_NUMBER / peak
    scale = jnp.sqrt(INJECTION / (0.5 * time_step * (power / cells + 1e-06)))
    clear_ends(low_ref, flux_ref)

    def forced(values, drive, tendency):
        result = list(tendency)
        for k in (1, 2, 3):
            result[k] = result[k] + scale * values[0] * drive[k - 1]
        result[4] = result[4] + scale * (
            values[1] * drive[0] + values[2] * drive[1] + values[3] * drive[2]
        )
        return result

    def settle(values, switch, inverse):
        kinetic = 0.5 * inverse * (values[1] ** 2 + values[2] ** 2 + values[3] ** 2)
        values[5] = jnp.where(switch == 0.0, values[4] - kinetic, values[5])

    @functools.partial(each, 6)
    def _(step):
        tile, plane = step // 3, step % 3
        for row in CHUNKS:
            rows = pl.ds(row, 8)
            values = [fields[tile, 3 * k + plane, rows, :] for k in range(7)]
            drive = [force[tile, 3 * k + plane, rows, :] for k in range(3)]
            rate = forced(values, drive, [tend[tile, 3 * k + plane, rows, :] for k in range(6)])
            stage = [values[k] + time_step * rate[k] for k in range(6)]
            inverse = 1.0 / stage[0]
            settle(stage, values[6], inverse)
            for k in range(6):
                section[tile, plane, k, rows, :] = stage[k]
            prims[tile, plane, 0, rows, :] = stage[0]
            for k in (1, 2, 3):
                prims[tile, plane, k, rows, :] = stage[k] * inverse
            prims[tile, plane, 4, rows, :] = (ADIABATIC - 1.0) * stage[5]
            prims[tile, plane, 5, rows, :] = stage[5] * inverse

    @functools.partial(each, 2)
    def _(step):
        inner = pl.ds(pl.multiple_of(8 * step, 8), 8)
        rows = pl.ds(pl.multiple_of(8 * step + 8, 8), 8)
        outer = [
            edge_primitives([edges[18 * side + 3 * k + plane, inner, :] for k in range(6)])
            for side in range(2)
            for plane in range(3)
        ]
        column = (
            outer[0:3] + [[prims[0, p, k, rows, :] for k in range(6)] for p in range(3)] + outer[3:6]
        )
        flux = z_fluxes(column)
        for plane in range(3):
            for k in range(6):
                difference = flux[plane + 1][k] - flux[plane][k]
                if k == 5:
                    spread = 0.5 * (column[plane + 4][3] - column[plane + 2][3])
                    difference = difference + column[plane + 3][4] * spread
                updated[k, plane, inner, :] = -difference

    @functools.partial(each, 3)
    def _(plane):
        x_sweep(prims.at[0, plane], low_ref, high_ref, face_ref, flux_ref)
        for row in (8, 16):
            rows = pl.ds(row, 8)
            inner = pl.ds(row - 8, 8)
            both = [[prims[tile, plane, k, rows, :] for k in range(6)] for tile in range(2)]
            differences, spread = y_differences(*both)
            before = prims[0, plane, 1, pl.ds(row - 1, 8), :]
            after = prims[0, plane, 1, pl.ds(row + 1, 8), :]
            spread = spread[0] + 0.5 * (after - before)
            rate = []
            for k in range(6):
                across = flux_ref[k, rows, :] - flux_ref[k, pl.ds(row - 1, 8), :]
                rate.append(updated[k, plane, inner, :] - differences[0][k] - across)
            rate[5] = rate[5] - both[0][4] * spread
            stage = [section[0, plane, k, rows, :] for k in range(6)]
            drive = [force[0, 3 * k + plane, rows, :] for k in range(3)]
            rate = forced(stage, drive, rate)
            values = [fields[0, 3 * k + plane, rows, :] for k in range(7)]
            result = [
                0.5 * values[k] + 0.5 * (stage[k] + time_step * rate[k]) for k in range(6)
            ]
            settle(result, values[6], 1.0 / result[0])
            for k in range(6):
                updated[k, plane, inner, :] = result[k]


def shape(*sizes):
    return jax.ShapeDtypeStruct(sizes, F32)


def vmem_specs(count):
    return [pl.BlockSpec(memory_space=pltpu.VMEM)] * count


def call(kernel, name, outs, scalars, arrays, scratch=(), cost=0):
    single = not isinstance(outs, tuple)
    return pl.pallas_call(
        kernel,
        out_shape=outs,
        in_specs=[pl.BlockSpec(memory_space=pltpu.SMEM)] * len(scalars) + vmem_specs(len(arrays)),
        out_specs=vmem_specs(1)[0] if single else tuple(vmem_specs(len(outs))),
        scratch_shapes=list(scratch),
        compiler_params=pltpu.CompilerParams(vmem_limit_bytes=VMEM_LIMIT),
        cost_estimate=pl.CostEstimate(flops=cost, bytes_accessed=cost, transcendentals=0),
        name=name,
    )(*scalars, *arrays)


def pairs(count, begin):
    table = []
    for first in range(begin, begin + count, 2):
        low, high = first % count, (first + 1) % count
        table += [(low, high), (high, low)]
    return table


def exchanged(rows, after, axes):
    count = lax.axis_size(axes)
    spread = pl.pallas_call(
        spread_kernel,
        out_shape=shape(count, 2, LANES),
        in_specs=[*vmem_specs(1), pl.BlockSpec(memory_space=pl.ANY)],
        out_specs=vmem_specs(1)[0],
        compiler_params=pltpu.CompilerParams(vmem_limit_bytes=VMEM_LIMIT),
        name="spread",
    )(rows, after)
    return lax.all_to_all(spread, axes, 0, 0, tiled=True)


GX = ("zl", "core")
GY = ("y", "zh", "x")


def local(fluid_state, switch, z_edges, forcing):
    count_x = lax.axis_size(GX)
    count_y = lax.axis_size(GY)
    cells = 3.0 * ROWS * LANES * count_x * count_y
    place = jnp.stack([lax.axis_index(GX) % 2, lax.axis_index(GY) % 2]).astype(jnp.int32)
    tile = (8, LANES)
    block = (ROWS, LANES)
    inputs = (
        fluid_state.reshape(18, *block),
        switch,
        z_edges.reshape(EDGES, *block),
        forcing.reshape(FORCES, *block),
    )
    pair_out, odd_out, *arrays = pl.pallas_call(
        first_kernel,
        out_shape=(
            shape(X_TILES + 1, *tile),
            shape(X_TILES, *tile),
            *(jax.ShapeDtypeStruct(values.shape, values.dtype) for values in inputs),
        ),
        in_specs=[
            pl.BlockSpec(memory_space=pltpu.SMEM),
            *([pl.BlockSpec(memory_space=pltpu.HBM)] * 4),
        ],
        out_specs=tuple(vmem_specs(6)),
        scratch_shapes=[pltpu.SemaphoreType.DMA((4,))],
        compiler_params=pltpu.CompilerParams(vmem_limit_bytes=VMEM_LIMIT),
        name="first",
    )(place, *(pltpu.with_memory_space_constraint(values, pltpu.HBM) for values in inputs))
    pair_in = lax.all_gather(pair_out, "core")
    odd_in = lax.ppermute(odd_out, GX, pairs(count_x, 1))
    totals = exchanged(pair_in[:, X_TILES, 0:2], place, ("y", "x"))
    strips = call(
        second_kernel,
        "second",
        (shape(EXT + 2 * ROWS, LANES), shape(EXT + 2 * ROWS, LANES)),
        (place,),
        (*arrays, pair_in, odd_in),
        cost=4_000_000,
    )
    even_in = lax.ppermute(strips[0], GY, pairs(count_y, 0))
    odd_y_in = lax.ppermute(strips[1], GY, pairs(count_y, 1))
    totals = exchanged(totals, even_in, ("zh", "zl"))
    extended = (EXT, LANES)
    work = [pltpu.VMEM((6, *extended), F32) for _ in range(4)]
    fields, force, tend = call(
        third_kernel,
        "third",
        (shape(2, FIELDS, *extended), shape(2, FORCES, *extended), shape(2, 18, *extended)),
        (place,),
        (*arrays, pair_in, odd_in, even_in, odd_y_in),
        [
            pltpu.VMEM((2, 3, 6, *extended), F32),
            pltpu.VMEM((2, 6, 6, *extended), F32),
            *work,
            pltpu.VMEM((2, EXT + 2 * ROWS, LANES), F32),
        ],
        cost=60_000_000,
    )
    return call(
        functools.partial(fourth_kernel, cells),
        "fourth",
        shape(6, 3, ROWS, LANES),
        (),
        (totals, fields, force, tend, arrays[2]),
        [
            pltpu.VMEM((2, 3, 6, *extended), F32),
            pltpu.VMEM((2, 3, 6, *extended), F32),
            *work,
        ],
        cost=8_000_000,
    )


def solution(mesh):
    count_x, count_y = mesh.devices.shape
    count_z = 2 if count_y % 8 == 0 else 1
    parts = (count_x // 2, 2, count_y // (4 * count_z), count_z, 4)
    split = Mesh(mesh.devices.reshape(parts), (*GX, *GY))
    return jax.shard_map(
        local,
        mesh=split,
        in_specs=(
            P(None, None, GX, GY),
            P(None, GX, GY),
            P(None, None, None, GX, GY),
            P(None, None, GX, GY),
        ),
        out_specs=P(None, None, GX, GY),
        check_vma=False,
    )
```

```python
import functools

import jax
import jax.numpy as jnp
from jax import lax
from jax.experimental import pallas as pl
from jax.experimental.pallas import tpu as pltpu
from jax.sharding import Mesh
from jax.sharding import PartitionSpec as P

ADIABATIC = 5.0 / 3.0
CFL_NUMBER = 0.4
INJECTION = 0.04
LANES = 128
ROWS = 16
EXT = 32
FIELDS = 21
EDGES = 36
FORCES = 9
X_TILES = FIELDS + EDGES + FORCES
VMEM_LIMIT = 16 * 1024 * 1024
F32 = jnp.float32


def lane_index(shape):
    return lax.broadcasted_iota(jnp.int32, shape, len(shape) - 1)


def roll(values, shift, axis):
    size = values.shape[axis]
    shift = shift % size
    return values if shift == 0 else pltpu.roll(values, shift, axis)


def each(count, body):
    def step(index, carry):
        body(index)
        return carry

    lax.fori_loop(0, count, step, 0)


def x_place(refs, index):
    state, switch, edges, forcing = refs
    if index < 18:
        return lambda rows: state[index, rows, :]
    index -= 18
    if index < 3:
        return lambda rows: switch[index, rows, :].astype(F32)
    index -= 3
    if index < EDGES:
        return lambda rows: edges[index, rows, :]
    index -= EDGES
    return lambda rows: forcing[index, rows, :]


def first_kernel(
    place, state_in, switch_in, edges_in, forcing_in,
    pair_out, odd_out, state, switch, edges, forcing, arrived,
):
    refs = (state, switch, edges, forcing)
    copies = [
        pltpu.make_async_copy(source, target, arrived.at[k])
        for k, (source, target) in enumerate(
            zip((state_in, switch_in, edges_in, forcing_in), refs, strict=True)
        )
    ]
    for copy in copies:
        copy.start()
    odd = place[0]
    near = pl.multiple_of(8 * (1 - odd), 8)
    far = pl.multiple_of(8 * odd, 8)
    for k in (0, 1, 3):
        copies[k].wait()
    peak = None
    total = None
    for plane in range(3):
        fields = [state[3 * k + plane] for k in range(6)]
        density = fields[0]
        inverse = 1.0 / density
        kinetic = 0.5 * inverse * (fields[1] ** 2 + fields[2] ** 2 + fields[3] ** 2)
        heat = jnp.where(switch[plane] == 1, fields[5], fields[4] - kinetic)
        sound = jnp.sqrt(ADIABATIC * (ADIABATIC - 1.0) * heat * inverse)
        speed = (
            jnp.abs(fields[1]) + jnp.abs(fields[2]) + jnp.abs(fields[3])
        ) * inverse + 3.0 * sound
        drive = [forcing[3 * k + plane] for k in range(3)]
        power = density * (drive[0] ** 2 + drive[1] ** 2 + drive[2] ** 2)
        peak = speed if peak is None else jnp.maximum(peak, speed)
        total = power if total is None else total + power
    row = lax.broadcasted_iota(jnp.int32, (8, LANES), 0)
    pair_out[X_TILES] = jnp.where(row == 0, jnp.max(peak), jnp.sum(total))
    copies[2].wait()
    for index in range(X_TILES):
        tile = x_place(refs, index)
        pair_out[index] = tile(pl.ds(near, 8))
        odd_out[index] = tile(pl.ds(far, 8))


def spread_kernel(rows, after, out):
    peak = jnp.max(rows[:, 0, :], axis=0, keepdims=True)
    total = jnp.sum(rows[:, 1, :], axis=0, keepdims=True)
    joined = jnp.concatenate([peak, total], axis=0)
    out[...] = jnp.broadcast_to(joined[None], out.shape)


def rows_around(odd_x, pair_in, odd_in, index, block):
    from_pair = pair_in[1 - odd_x, index]
    from_odd = odd_in[index]
    below = jnp.where(odd_x == 0, from_odd, from_pair)
    above = jnp.where(odd_x == 0, from_pair, from_odd)
    return jnp.concatenate([below, block, above], axis=0)


def turned(values, shift):
    return pltpu.roll(values, lax.rem(shift + LANES, LANES), 1)


def second_kernel(place, state, switch, edges, forcing, pair_in, odd_in, even_out, odd_out):
    odd_x = place[0]
    odd_y = place[1]
    lane = lane_index((EXT, LANES))
    high = jnp.zeros((EXT, LANES), F32)
    low = jnp.zeros((EXT, LANES), F32)
    for index in range(FIELDS):
        block = x_place((state, switch, edges, forcing), index)(slice(0, ROWS))
        column = rows_around(odd_x, pair_in, odd_in, index, block)
        mine = (lane >= 6 * index) & (lane < 6 * index + 6)
        high = jnp.where(mine, roll(column, 6 * index - 122, 1), high)
        low = jnp.where(mine, roll(column, 6 * index, 1), low)
    even_out[0:EXT] = jnp.where(odd_y == 0, high, low)
    odd_out[0:EXT] = jnp.where(odd_y == 0, low, high)
    lane = lane[0:ROWS]
    for source, count, row in ((edges, EDGES, EXT), (forcing, FORCES, EXT + ROWS)):
        high = jnp.zeros((ROWS, LANES), F32)
        low = jnp.zeros((ROWS, LANES), F32)
        for index in range(count):
            mine = (lane >= 3 * index) & (lane < 3 * index + 3)
            high = jnp.where(mine, roll(source[index], 3 * index - 125, 1), high)
            low = jnp.where(mine, roll(source[index], 3 * index, 1), low)
        even_out[row : row + ROWS] = jnp.where(odd_y == 0, high, low)
        odd_out[row : row + ROWS] = jnp.where(odd_y == 0, low, high)


def median(one, two, three):
    return jnp.maximum(jnp.minimum(one, two), jnp.minimum(jnp.maximum(one, two), three))


def face_above(before, here, after, beyond):
    value = (7.0 / 12.0) * (here + after) - (1.0 / 12.0) * (before + beyond)
    return median(here, after, value)


def limited(here, face_low, face_high):
    thrice = 3.0 * here
    return (
        median(here, face_low, thrice - (face_high + face_high)),
        median(here, face_high, thrice - (face_low + face_low)),
    )


def sound_of(state):
    push = ADIABATIC * state[4]
    return push * lax.rsqrt(push * state[0])


def face_flux(left, right, normal):
    left_u, right_u = left[1 + normal], right[1 + normal]
    left_sound, right_sound = sound_of(left), sound_of(right)
    slow = jnp.minimum(jnp.minimum(left_u - left_sound, right_u - right_sound), 0.0)
    fast = jnp.maximum(jnp.maximum(left_u + left_sound, right_u + right_sound), 0.0)
    share = 1.0 / (fast - slow)
    left_part = fast * share
    right_part = -slow * share
    left_lead = left_u - slow
    right_lead = right_u - fast
    left_mass = left_part * left_lead * left[0]
    right_mass = right_part * right_lead * right[0]
    left_square = left[1] * left[1] + left[2] * left[2] + left[3] * left[3]
    right_square = right[1] * right[1] + right[2] * right[2] + right[3] * right[3]
    flux = [left_mass + right_mass]
    for k in (1, 2, 3):
        flux.append(left_mass * left[k] + right_mass * right[k])
    left_push = left_part * left[4]
    right_push = right_part * right[4]
    flux[1 + normal] = flux[1 + normal] + (left_push + right_push)
    flux.append(
        0.5 * (left_mass * left_square + right_mass * right_square)
        + left_push * (1.5 * left_lead + left_u)
        + right_push * (1.5 * right_lead + right_u)
    )
    flux.append(left_mass * left[5] + right_mass * right[5])
    return flux


def z_fluxes(planes):
    lower, upper = [], []
    for k in range(6):
        column = [planes[j][k] for j in range(9)]
        faces = [face_above(*column[j : j + 4]) for j in range(6)]
        cells = [limited(column[j + 2], faces[j], faces[j + 1]) for j in range(5)]
        lower.append([cells[j][1] for j in range(4)])
        upper.append([cells[j + 1][0] for j in range(4)])
    return [
        face_flux([lower[k][j] for k in range(6)], [upper[k][j] for k in range(6)], 2)
        for j in range(4)
    ]


def edge_primitives(fields):
    density = fields[0]
    inverse = 1.0 / density
    kinetic = 0.5 * inverse * (fields[1] ** 2 + fields[2] ** 2 + fields[3] ** 2)
    return [
        density,
        fields[1] * inverse,
        fields[2] * inverse,
        fields[3] * inverse,
        (ADIABATIC - 1.0) * (fields[4] - kinetic),
        fields[5] * inverse,
    ]


def shift_pair(main, rim, step):
    lane = lane_index(main.shape)
    main_rolled = roll(main, -step, 1)
    rim_rolled = roll(rim, -step, 1)
    inside = lane < LANES - step if step > 0 else lane >= -step
    return (
        jnp.where(inside, main_rolled, rim_rolled),
        jnp.where(inside, rim_rolled, main_rolled),
    )


def y_differences(main, rim):
    lows, highs = ([], []), ([], [])
    spread = None
    for k in range(6):
        here = (main[k], rim[k])
        before = shift_pair(*here, -1)
        after = shift_pair(*here, 1)
        beyond = shift_pair(*here, 2)
        faces = [face_above(before[j], here[j], after[j], beyond[j]) for j in range(2)]
        below = shift_pair(*faces, -1)
        cells = [limited(here[j], below[j], faces[j]) for j in range(2)]
        nexts = shift_pair(cells[0][0], cells[1][0], 1)
        for j in range(2):
            lows[j].append(cells[j][1])
            highs[j].append(nexts[j])
        if k == 2:
            spread = [0.5 * (after[j] - before[j]) for j in range(2)]
    fluxes = [face_flux(lows[j], highs[j], 1) for j in range(2)]
    differences = ([], [])
    for k in range(6):
        below = shift_pair(fluxes[0][k], fluxes[1][k], -1)
        for j in range(2):
            differences[j].append(fluxes[j][k] - below[j])
    return differences, spread


CHUNKS = (4, 12, 20)


def x_sweep(prims, low_ref, high_ref, face_ref, flux_ref):
    for row in CHUNKS:
        for k in range(6):
            before, here, after, beyond = [
                prims[k, pl.ds(row + s, 8), :] for s in (-1, 0, 1, 2)
            ]
            if row == CHUNKS[0]:
                below = face_above(prims[k, pl.ds(row - 2, 8), :], before, here, after)
            above = face_above(before, here, after, beyond)
            face_ref[k, pl.ds(row, 8), :] = above
            if row != CHUNKS[0]:
                below = face_ref[k, pl.ds(row - 1, 8), :]
            low_ref[k, pl.ds(row, 8), :], high_ref[k, pl.ds(row, 8), :] = limited(
                here, below, above
            )
    for row in CHUNKS:
        left = [high_ref[k, pl.ds(row, 8), :] for k in range(6)]
        right = [low_ref[k, pl.ds(row + 1, 8), :] for k in range(6)]
        flux = face_flux(left, right, 0)
        for k in range(6):
            flux_ref[k, pl.ds(row, 8), :] = flux[k]


def clear_ends(low_ref, flux_ref):
    for k in range(6):
        low_ref[k, pl.ds(28, 4), :] = jnp.ones((4, LANES), F32)
        flux_ref[k, pl.ds(0, 4), :] = jnp.zeros((4, LANES), F32)


def third_kernel(
    place, state, switch, edges, forcing, pair_in, odd_in, even_in, odd_y_in,
    fields, force, tend, prims, planes, low_ref, high_ref, face_ref, flux_ref, strip_ref,
):
    odd_x = place[0]
    odd_y = place[1]
    strip_ref[0] = jnp.where(odd_y == 0, even_in[...], odd_y_in[...])
    strip_ref[1] = jnp.where(odd_y == 0, odd_y_in[...], even_in[...])
    clear_ends(low_ref, flux_ref)
    lane = lane_index((EXT, LANES))
    edge_lane = lane[0:ROWS]

    def field_tiles(index, block):
        fields[0, index] = rows_around(odd_x, pair_in, odd_in, index, block)
        fields[1, index] = jnp.where(
            lane < 64,
            turned(strip_ref[0, 0:EXT], -6 * index),
            turned(strip_ref[1, 0:EXT], 122 - 6 * index),
        )

    def rim_tile(row, index):
        return jnp.where(
            edge_lane < 64,
            turned(strip_ref[0, row : row + ROWS], -3 * index),
            turned(strip_ref[1, row : row + ROWS], 125 - 3 * index),
        )

    @functools.partial(each, 6)
    def _(field):
        for plane in range(3):
            index = 3 * field + plane
            field_tiles(index, state[index])

    for plane in range(3):
        field_tiles(18 + plane, switch[plane].astype(F32))

    @functools.partial(each, 3)
    def _(part):
        for k in range(3):
            index = 3 * part + k
            force[0, index] = rows_around(
                odd_x, pair_in, odd_in, FIELDS + EDGES + index, forcing[index]
            )
            force[1, index, 0:8] = jnp.zeros((8, LANES), F32)
            force[1, index, 8:24] = rim_tile(EXT + ROWS, index)
            force[1, index, 24:32] = jnp.zeros((8, LANES), F32)

    @functools.partial(each, 6)
    def _(step):
        tile, plane = step // 3, step % 3
        values = [fields[tile, 3 * k + plane] for k in range(7)]
        density = values[0]
        inverse = 1.0 / density
        kinetic = 0.5 * inverse * (values[1] ** 2 + values[2] ** 2 + values[3] ** 2)
        heat = jnp.where(values[6] == 1.0, values[5], values[4] - kinetic)
        prims[tile, plane, 0] = density
        for k in (1, 2, 3):
            prims[tile, plane, k] = values[k] * inverse
        prims[tile, plane, 4] = (ADIABATIC - 1.0) * heat
        prims[tile, plane, 5] = values[5] * inverse

    @functools.partial(each, 6)
    def _(step):
        first = 18 * (step // 3) + step % 3
        places = [first + 3 * k for k in range(6)]
        values = edge_primitives(
            [rows_around(odd_x, pair_in, odd_in, FIELDS + k, edges[k]) for k in places]
        )
        for k in range(6):
            planes[0, step, k] = values[k]
        values = edge_primitives([rim_tile(EXT, k) for k in places])
        for k in range(6):
            planes[1, step, k, 0:8] = jnp.ones((8, LANES), F32)
            planes[1, step, k, 8:24] = values[k]
            planes[1, step, k, 24:32] = jnp.ones((8, LANES), F32)

    @functools.partial(each, 3)
    def _(plane):
        for row in CHUNKS:
            rows = pl.ds(row, 8)
            both = [[prims[tile, plane, k, rows, :] for k in range(6)] for tile in range(2)]
            differences, spread = y_differences(*both)
            for tile in range(2):
                for k in range(5):
                    tend[tile, 3 * k + plane, rows, :] = -differences[tile][k]
                tend[tile, 15 + plane, rows, :] = (
                    -differences[tile][5] - both[tile][4] * spread[tile]
                )

    @functools.partial(each, 6)
    def _(step):
        tile, plane = step // 3, step % 3
        x_sweep(prims.at[tile, plane], low_ref, high_ref, face_ref, flux_ref)
        for row in CHUNKS:
            rows = pl.ds(row, 8)
            for k in range(6):
                difference = flux_ref[k, rows, :] - flux_ref[k, pl.ds(row - 1, 8), :]
                if k == 5:
                    before = prims[tile, plane, 1, pl.ds(row - 1, 8), :]
                    after = prims[tile, plane, 1, pl.ds(row + 1, 8), :]
                    spread = 0.5 * (after - before)
                    difference = difference + prims[tile, plane, 4, rows, :] * spread
                tend[tile, 3 * k + plane, rows, :] -= difference

    @functools.partial(each, 2)
    def _(tile):
        for row in CHUNKS:
            rows = pl.ds(row, 8)
            column = (
                [[planes[tile, p, k, rows, :] for k in range(6)] for p in range(3)]
                + [[prims[tile, p, k, rows, :] for k in range(6)] for p in range(3)]
                + [[planes[tile, 3 + p, k, rows, :] for k in range(6)] for p in range(3)]
            )
            flux = z_fluxes(column)
            for plane in range(3):
                for k in range(6):
                    difference = flux[plane + 1][k] - flux[plane][k]
                    if k == 5:
                        spread = 0.5 * (column[plane + 4][3] - column[plane + 2][3])
                        difference = difference + column[plane + 3][4] * spread
                    tend[tile, 3 * k + plane, rows, :] -= difference


def fourth_kernel(
    cells, totals, fields, force, tend, edges, out,
    updated, section, prims, low_ref, high_ref, face_ref, flux_ref, sent,
):
    peak = jnp.max(totals[:, 0, :], axis=0, keepdims=True)
    power = jnp.sum(totals[:, 1, :], axis=0, keepdims=True)
    time_step = CFL_NUMBER / peak
    scale = jnp.sqrt(INJECTION / (0.5 * time_step * (power / cells + 1e-06)))
    clear_ends(low_ref, flux_ref)

    def forced(values, drive, tendency):
        result = list(tendency)
        for k in (1, 2, 3):
            result[k] = result[k] + scale * values[0] * drive[k - 1]
        result[4] = result[4] + scale * (
            values[1] * drive[0] + values[2] * drive[1] + values[3] * drive[2]
        )
        return result

    def settle(values, switch, inverse):
        kinetic = 0.5 * inverse * (values[1] ** 2 + values[2] ** 2 + values[3] ** 2)
        values[5] = jnp.where(switch == 0.0, values[4] - kinetic, values[5])

    @functools.partial(each, 6)
    def _(step):
        tile, plane = step // 3, step % 3
        for row in CHUNKS:
            rows = pl.ds(row, 8)
            values = [fields[tile, 3 * k + plane, rows, :] for k in range(7)]
            drive = [force[tile, 3 * k + plane, rows, :] for k in range(3)]
            rate = forced(values, drive, [tend[tile, 3 * k + plane, rows, :] for k in range(6)])
            stage = [values[k] + time_step * rate[k] for k in range(6)]
            inverse = 1.0 / stage[0]
            settle(stage, values[6], inverse)
            for k in range(6):
                section[tile, plane, k, rows, :] = stage[k]
            prims[tile, plane, 0, rows, :] = stage[0]
            for k in (1, 2, 3):
                prims[tile, plane, k, rows, :] = stage[k] * inverse
            prims[tile, plane, 4, rows, :] = (ADIABATIC - 1.0) * stage[5]
            prims[tile, plane, 5, rows, :] = stage[5] * inverse

    @functools.partial(each, 2)
    def _(step):
        inner = pl.ds(pl.multiple_of(8 * step, 8), 8)
        rows = pl.ds(pl.multiple_of(8 * step + 8, 8), 8)
        outer = [
            edge_primitives([edges[18 * side + 3 * k + plane, inner, :] for k in range(6)])
            for side in range(2)
            for plane in range(3)
        ]
        column = (
            outer[0:3] + [[prims[0, p, k, rows, :] for k in range(6)] for p in range(3)] + outer[3:6]
        )
        flux = z_fluxes(column)
        for plane in range(3):
            for k in range(6):
                difference = flux[plane + 1][k] - flux[plane][k]
                if k == 5:
                    spread = 0.5 * (column[plane + 4][3] - column[plane + 2][3])
                    difference = difference + column[plane + 3][4] * spread
                updated[k, plane, inner, :] = -difference

    @functools.partial(each, 3)
    def _(plane):
        x_sweep(prims.at[0, plane], low_ref, high_ref, face_ref, flux_ref)
        for row in (8, 16):
            rows = pl.ds(row, 8)
            inner = pl.ds(row - 8, 8)
            both = [[prims[tile, plane, k, rows, :] for k in range(6)] for tile in range(2)]
            differences, spread = y_differences(*both)
            before = prims[0, plane, 1, pl.ds(row - 1, 8), :]
            after = prims[0, plane, 1, pl.ds(row + 1, 8), :]
            spread = spread[0] + 0.5 * (after - before)
            rate = []
            for k in range(6):
                across = flux_ref[k, rows, :] - flux_ref[k, pl.ds(row - 1, 8), :]
                rate.append(updated[k, plane, inner, :] - differences[0][k] - across)
            rate[5] = rate[5] - both[0][4] * spread
            stage = [section[0, plane, k, rows, :] for k in range(6)]
            drive = [force[0, 3 * k + plane, rows, :] for k in range(3)]
            rate = forced(stage, drive, rate)
            values = [fields[0, 3 * k + plane, rows, :] for k in range(7)]
            result = [
                0.5 * values[k] + 0.5 * (stage[k] + time_step * rate[k]) for k in range(6)
            ]
            settle(result, values[6], 1.0 / result[0])
            for k in range(6):
                updated[k, plane, inner, :] = result[k]
        pltpu.make_async_copy(updated.at[:, plane], out.at[:, plane], sent.at[plane]).start()

    for plane in range(3):
        pltpu.make_async_copy(updated.at[:, plane], out.at[:, plane], sent.at[plane]).wait()


def shape(*sizes):
    return jax.ShapeDtypeStruct(sizes, F32)


def vmem_specs(count):
    return [pl.BlockSpec(memory_space=pltpu.VMEM)] * count


def call(kernel, name, outs, scalars, arrays, scratch=(), cost=0, out_space=pltpu.VMEM):
    single = not isinstance(outs, tuple)
    out_spec = pl.BlockSpec(memory_space=out_space)
    return pl.pallas_call(
        kernel,
        out_shape=outs,
        in_specs=[pl.BlockSpec(memory_space=pltpu.SMEM)] * len(scalars) + vmem_specs(len(arrays)),
        out_specs=out_spec if single else (out_spec,) * len(outs),
        scratch_shapes=list(scratch),
        compiler_params=pltpu.CompilerParams(vmem_limit_bytes=VMEM_LIMIT),
        cost_estimate=pl.CostEstimate(flops=cost, bytes_accessed=cost, transcendentals=0),
        name=name,
    )(*scalars, *arrays)


def pairs(count, begin):
    table = []
    for first in range(begin, begin + count, 2):
        low, high = first % count, (first + 1) % count
        table += [(low, high), (high, low)]
    return table


def exchanged(rows, after, axes):
    count = lax.axis_size(axes)
    spread = pl.pallas_call(
        spread_kernel,
        out_shape=shape(count, 2, LANES),
        in_specs=[*vmem_specs(1), pl.BlockSpec(memory_space=pl.ANY)],
        out_specs=vmem_specs(1)[0],
        compiler_params=pltpu.CompilerParams(vmem_limit_bytes=VMEM_LIMIT),
        name="spread",
    )(rows, after)
    return lax.all_to_all(spread, axes, 0, 0, tiled=True)


GX = ("zl", "core")
GY = ("y", "zh", "x")


def local(fluid_state, switch, z_edges, forcing):
    count_x = lax.axis_size(GX)
    count_y = lax.axis_size(GY)
    cells = 3.0 * ROWS * LANES * count_x * count_y
    place = jnp.stack([lax.axis_index(GX) % 2, lax.axis_index(GY) % 2]).astype(jnp.int32)
    tile = (8, LANES)
    block = (ROWS, LANES)
    inputs = (
        fluid_state.reshape(18, *block),
        switch,
        z_edges.reshape(EDGES, *block),
        forcing.reshape(FORCES, *block),
    )
    pair_out, odd_out, *arrays = pl.pallas_call(
        first_kernel,
        out_shape=(
            shape(X_TILES + 1, *tile),
            shape(X_TILES, *tile),
            *(jax.ShapeDtypeStruct(values.shape, values.dtype) for values in inputs),
        ),
        in_specs=[
            pl.BlockSpec(memory_space=pltpu.SMEM),
            *([pl.BlockSpec(memory_space=pltpu.HBM)] * 4),
        ],
        out_specs=tuple(vmem_specs(6)),
        scratch_shapes=[pltpu.SemaphoreType.DMA((4,))],
        compiler_params=pltpu.CompilerParams(vmem_limit_bytes=VMEM_LIMIT),
        name="first",
    )(place, *(pltpu.with_memory_space_constraint(values, pltpu.HBM) for values in inputs))
    pair_in = lax.all_gather(pair_out, "core")
    odd_in = lax.ppermute(odd_out, GX, pairs(count_x, 1))
    totals = exchanged(pair_in[:, X_TILES, 0:2], place, ("y", "x"))
    strips = call(
        second_kernel,
        "second",
        (shape(EXT + 2 * ROWS, LANES), shape(EXT + 2 * ROWS, LANES)),
        (place,),
        (*arrays, pair_in, odd_in),
        cost=4_000_000,
    )
    even_in = lax.ppermute(strips[0], GY, pairs(count_y, 0))
    odd_y_in = lax.ppermute(strips[1], GY, pairs(count_y, 1))
    totals = exchanged(totals, even_in, ("zh", "zl"))
    extended = (EXT, LANES)
    work = [pltpu.VMEM((6, *extended), F32) for _ in range(4)]
    fields, force, tend = call(
        third_kernel,
        "third",
        (shape(2, FIELDS, *extended), shape(2, FORCES, *extended), shape(2, 18, *extended)),
        (place,),
        (*arrays, pair_in, odd_in, even_in, odd_y_in),
        [
            pltpu.VMEM((2, 3, 6, *extended), F32),
            pltpu.VMEM((2, 6, 6, *extended), F32),
            *work,
            pltpu.VMEM((2, EXT + 2 * ROWS, LANES), F32),
        ],
        cost=60_000_000,
    )
    return call(
        functools.partial(fourth_kernel, cells),
        "fourth",
        shape(6, 3, ROWS, LANES),
        (),
        (totals, fields, force, tend, arrays[2]),
        [
            pltpu.VMEM((6, 3, ROWS, LANES), F32),
            pltpu.VMEM((2, 3, 6, *extended), F32),
            pltpu.VMEM((2, 3, 6, *extended), F32),
            *work,
            pltpu.SemaphoreType.DMA((3,)),
        ],
        cost=8_000_000,
        out_space=pltpu.HBM,
    )


def solution(mesh):
    count_x, count_y = mesh.devices.shape
    count_z = 2 if count_y % 8 == 0 else 1
    parts = (count_x // 2, 2, count_y // (4 * count_z), count_z, 4)
    split = Mesh(mesh.devices.reshape(parts), (*GX, *GY))
    return jax.shard_map(
        local,
        mesh=split,
        in_specs=(
            P(None, None, GX, GY),
            P(None, GX, GY),
            P(None, None, None, GX, GY),
            P(None, None, GX, GY),
        ),
        out_specs=P(None, None, GX, GY),
        check_vma=False,
    )
```

```python
import functools

import jax
import jax.numpy as jnp
from jax import lax
from jax.experimental import pallas as pl
from jax.experimental.pallas import tpu as pltpu
from jax.sharding import Mesh
from jax.sharding import PartitionSpec as P

ADIABATIC = 5.0 / 3.0
CFL_NUMBER = 0.4
INJECTION = 0.04
LANES = 128
ROWS = 16
EXT = 32
FIELDS = 21
EDGES = 36
FORCES = 9
X_TILES = FIELDS + EDGES + FORCES
VMEM_LIMIT = 16 * 1024 * 1024
F32 = jnp.float32


def lane_index(shape):
    return lax.broadcasted_iota(jnp.int32, shape, len(shape) - 1)


def roll(values, shift, axis):
    size = values.shape[axis]
    shift = shift % size
    return values if shift == 0 else pltpu.roll(values, shift, axis)


def each(count, body):
    def step(index, carry):
        body(index)
        return carry

    lax.fori_loop(0, count, step, 0)


def x_place(refs, index):
    state, switch, edges, forcing = refs
    if index < 18:
        return lambda rows: state[index, rows, :]
    index -= 18
    if index < 3:
        return lambda rows: switch[index, rows, :].astype(F32)
    index -= 3
    if index < EDGES:
        return lambda rows: edges[index, rows, :]
    index -= EDGES
    return lambda rows: forcing[index, rows, :]


def first_kernel(
    place, state_in, switch_in, edges_in, forcing_in,
    pair_out, odd_out, state, switch, edges, forcing, arrived,
):
    refs = (state, switch, edges, forcing)
    copies = [
        pltpu.make_async_copy(source, target, arrived.at[k])
        for k, (source, target) in enumerate(
            zip((state_in, switch_in, edges_in, forcing_in), refs, strict=True)
        )
    ]
    for copy in copies:
        copy.start()
    odd = place[0]
    near = pl.multiple_of(8 * (1 - odd), 8)
    far = pl.multiple_of(8 * odd, 8)
    for k in (0, 1, 3):
        copies[k].wait()
    peak = None
    total = None
    for plane in range(3):
        fields = [state[3 * k + plane] for k in range(6)]
        density = fields[0]
        inverse = 1.0 / density
        kinetic = 0.5 * inverse * (fields[1] ** 2 + fields[2] ** 2 + fields[3] ** 2)
        heat = jnp.where(switch[plane] == 1, fields[5], fields[4] - kinetic)
        sound = jnp.sqrt(ADIABATIC * (ADIABATIC - 1.0) * heat * inverse)
        speed = (
            jnp.abs(fields[1]) + jnp.abs(fields[2]) + jnp.abs(fields[3])
        ) * inverse + 3.0 * sound
        drive = [forcing[3 * k + plane] for k in range(3)]
        power = density * (drive[0] ** 2 + drive[1] ** 2 + drive[2] ** 2)
        peak = speed if peak is None else jnp.maximum(peak, speed)
        total = power if total is None else total + power
    row = lax.broadcasted_iota(jnp.int32, (8, LANES), 0)
    pair_out[X_TILES] = jnp.where(row == 0, jnp.max(peak), jnp.sum(total))
    copies[2].wait()
    for index in range(X_TILES):
        tile = x_place(refs, index)
        pair_out[index] = tile(pl.ds(near, 8))
        odd_out[index] = tile(pl.ds(far, 8))


def spread_kernel(rows, after, out):
    peak = jnp.max(rows[:, 0, :], axis=0, keepdims=True)
    total = jnp.sum(rows[:, 1, :], axis=0, keepdims=True)
    joined = jnp.concatenate([peak, total], axis=0)
    out[...] = jnp.broadcast_to(joined[None], out.shape)


def rows_around(odd_x, pair_in, odd_in, index, block):
    from_pair = pair_in[1 - odd_x, index]
    from_odd = odd_in[index]
    below = jnp.where(odd_x == 0, from_odd, from_pair)
    above = jnp.where(odd_x == 0, from_pair, from_odd)
    return jnp.concatenate([below, block, above], axis=0)


def turned(values, shift):
    return pltpu.roll(values, lax.rem(shift + LANES, LANES), 1)


def second_kernel(place, state, switch, edges, forcing, pair_in, odd_in, even_out, odd_out):
    odd_x = place[0]
    odd_y = place[1]
    lane = lane_index((EXT, LANES))
    high = jnp.zeros((EXT, LANES), F32)
    low = jnp.zeros((EXT, LANES), F32)
    for index in range(FIELDS):
        block = x_place((state, switch, edges, forcing), index)(slice(0, ROWS))
        column = rows_around(odd_x, pair_in, odd_in, index, block)
        mine = (lane >= 6 * index) & (lane < 6 * index + 6)
        high = jnp.where(mine, roll(column, 6 * index - 122, 1), high)
        low = jnp.where(mine, roll(column, 6 * index, 1), low)
    even_out[0:EXT] = jnp.where(odd_y == 0, high, low)
    odd_out[0:EXT] = jnp.where(odd_y == 0, low, high)
    lane = lane[0:ROWS]
    for source, count, row in ((edges, EDGES, EXT), (forcing, FORCES, EXT + ROWS)):
        high = jnp.zeros((ROWS, LANES), F32)
        low = jnp.zeros((ROWS, LANES), F32)
        for index in range(count):
            mine = (lane >= 3 * index) & (lane < 3 * index + 3)
            high = jnp.where(mine, roll(source[index], 3 * index - 125, 1), high)
            low = jnp.where(mine, roll(source[index], 3 * index, 1), low)
        even_out[row : row + ROWS] = jnp.where(odd_y == 0, high, low)
        odd_out[row : row + ROWS] = jnp.where(odd_y == 0, low, high)


def median(one, two, three):
    return jnp.maximum(jnp.minimum(one, two), jnp.minimum(jnp.maximum(one, two), three))


def face_above(before, here, after, beyond):
    value = (7.0 / 12.0) * (here + after) - (1.0 / 12.0) * (before + beyond)
    return median(here, after, value)


def limited(here, face_low, face_high):
    thrice = 3.0 * here
    return (
        median(here, face_low, thrice - (face_high + face_high)),
        median(here, face_high, thrice - (face_low + face_low)),
    )


def sound_of(state):
    push = ADIABATIC * state[4]
    return push * lax.rsqrt(push * state[0])


def face_flux(left, right, normal):
    left_u, right_u = left[1 + normal], right[1 + normal]
    left_sound, right_sound = sound_of(left), sound_of(right)
    slow = jnp.minimum(jnp.minimum(left_u - left_sound, right_u - right_sound), 0.0)
    fast = jnp.maximum(jnp.maximum(left_u + left_sound, right_u + right_sound), 0.0)
    share = 1.0 / (fast - slow)
    left_part = fast * share
    right_part = -slow * share
    left_lead = left_u - slow
    right_lead = right_u - fast
    left_mass = left_part * left_lead * left[0]
    right_mass = right_part * right_lead * right[0]
    left_square = left[1] * left[1] + left[2] * left[2] + left[3] * left[3]
    right_square = right[1] * right[1] + right[2] * right[2] + right[3] * right[3]
    flux = [left_mass + right_mass]
    for k in (1, 2, 3):
        flux.append(left_mass * left[k] + right_mass * right[k])
    left_push = left_part * left[4]
    right_push = right_part * right[4]
    flux[1 + normal] = flux[1 + normal] + (left_push + right_push)
    flux.append(
        0.5 * (left_mass * left_square + right_mass * right_square)
        + left_push * (1.5 * left_lead + left_u)
        + right_push * (1.5 * right_lead + right_u)
    )
    flux.append(left_mass * left[5] + right_mass * right[5])
    return flux


def z_fluxes(planes):
    lower, upper = [], []
    for k in range(6):
        column = [planes[j][k] for j in range(9)]
        faces = [face_above(*column[j : j + 4]) for j in range(6)]
        cells = [limited(column[j + 2], faces[j], faces[j + 1]) for j in range(5)]
        lower.append([cells[j][1] for j in range(4)])
        upper.append([cells[j + 1][0] for j in range(4)])
    return [
        face_flux([lower[k][j] for k in range(6)], [upper[k][j] for k in range(6)], 2)
        for j in range(4)
    ]


def edge_primitives(fields):
    density = fields[0]
    inverse = 1.0 / density
    kinetic = 0.5 * inverse * (fields[1] ** 2 + fields[2] ** 2 + fields[3] ** 2)
    return [
        density,
        fields[1] * inverse,
        fields[2] * inverse,
        fields[3] * inverse,
        (ADIABATIC - 1.0) * (fields[4] - kinetic),
        fields[5] * inverse,
    ]


def shift_pair(main, rim, step):
    lane = lane_index(main.shape)
    main_rolled = roll(main, -step, 1)
    rim_rolled = roll(rim, -step, 1)
    inside = lane < LANES - step if step > 0 else lane >= -step
    return (
        jnp.where(inside, main_rolled, rim_rolled),
        jnp.where(inside, rim_rolled, main_rolled),
    )


def y_differences(main, rim):
    lows, highs = ([], []), ([], [])
    spread = None
    for k in range(6):
        here = (main[k], rim[k])
        before = shift_pair(*here, -1)
        after = shift_pair(*here, 1)
        beyond = shift_pair(*here, 2)
        faces = [face_above(before[j], here[j], after[j], beyond[j]) for j in range(2)]
        below = shift_pair(*faces, -1)
        cells = [limited(here[j], below[j], faces[j]) for j in range(2)]
        nexts = shift_pair(cells[0][0], cells[1][0], 1)
        for j in range(2):
            lows[j].append(cells[j][1])
            highs[j].append(nexts[j])
        if k == 2:
            spread = [0.5 * (after[j] - before[j]) for j in range(2)]
    fluxes = [face_flux(lows[j], highs[j], 1) for j in range(2)]
    differences = ([], [])
    for k in range(6):
        below = shift_pair(fluxes[0][k], fluxes[1][k], -1)
        for j in range(2):
            differences[j].append(fluxes[j][k] - below[j])
    return differences, spread


CHUNKS = (4, 12, 20)


def x_sweep(prims, low_ref, high_ref, face_ref, flux_ref):
    for row in CHUNKS:
        for k in range(6):
            before, here, after, beyond = [
                prims[k, pl.ds(row + s, 8), :] for s in (-1, 0, 1, 2)
            ]
            if row == CHUNKS[0]:
                below = face_above(prims[k, pl.ds(row - 2, 8), :], before, here, after)
            above = face_above(before, here, after, beyond)
            face_ref[k, pl.ds(row, 8), :] = above
            if row != CHUNKS[0]:
                below = face_ref[k, pl.ds(row - 1, 8), :]
            low_ref[k, pl.ds(row, 8), :], high_ref[k, pl.ds(row, 8), :] = limited(
                here, below, above
            )
    for row in CHUNKS:
        left = [high_ref[k, pl.ds(row, 8), :] for k in range(6)]
        right = [low_ref[k, pl.ds(row + 1, 8), :] for k in range(6)]
        flux = face_flux(left, right, 0)
        for k in range(6):
            flux_ref[k, pl.ds(row, 8), :] = flux[k]


def clear_ends(low_ref, flux_ref):
    for k in range(6):
        low_ref[k, pl.ds(28, 4), :] = jnp.ones((4, LANES), F32)
        flux_ref[k, pl.ds(0, 4), :] = jnp.zeros((4, LANES), F32)


def third_kernel(
    place, state, switch, edges, forcing, pair_in, odd_in, even_in, odd_y_in,
    fields, force, tend, prims, planes, low_ref, high_ref, face_ref, flux_ref, strip_ref,
):
    odd_x = place[0]
    odd_y = place[1]
    strip_ref[0] = jnp.where(odd_y == 0, even_in[...], odd_y_in[...])
    strip_ref[1] = jnp.where(odd_y == 0, odd_y_in[...], even_in[...])
    clear_ends(low_ref, flux_ref)
    lane = lane_index((EXT, LANES))
    edge_lane = lane[0:ROWS]

    def field_tiles(index, block):
        fields[0, index] = rows_around(odd_x, pair_in, odd_in, index, block)
        fields[1, index] = jnp.where(
            lane < 64,
            turned(strip_ref[0, 0:EXT], -6 * index),
            turned(strip_ref[1, 0:EXT], 122 - 6 * index),
        )

    def rim_tile(row, index):
        return jnp.where(
            edge_lane < 64,
            turned(strip_ref[0, row : row + ROWS], -3 * index),
            turned(strip_ref[1, row : row + ROWS], 125 - 3 * index),
        )

    @functools.partial(each, 6)
    def _(field):
        for plane in range(3):
            index = 3 * field + plane
            field_tiles(index, state[index])

    for plane in range(3):
        field_tiles(18 + plane, switch[plane].astype(F32))

    @functools.partial(each, 3)
    def _(part):
        for k in range(3):
            index = 3 * part + k
            force[0, index] = rows_around(
                odd_x, pair_in, odd_in, FIELDS + EDGES + index, forcing[index]
            )
            force[1, index, 0:8] = jnp.zeros((8, LANES), F32)
            force[1, index, 8:24] = rim_tile(EXT + ROWS, index)
            force[1, index, 24:32] = jnp.zeros((8, LANES), F32)

    @functools.partial(each, 6)
    def _(step):
        tile, plane = step // 3, step % 3
        values = [fields[tile, 3 * k + plane] for k in range(7)]
        density = values[0]
        inverse = 1.0 / density
        kinetic = 0.5 * inverse * (values[1] ** 2 + values[2] ** 2 + values[3] ** 2)
        heat = jnp.where(values[6] == 1.0, values[5], values[4] - kinetic)
        prims[tile, plane, 0] = density
        for k in (1, 2, 3):
            prims[tile, plane, k] = values[k] * inverse
        prims[tile, plane, 4] = (ADIABATIC - 1.0) * heat
        prims[tile, plane, 5] = values[5] * inverse

    @functools.partial(each, 6)
    def _(step):
        first = 18 * (step // 3) + step % 3
        places = [first + 3 * k for k in range(6)]
        values = edge_primitives(
            [rows_around(odd_x, pair_in, odd_in, FIELDS + k, edges[k]) for k in places]
        )
        for k in range(6):
            planes[0, step, k] = values[k]
        values = edge_primitives([rim_tile(EXT, k) for k in places])
        for k in range(6):
            planes[1, step, k, 0:8] = jnp.ones((8, LANES), F32)
            planes[1, step, k, 8:24] = values[k]
            planes[1, step, k, 24:32] = jnp.ones((8, LANES), F32)

    @functools.partial(each, 3)
    def _(plane):
        for row in CHUNKS:
            rows = pl.ds(row, 8)
            both = [[prims[tile, plane, k, rows, :] for k in range(6)] for tile in range(2)]
            differences, spread = y_differences(*both)
            for tile in range(2):
                for k in range(5):
                    tend[tile, 3 * k + plane, rows, :] = -differences[tile][k]
                tend[tile, 15 + plane, rows, :] = (
                    -differences[tile][5] - both[tile][4] * spread[tile]
                )

    @functools.partial(each, 6)
    def _(step):
        tile, plane = step // 3, step % 3
        x_sweep(prims.at[tile, plane], low_ref, high_ref, face_ref, flux_ref)
        for row in CHUNKS:
            rows = pl.ds(row, 8)
            for k in range(6):
                difference = flux_ref[k, rows, :] - flux_ref[k, pl.ds(row - 1, 8), :]
                if k == 5:
                    before = prims[tile, plane, 1, pl.ds(row - 1, 8), :]
                    after = prims[tile, plane, 1, pl.ds(row + 1, 8), :]
                    spread = 0.5 * (after - before)
                    difference = difference + prims[tile, plane, 4, rows, :] * spread
                tend[tile, 3 * k + plane, rows, :] -= difference

    @functools.partial(each, 2)
    def _(tile):
        for row in CHUNKS:
            rows = pl.ds(row, 8)
            column = (
                [[planes[tile, p, k, rows, :] for k in range(6)] for p in range(3)]
                + [[prims[tile, p, k, rows, :] for k in range(6)] for p in range(3)]
                + [[planes[tile, 3 + p, k, rows, :] for k in range(6)] for p in range(3)]
            )
            flux = z_fluxes(column)
            for plane in range(3):
                for k in range(6):
                    difference = flux[plane + 1][k] - flux[plane][k]
                    if k == 5:
                        spread = 0.5 * (column[plane + 4][3] - column[plane + 2][3])
                        difference = difference + column[plane + 3][4] * spread
                    tend[tile, 3 * k + plane, rows, :] -= difference


def fourth_kernel(
    cells, totals, fields, force, tend, edges, out,
    updated, section, prims, low_ref, high_ref, face_ref, flux_ref, sent,
):
    peak = jnp.max(totals[:, 0, :], axis=0, keepdims=True)
    power = jnp.sum(totals[:, 1, :], axis=0, keepdims=True)
    time_step = CFL_NUMBER / peak
    scale = jnp.sqrt(INJECTION / (0.5 * time_step * (power / cells + 1e-06)))
    clear_ends(low_ref, flux_ref)

    def forced(values, drive, tendency):
        result = list(tendency)
        for k in (1, 2, 3):
            result[k] = result[k] + scale * values[0] * drive[k - 1]
        result[4] = result[4] + scale * (
            values[1] * drive[0] + values[2] * drive[1] + values[3] * drive[2]
        )
        return result

    def settle(values, switch, inverse):
        kinetic = 0.5 * inverse * (values[1] ** 2 + values[2] ** 2 + values[3] ** 2)
        values[5] = jnp.where(switch == 0.0, values[4] - kinetic, values[5])

    @functools.partial(each, 6)
    def _(step):
        tile, plane = step // 3, step % 3
        for row in CHUNKS:
            rows = pl.ds(row, 8)
            values = [fields[tile, 3 * k + plane, rows, :] for k in range(7)]
            drive = [force[tile, 3 * k + plane, rows, :] for k in range(3)]
            rate = forced(values, drive, [tend[tile, 3 * k + plane, rows, :] for k in range(6)])
            stage = [values[k] + time_step * rate[k] for k in range(6)]
            inverse = 1.0 / stage[0]
            settle(stage, values[6], inverse)
            for k in range(6):
                section[tile, plane, k, rows, :] = stage[k]
            prims[tile, plane, 0, rows, :] = stage[0]
            for k in (1, 2, 3):
                prims[tile, plane, k, rows, :] = stage[k] * inverse
            prims[tile, plane, 4, rows, :] = (ADIABATIC - 1.0) * stage[5]
            prims[tile, plane, 5, rows, :] = stage[5] * inverse

    @functools.partial(each, 2)
    def _(step):
        inner = pl.ds(pl.multiple_of(8 * step, 8), 8)
        rows = pl.ds(pl.multiple_of(8 * step + 8, 8), 8)
        outer = [
            edge_primitives([edges[18 * side + 3 * k + plane, inner, :] for k in range(6)])
            for side in range(2)
            for plane in range(3)
        ]
        column = (
            outer[0:3] + [[prims[0, p, k, rows, :] for k in range(6)] for p in range(3)] + outer[3:6]
        )
        flux = z_fluxes(column)
        for plane in range(3):
            for k in range(6):
                difference = flux[plane + 1][k] - flux[plane][k]
                if k == 5:
                    spread = 0.5 * (column[plane + 4][3] - column[plane + 2][3])
                    difference = difference + column[plane + 3][4] * spread
                updated[k, plane, inner, :] = -difference

    @functools.partial(each, 3)
    def _(plane):
        x_sweep(prims.at[0, plane], low_ref, high_ref, face_ref, flux_ref)
        for row in (8, 16):
            rows = pl.ds(row, 8)
            inner = pl.ds(row - 8, 8)
            both = [[prims[tile, plane, k, rows, :] for k in range(6)] for tile in range(2)]
            differences, spread = y_differences(*both)
            before = prims[0, plane, 1, pl.ds(row - 1, 8), :]
            after = prims[0, plane, 1, pl.ds(row + 1, 8), :]
            spread = spread[0] + 0.5 * (after - before)
            rate = []
            for k in range(6):
                across = flux_ref[k, rows, :] - flux_ref[k, pl.ds(row - 1, 8), :]
                rate.append(updated[k, plane, inner, :] - differences[0][k] - across)
            rate[5] = rate[5] - both[0][4] * spread
            stage = [section[0, plane, k, rows, :] for k in range(6)]
            drive = [force[0, 3 * k + plane, rows, :] for k in range(3)]
            rate = forced(stage, drive, rate)
            values = [fields[0, 3 * k + plane, rows, :] for k in range(7)]
            result = [
                0.5 * values[k] + 0.5 * (stage[k] + time_step * rate[k]) for k in range(6)
            ]
            settle(result, values[6], 1.0 / result[0])
            for k in range(6):
                updated[k, plane, inner, :] = result[k]
        pltpu.make_async_copy(updated.at[:, plane], out.at[:, plane], sent.at[plane]).start()

    for plane in range(3):
        pltpu.make_async_copy(updated.at[:, plane], out.at[:, plane], sent.at[plane]).wait()


def shape(*sizes):
    return jax.ShapeDtypeStruct(sizes, F32)


def vmem_specs(count):
    return [pl.BlockSpec(memory_space=pltpu.VMEM)] * count


def call(kernel, name, outs, scalars, arrays, scratch=(), cost=0, out_space=pltpu.VMEM):
    single = not isinstance(outs, tuple)
    out_spec = pl.BlockSpec(memory_space=out_space)
    return pl.pallas_call(
        kernel,
        out_shape=outs,
        in_specs=[pl.BlockSpec(memory_space=pltpu.SMEM)] * len(scalars) + vmem_specs(len(arrays)),
        out_specs=out_spec if single else (out_spec,) * len(outs),
        scratch_shapes=list(scratch),
        compiler_params=pltpu.CompilerParams(vmem_limit_bytes=VMEM_LIMIT),
        cost_estimate=pl.CostEstimate(flops=cost, bytes_accessed=cost, transcendentals=0),
        name=name,
    )(*scalars, *arrays)


def pairs(count, begin):
    table = []
    for first in range(begin, begin + count, 2):
        low, high = first % count, (first + 1) % count
        table += [(low, high), (high, low)]
    return table


def exchanged(rows, after, axes):
    count = lax.axis_size(axes)
    spread = pl.pallas_call(
        spread_kernel,
        out_shape=shape(count, 2, LANES),
        in_specs=[*vmem_specs(1), pl.BlockSpec(memory_space=pl.ANY)],
        out_specs=vmem_specs(1)[0],
        compiler_params=pltpu.CompilerParams(vmem_limit_bytes=VMEM_LIMIT),
        name="spread",
    )(rows, after)
    return lax.all_to_all(spread, axes, 0, 0, tiled=True)


GX = ("zl", "core")
GY = ("y", "zh", "x")


def local(fluid_state, switch, z_edges, forcing):
    count_x = lax.axis_size(GX)
    count_y = lax.axis_size(GY)
    cells = 3.0 * ROWS * LANES * count_x * count_y
    place = jnp.stack([lax.axis_index(GX) % 2, lax.axis_index(GY) % 2]).astype(jnp.int32)
    tile = (8, LANES)
    block = (ROWS, LANES)
    inputs = (
        fluid_state.reshape(18, *block),
        switch,
        z_edges.reshape(EDGES, *block),
        forcing.reshape(FORCES, *block),
    )
    pair_out, odd_out, *arrays = pl.pallas_call(
        first_kernel,
        out_shape=(
            shape(X_TILES + 1, *tile),
            shape(X_TILES, *tile),
            *(jax.ShapeDtypeStruct(values.shape, values.dtype) for values in inputs),
        ),
        in_specs=[
            pl.BlockSpec(memory_space=pltpu.SMEM),
            *([pl.BlockSpec(memory_space=pltpu.HBM)] * 4),
        ],
        out_specs=tuple(vmem_specs(6)),
        scratch_shapes=[pltpu.SemaphoreType.DMA((4,))],
        compiler_params=pltpu.CompilerParams(vmem_limit_bytes=VMEM_LIMIT),
        name="first",
    )(place, *(pltpu.with_memory_space_constraint(values, pltpu.HBM) for values in inputs))
    pair_in = lax.all_gather(pair_out, "core")
    odd_out, pair_in = lax.optimization_barrier((odd_out, pair_in))
    odd_in = lax.ppermute(odd_out, GX, pairs(count_x, 1))
    totals = exchanged(pair_in[:, X_TILES, 0:2], place, ("y", "x"))
    strips = call(
        second_kernel,
        "second",
        (shape(EXT + 2 * ROWS, LANES), shape(EXT + 2 * ROWS, LANES)),
        (place,),
        (*arrays, pair_in, odd_in),
        cost=4_000_000,
    )
    even_in = lax.ppermute(strips[0], GY, pairs(count_y, 0))
    odd_y_in = lax.ppermute(strips[1], GY, pairs(count_y, 1))
    totals = exchanged(totals, even_in, ("zh", "zl"))
    extended = (EXT, LANES)
    work = [pltpu.VMEM((6, *extended), F32) for _ in range(4)]
    fields, force, tend = call(
        third_kernel,
        "third",
        (shape(2, FIELDS, *extended), shape(2, FORCES, *extended), shape(2, 18, *extended)),
        (place,),
        (*arrays, pair_in, odd_in, even_in, odd_y_in),
        [
            pltpu.VMEM((2, 3, 6, *extended), F32),
            pltpu.VMEM((2, 6, 6, *extended), F32),
            *work,
            pltpu.VMEM((2, EXT + 2 * ROWS, LANES), F32),
        ],
        cost=60_000_000,
    )
    return call(
        functools.partial(fourth_kernel, cells),
        "fourth",
        shape(6, 3, ROWS, LANES),
        (),
        (totals, fields, force, tend, arrays[2]),
        [
            pltpu.VMEM((6, 3, ROWS, LANES), F32),
            pltpu.VMEM((2, 3, 6, *extended), F32),
            pltpu.VMEM((2, 3, 6, *extended), F32),
            *work,
            pltpu.SemaphoreType.DMA((3,)),
        ],
        cost=8_000_000,
        out_space=pltpu.HBM,
    )


def solution(mesh):
    count_x, count_y = mesh.devices.shape
    count_z = 2 if count_y % 8 == 0 else 1
    parts = (count_x // 2, 2, count_y // (4 * count_z), count_z, 4)
    split = Mesh(mesh.devices.reshape(parts), (*GX, *GY))
    return jax.shard_map(
        local,
        mesh=split,
        in_specs=(
            P(None, None, GX, GY),
            P(None, GX, GY),
            P(None, None, None, GX, GY),
            P(None, None, GX, GY),
        ),
        out_specs=P(None, None, GX, GY),
        check_vma=False,
    )
```

```python
import functools

import jax
import jax.numpy as jnp
from jax import lax
from jax.experimental import pallas as pl
from jax.experimental.pallas import tpu as pltpu
from jax.sharding import Mesh
from jax.sharding import PartitionSpec as P

ADIABATIC = 5.0 / 3.0
CFL_NUMBER = 0.4
INJECTION = 0.04
LANES = 128
ROWS = 16
EXT = 32
FIELDS = 21
EDGES = 36
FORCES = 9
X_TILES = FIELDS + EDGES + FORCES
VMEM_LIMIT = 16 * 1024 * 1024
F32 = jnp.float32


def lane_index(shape):
    return lax.broadcasted_iota(jnp.int32, shape, len(shape) - 1)


def roll(values, shift, axis):
    size = values.shape[axis]
    shift = shift % size
    return values if shift == 0 else pltpu.roll(values, shift, axis)


def parities():
    return lax.axis_index("core"), lax.rem(lax.axis_index("x"), 2)


def each(count, body):
    def step(index, carry):
        body(index)
        return carry

    lax.fori_loop(0, count, step, 0)


def x_place(refs, index):
    state, switch, edges, forcing = refs
    if index < 18:
        return lambda rows: state[index, rows, :]
    index -= 18
    if index < 3:
        return lambda rows: switch[index, rows, :].astype(F32)
    index -= 3
    if index < EDGES:
        return lambda rows: edges[index, rows, :]
    index -= EDGES
    return lambda rows: forcing[index, rows, :]


def first_kernel(
    state_in, switch_in, edges_in, forcing_in,
    pair_out, odd_out, state, switch, edges, forcing, arrived,
):
    refs = (state, switch, edges, forcing)
    copies = [
        pltpu.make_async_copy(source, target, arrived.at[k])
        for k, (source, target) in enumerate(
            zip((state_in, switch_in, edges_in, forcing_in), refs, strict=True)
        )
    ]
    for copy in copies:
        copy.start()
    odd, _ = parities()
    near = pl.multiple_of(8 * (1 - odd), 8)
    far = pl.multiple_of(8 * odd, 8)
    for k in (0, 1, 3):
        copies[k].wait()
    peak = None
    total = None
    for plane in range(3):
        fields = [state[3 * k + plane] for k in range(6)]
        density = fields[0]
        inverse = 1.0 / density
        kinetic = 0.5 * inverse * (fields[1] ** 2 + fields[2] ** 2 + fields[3] ** 2)
        heat = jnp.where(switch[plane] == 1, fields[5], fields[4] - kinetic)
        sound = jnp.sqrt(ADIABATIC * (ADIABATIC - 1.0) * heat * inverse)
        speed = (
            jnp.abs(fields[1]) + jnp.abs(fields[2]) + jnp.abs(fields[3])
        ) * inverse + 3.0 * sound
        drive = [forcing[3 * k + plane] for k in range(3)]
        power = density * (drive[0] ** 2 + drive[1] ** 2 + drive[2] ** 2)
        peak = speed if peak is None else jnp.maximum(peak, speed)
        total = power if total is None else total + power
    row = lax.broadcasted_iota(jnp.int32, (8, LANES), 0)
    pair_out[X_TILES] = jnp.where(row == 0, jnp.max(peak), jnp.sum(total))
    copies[2].wait()
    for index in range(X_TILES):
        tile = x_place(refs, index)
        pair_out[index] = tile(pl.ds(near, 8))
        odd_out[index] = tile(pl.ds(far, 8))


def spread_kernel(rows, after, out):
    peak = jnp.max(rows[:, 0, :], axis=0, keepdims=True)
    total = jnp.sum(rows[:, 1, :], axis=0, keepdims=True)
    joined = jnp.concatenate([peak, total], axis=0)
    out[...] = jnp.broadcast_to(joined[None], out.shape)


def rows_around(odd_x, pair_in, odd_in, index, block):
    from_pair = pair_in[1 - odd_x, index]
    from_odd = odd_in[index]
    below = jnp.where(odd_x == 0, from_odd, from_pair)
    above = jnp.where(odd_x == 0, from_pair, from_odd)
    return jnp.concatenate([below, block, above], axis=0)


def turned(values, shift):
    return pltpu.roll(values, lax.rem(shift + LANES, LANES), 1)


def second_kernel(state, switch, edges, forcing, pair_in, odd_in, even_out, odd_out):
    odd_x, odd_y = parities()
    lane = lane_index((EXT, LANES))
    high = jnp.zeros((EXT, LANES), F32)
    low = jnp.zeros((EXT, LANES), F32)
    for index in range(FIELDS):
        block = x_place((state, switch, edges, forcing), index)(slice(0, ROWS))
        column = rows_around(odd_x, pair_in, odd_in, index, block)
        mine = (lane >= 6 * index) & (lane < 6 * index + 6)
        high = jnp.where(mine, roll(column, 6 * index - 122, 1), high)
        low = jnp.where(mine, roll(column, 6 * index, 1), low)
    even_out[0:EXT] = jnp.where(odd_y == 0, high, low)
    odd_out[0:EXT] = jnp.where(odd_y == 0, low, high)
    lane = lane[0:ROWS]
    for source, count, row in ((edges, EDGES, EXT), (forcing, FORCES, EXT + ROWS)):
        high = jnp.zeros((ROWS, LANES), F32)
        low = jnp.zeros((ROWS, LANES), F32)
        for index in range(count):
            mine = (lane >= 3 * index) & (lane < 3 * index + 3)
            high = jnp.where(mine, roll(source[index], 3 * index - 125, 1), high)
            low = jnp.where(mine, roll(source[index], 3 * index, 1), low)
        even_out[row : row + ROWS] = jnp.where(odd_y == 0, high, low)
        odd_out[row : row + ROWS] = jnp.where(odd_y == 0, low, high)


def median(one, two, three):
    return jnp.maximum(jnp.minimum(one, two), jnp.minimum(jnp.maximum(one, two), three))


def face_above(before, here, after, beyond):
    value = (7.0 / 12.0) * (here + after) - (1.0 / 12.0) * (before + beyond)
    return median(here, after, value)


def limited(here, face_low, face_high):
    thrice = 3.0 * here
    return (
        median(here, face_low, thrice - (face_high + face_high)),
        median(here, face_high, thrice - (face_low + face_low)),
    )


def sound_of(state):
    push = ADIABATIC * state[4]
    return push * lax.rsqrt(push * state[0])


def face_flux(left, right, normal):
    left_u, right_u = left[1 + normal], right[1 + normal]
    left_sound, right_sound = sound_of(left), sound_of(right)
    slow = jnp.minimum(jnp.minimum(left_u - left_sound, right_u - right_sound), 0.0)
    fast = jnp.maximum(jnp.maximum(left_u + left_sound, right_u + right_sound), 0.0)
    share = 1.0 / (fast - slow)
    left_part = fast * share
    right_part = -slow * share
    left_lead = left_u - slow
    right_lead = right_u - fast
    left_mass = left_part * left_lead * left[0]
    right_mass = right_part * right_lead * right[0]
    left_square = left[1] * left[1] + left[2] * left[2] + left[3] * left[3]
    right_square = right[1] * right[1] + right[2] * right[2] + right[3] * right[3]
    flux = [left_mass + right_mass]
    for k in (1, 2, 3):
        flux.append(left_mass * left[k] + right_mass * right[k])
    left_push = left_part * left[4]
    right_push = right_part * right[4]
    flux[1 + normal] = flux[1 + normal] + (left_push + right_push)
    flux.append(
        0.5 * (left_mass * left_square + right_mass * right_square)
        + left_push * (1.5 * left_lead + left_u)
        + right_push * (1.5 * right_lead + right_u)
    )
    flux.append(left_mass * left[5] + right_mass * right[5])
    return flux


def z_fluxes(planes):
    lower, upper = [], []
    for k in range(6):
        column = [planes[j][k] for j in range(9)]
        faces = [face_above(*column[j : j + 4]) for j in range(6)]
        cells = [limited(column[j + 2], faces[j], faces[j + 1]) for j in range(5)]
        lower.append([cells[j][1] for j in range(4)])
        upper.append([cells[j + 1][0] for j in range(4)])
    return [
        face_flux([lower[k][j] for k in range(6)], [upper[k][j] for k in range(6)], 2)
        for j in range(4)
    ]


def edge_primitives(fields):
    density = fields[0]
    inverse = 1.0 / density
    kinetic = 0.5 * inverse * (fields[1] ** 2 + fields[2] ** 2 + fields[3] ** 2)
    return [
        density,
        fields[1] * inverse,
        fields[2] * inverse,
        fields[3] * inverse,
        (ADIABATIC - 1.0) * (fields[4] - kinetic),
        fields[5] * inverse,
    ]


def shift_pair(main, rim, step):
    lane = lane_index(main.shape)
    main_rolled = roll(main, -step, 1)
    rim_rolled = roll(rim, -step, 1)
    inside = lane < LANES - step if step > 0 else lane >= -step
    return (
        jnp.where(inside, main_rolled, rim_rolled),
        jnp.where(inside, rim_rolled, main_rolled),
    )


def y_differences(main, rim):
    lows, highs = ([], []), ([], [])
    spread = None
    for k in range(6):
        here = (main[k], rim[k])
        before = shift_pair(*here, -1)
        after = shift_pair(*here, 1)
        beyond = shift_pair(*here, 2)
        faces = [face_above(before[j], here[j], after[j], beyond[j]) for j in range(2)]
        below = shift_pair(*faces, -1)
        cells = [limited(here[j], below[j], faces[j]) for j in range(2)]
        nexts = shift_pair(cells[0][0], cells[1][0], 1)
        for j in range(2):
            lows[j].append(cells[j][1])
            highs[j].append(nexts[j])
        if k == 2:
            spread = [0.5 * (after[j] - before[j]) for j in range(2)]
    fluxes = [face_flux(lows[j], highs[j], 1) for j in range(2)]
    differences = ([], [])
    for k in range(6):
        below = shift_pair(fluxes[0][k], fluxes[1][k], -1)
        for j in range(2):
            differences[j].append(fluxes[j][k] - below[j])
    return differences, spread


CHUNKS = (4, 12, 20)


def x_sweep(prims, low_ref, high_ref, face_ref, flux_ref):
    for row in CHUNKS:
        for k in range(6):
            before, here, after, beyond = [
                prims[k, pl.ds(row + s, 8), :] for s in (-1, 0, 1, 2)
            ]
            if row == CHUNKS[0]:
                below = face_above(prims[k, pl.ds(row - 2, 8), :], before, here, after)
            above = face_above(before, here, after, beyond)
            face_ref[k, pl.ds(row, 8), :] = above
            if row != CHUNKS[0]:
                below = face_ref[k, pl.ds(row - 1, 8), :]
            low_ref[k, pl.ds(row, 8), :], high_ref[k, pl.ds(row, 8), :] = limited(
                here, below, above
            )
    for row in CHUNKS:
        left = [high_ref[k, pl.ds(row, 8), :] for k in range(6)]
        right = [low_ref[k, pl.ds(row + 1, 8), :] for k in range(6)]
        flux = face_flux(left, right, 0)
        for k in range(6):
            flux_ref[k, pl.ds(row, 8), :] = flux[k]


def clear_ends(low_ref, flux_ref):
    for k in range(6):
        low_ref[k, pl.ds(28, 4), :] = jnp.ones((4, LANES), F32)
        flux_ref[k, pl.ds(0, 4), :] = jnp.zeros((4, LANES), F32)


def third_kernel(
    state, switch, edges, forcing, pair_in, odd_in, even_in, odd_y_in,
    fields, force, tend, outer, prims, planes, low_ref, high_ref, face_ref, flux_ref, strip_ref,
):
    odd_x, odd_y = parities()
    strip_ref[0] = jnp.where(odd_y == 0, even_in[...], odd_y_in[...])
    strip_ref[1] = jnp.where(odd_y == 0, odd_y_in[...], even_in[...])
    clear_ends(low_ref, flux_ref)
    lane = lane_index((EXT, LANES))
    edge_lane = lane[0:ROWS]

    def field_tiles(index, block):
        fields[0, index] = rows_around(odd_x, pair_in, odd_in, index, block)
        fields[1, index] = jnp.where(
            lane < 64,
            turned(strip_ref[0, 0:EXT], -6 * index),
            turned(strip_ref[1, 0:EXT], 122 - 6 * index),
        )

    def rim_tile(row, index):
        return jnp.where(
            edge_lane < 64,
            turned(strip_ref[0, row : row + ROWS], -3 * index),
            turned(strip_ref[1, row : row + ROWS], 125 - 3 * index),
        )

    @functools.partial(each, 6)
    def _(field):
        for plane in range(3):
            index = 3 * field + plane
            field_tiles(index, state[index])

    for plane in range(3):
        field_tiles(18 + plane, switch[plane].astype(F32))

    @functools.partial(each, 3)
    def _(part):
        for k in range(3):
            index = 3 * part + k
            force[0, index] = rows_around(
                odd_x, pair_in, odd_in, FIELDS + EDGES + index, forcing[index]
            )
            force[1, index, 0:8] = jnp.zeros((8, LANES), F32)
            force[1, index, 8:24] = rim_tile(EXT + ROWS, index)
            force[1, index, 24:32] = jnp.zeros((8, LANES), F32)

    @functools.partial(each, 6)
    def _(step):
        tile, plane = step // 3, step % 3
        values = [fields[tile, 3 * k + plane] for k in range(7)]
        density = values[0]
        inverse = 1.0 / density
        kinetic = 0.5 * inverse * (values[1] ** 2 + values[2] ** 2 + values[3] ** 2)
        heat = jnp.where(values[6] == 1.0, values[5], values[4] - kinetic)
        prims[tile, plane, 0] = density
        for k in (1, 2, 3):
            prims[tile, plane, k] = values[k] * inverse
        prims[tile, plane, 4] = (ADIABATIC - 1.0) * heat
        prims[tile, plane, 5] = values[5] * inverse

    @functools.partial(each, 6)
    def _(step):
        first = 18 * (step // 3) + step % 3
        places = [first + 3 * k for k in range(6)]
        values = edge_primitives(
            [rows_around(odd_x, pair_in, odd_in, FIELDS + k, edges[k]) for k in places]
        )
        for k in range(6):
            planes[0, step, k] = values[k]
            outer[step, k] = values[k][8:24]
        values = edge_primitives([rim_tile(EXT, k) for k in places])
        for k in range(6):
            planes[1, step, k, 0:8] = jnp.ones((8, LANES), F32)
            planes[1, step, k, 8:24] = values[k]
            planes[1, step, k, 24:32] = jnp.ones((8, LANES), F32)

    @functools.partial(each, 3)
    def _(plane):
        for row in CHUNKS:
            rows = pl.ds(row, 8)
            both = [[prims[tile, plane, k, rows, :] for k in range(6)] for tile in range(2)]
            differences, spread = y_differences(*both)
            for tile in range(2):
                for k in range(5):
                    tend[tile, 3 * k + plane, rows, :] = -differences[tile][k]
                tend[tile, 15 + plane, rows, :] = (
                    -differences[tile][5] - both[tile][4] * spread[tile]
                )

    @functools.partial(each, 6)
    def _(step):
        tile, plane = step // 3, step % 3
        x_sweep(prims.at[tile, plane], low_ref, high_ref, face_ref, flux_ref)
        for row in CHUNKS:
            rows = pl.ds(row, 8)
            for k in range(6):
                difference = flux_ref[k, rows, :] - flux_ref[k, pl.ds(row - 1, 8), :]
                if k == 5:
                    before = prims[tile, plane, 1, pl.ds(row - 1, 8), :]
                    after = prims[tile, plane, 1, pl.ds(row + 1, 8), :]
                    spread = 0.5 * (after - before)
                    difference = difference + prims[tile, plane, 4, rows, :] * spread
                tend[tile, 3 * k + plane, rows, :] -= difference

    @functools.partial(each, 2)
    def _(tile):
        for row in CHUNKS:
            rows = pl.ds(row, 8)
            column = (
                [[planes[tile, p, k, rows, :] for k in range(6)] for p in range(3)]
                + [[prims[tile, p, k, rows, :] for k in range(6)] for p in range(3)]
                + [[planes[tile, 3 + p, k, rows, :] for k in range(6)] for p in range(3)]
            )
            flux = z_fluxes(column)
            for plane in range(3):
                for k in range(6):
                    difference = flux[plane + 1][k] - flux[plane][k]
                    if k == 5:
                        spread = 0.5 * (column[plane + 4][3] - column[plane + 2][3])
                        difference = difference + column[plane + 3][4] * spread
                    tend[tile, 3 * k + plane, rows, :] -= difference


def fourth_kernel(
    cells, totals, fields, force, tend, outer_prims, out,
    updated, section, prims, low_ref, high_ref, face_ref, flux_ref, sent,
):
    peak = jnp.max(totals[:, 0, :], axis=0, keepdims=True)
    power = jnp.sum(totals[:, 1, :], axis=0, keepdims=True)
    time_step = CFL_NUMBER / peak
    scale = jnp.sqrt(INJECTION / (0.5 * time_step * (power / cells + 1e-06)))
    clear_ends(low_ref, flux_ref)

    def forced(values, drive, tendency):
        result = list(tendency)
        for k in (1, 2, 3):
            result[k] = result[k] + scale * values[0] * drive[k - 1]
        result[4] = result[4] + scale * (
            values[1] * drive[0] + values[2] * drive[1] + values[3] * drive[2]
        )
        return result

    def settle(values, switch, inverse):
        kinetic = 0.5 * inverse * (values[1] ** 2 + values[2] ** 2 + values[3] ** 2)
        values[5] = jnp.where(switch == 0.0, values[4] - kinetic, values[5])

    @functools.partial(each, 6)
    def _(step):
        tile, plane = step // 3, step % 3
        for row in CHUNKS:
            rows = pl.ds(row, 8)
            values = [fields[tile, 3 * k + plane, rows, :] for k in range(7)]
            drive = [force[tile, 3 * k + plane, rows, :] for k in range(3)]
            rate = forced(values, drive, [tend[tile, 3 * k + plane, rows, :] for k in range(6)])
            stage = [values[k] + time_step * rate[k] for k in range(6)]
            inverse = 1.0 / stage[0]
            settle(stage, values[6], inverse)
            for k in range(6):
                section[tile, plane, k, rows, :] = stage[k]
            prims[tile, plane, 0, rows, :] = stage[0]
            for k in (1, 2, 3):
                prims[tile, plane, k, rows, :] = stage[k] * inverse
            prims[tile, plane, 4, rows, :] = (ADIABATIC - 1.0) * stage[5]
            prims[tile, plane, 5, rows, :] = stage[5] * inverse

    @functools.partial(each, 2)
    def _(step):
        inner = pl.ds(pl.multiple_of(8 * step, 8), 8)
        rows = pl.ds(pl.multiple_of(8 * step + 8, 8), 8)
        outer = [[outer_prims[p, k, inner, :] for k in range(6)] for p in range(6)]
        column = (
            outer[0:3] + [[prims[0, p, k, rows, :] for k in range(6)] for p in range(3)] + outer[3:6]
        )
        flux = z_fluxes(column)
        for plane in range(3):
            for k in range(6):
                difference = flux[plane + 1][k] - flux[plane][k]
                if k == 5:
                    spread = 0.5 * (column[plane + 4][3] - column[plane + 2][3])
                    difference = difference + column[plane + 3][4] * spread
                updated[k, plane, inner, :] = -difference

    @functools.partial(each, 3)
    def _(plane):
        x_sweep(prims.at[0, plane], low_ref, high_ref, face_ref, flux_ref)
        for row in (8, 16):
            rows = pl.ds(row, 8)
            inner = pl.ds(row - 8, 8)
            both = [[prims[tile, plane, k, rows, :] for k in range(6)] for tile in range(2)]
            differences, spread = y_differences(*both)
            before = prims[0, plane, 1, pl.ds(row - 1, 8), :]
            after = prims[0, plane, 1, pl.ds(row + 1, 8), :]
            spread = spread[0] + 0.5 * (after - before)
            rate = []
            for k in range(6):
                across = flux_ref[k, rows, :] - flux_ref[k, pl.ds(row - 1, 8), :]
                rate.append(updated[k, plane, inner, :] - differences[0][k] - across)
            rate[5] = rate[5] - both[0][4] * spread
            stage = [section[0, plane, k, rows, :] for k in range(6)]
            drive = [force[0, 3 * k + plane, rows, :] for k in range(3)]
            rate = forced(stage, drive, rate)
            values = [fields[0, 3 * k + plane, rows, :] for k in range(7)]
            result = [
                0.5 * values[k] + 0.5 * (stage[k] + time_step * rate[k]) for k in range(6)
            ]
            settle(result, values[6], 1.0 / result[0])
            for k in range(6):
                updated[k, plane, inner, :] = result[k]
        pltpu.make_async_copy(updated.at[:, plane], out.at[:, plane], sent.at[plane]).start()

    for plane in range(3):
        pltpu.make_async_copy(updated.at[:, plane], out.at[:, plane], sent.at[plane]).wait()


def shape(*sizes):
    return jax.ShapeDtypeStruct(sizes, F32)


def vmem_specs(count):
    return [pl.BlockSpec(memory_space=pltpu.VMEM)] * count


def call(kernel, name, outs, arrays, scratch=(), cost=0, out_space=pltpu.VMEM):
    single = not isinstance(outs, tuple)
    out_spec = pl.BlockSpec(memory_space=out_space)
    return pl.pallas_call(
        kernel,
        out_shape=outs,
        in_specs=vmem_specs(len(arrays)),
        out_specs=out_spec if single else (out_spec,) * len(outs),
        scratch_shapes=list(scratch),
        compiler_params=pltpu.CompilerParams(vmem_limit_bytes=VMEM_LIMIT),
        cost_estimate=pl.CostEstimate(flops=cost, bytes_accessed=cost, transcendentals=0),
        name=name,
    )(*arrays)


def pairs(count, begin):
    table = []
    for first in range(begin, begin + count, 2):
        low, high = first % count, (first + 1) % count
        table += [(low, high), (high, low)]
    return table


def spread_over(rows, after, axes):
    return pl.pallas_call(
        spread_kernel,
        out_shape=shape(lax.axis_size(axes), 2, LANES),
        in_specs=[*vmem_specs(1), pl.BlockSpec(memory_space=pl.ANY)],
        out_specs=vmem_specs(1)[0],
        compiler_params=pltpu.CompilerParams(vmem_limit_bytes=VMEM_LIMIT),
        name="spread",
    )(rows, after)


def exchanged(spread, axes):
    return lax.all_to_all(spread, axes, 0, 0, tiled=True)


GX = ("zl", "core")
GY = ("y", "zh", "x")


def local(fluid_state, switch, z_edges, forcing):
    count_x = lax.axis_size(GX)
    count_y = lax.axis_size(GY)
    cells = 3.0 * ROWS * LANES * count_x * count_y
    tile = (8, LANES)
    block = (ROWS, LANES)
    inputs = (
        fluid_state.reshape(18, *block),
        switch,
        z_edges.reshape(EDGES, *block),
        forcing.reshape(FORCES, *block),
    )
    pair_out, odd_out, *arrays = pl.pallas_call(
        first_kernel,
        out_shape=(
            shape(X_TILES + 1, *tile),
            shape(X_TILES, *tile),
            *(jax.ShapeDtypeStruct(values.shape, values.dtype) for values in inputs),
        ),
        in_specs=[
            *([pl.BlockSpec(memory_space=pltpu.HBM)] * 4),
        ],
        out_specs=tuple(vmem_specs(6)),
        scratch_shapes=[pltpu.SemaphoreType.DMA((4,))],
        compiler_params=pltpu.CompilerParams(vmem_limit_bytes=VMEM_LIMIT),
        name="first",
    )(*(pltpu.with_memory_space_constraint(values, pltpu.HBM) for values in inputs))
    pair_in = lax.all_gather(pair_out, "core")
    odd_out, pair_in = lax.optimization_barrier((odd_out, pair_in))
    odd_in = lax.ppermute(odd_out, GX, pairs(count_x, 1))
    rows = pair_in[:, X_TILES, 0:2]
    spread = spread_over(rows, rows, ("y", "x"))
    totals = exchanged(spread, ("y", "x"))
    strips = call(
        second_kernel,
        "second",
        (shape(EXT + 2 * ROWS, LANES), shape(EXT + 2 * ROWS, LANES)),
        (*arrays, pair_in, odd_in),
        cost=4_000_000,
    )
    even_in = lax.ppermute(strips[0], GY, pairs(count_y, 0))
    odd_y_in = lax.ppermute(strips[1], GY, pairs(count_y, 1))
    totals = exchanged(spread_over(totals, even_in, ("zh", "zl")), ("zh", "zl"))
    extended = (EXT, LANES)
    work = [pltpu.VMEM((6, *extended), F32) for _ in range(4)]
    fields, force, tend, outer = call(
        third_kernel,
        "third",
        (
            shape(2, FIELDS, *extended),
            shape(2, FORCES, *extended),
            shape(2, 18, *extended),
            shape(6, 6, ROWS, LANES),
        ),
        (*arrays, pair_in, odd_in, even_in, odd_y_in),
        [
            pltpu.VMEM((2, 3, 6, *extended), F32),
            pltpu.VMEM((2, 6, 6, *extended), F32),
            *work,
            pltpu.VMEM((2, EXT + 2 * ROWS, LANES), F32),
        ],
        cost=60_000_000,
    )
    return call(
        functools.partial(fourth_kernel, cells),
        "fourth",
        shape(6, 3, ROWS, LANES),
        (totals, fields, force, tend, outer),
        [
            pltpu.VMEM((6, 3, ROWS, LANES), F32),
            pltpu.VMEM((2, 3, 6, *extended), F32),
            pltpu.VMEM((2, 3, 6, *extended), F32),
            *work,
            pltpu.SemaphoreType.DMA((3,)),
        ],
        cost=8_000_000,
        out_space=pltpu.HBM,
    )


def solution(mesh):
    count_x, count_y = mesh.devices.shape
    count_z = 2 if count_y % 8 == 0 else 1
    parts = (count_x // 2, 2, count_y // (4 * count_z), count_z, 4)
    split = Mesh(mesh.devices.reshape(parts), (*GX, *GY))
    return jax.shard_map(
        local,
        mesh=split,
        in_specs=(
            P(None, None, GX, GY),
            P(None, GX, GY),
            P(None, None, None, GX, GY),
            P(None, None, GX, GY),
        ),
        out_specs=P(None, None, GX, GY),
        check_vma=False,
    )
```

```python
import functools

import jax
import jax.numpy as jnp
from jax import lax
from jax.experimental import pallas as pl
from jax.experimental.pallas import tpu as pltpu
from jax.sharding import Mesh
from jax.sharding import PartitionSpec as P

ADIABATIC = 5.0 / 3.0
CFL_NUMBER = 0.4
INJECTION = 0.04
LANES = 128
ROWS = 16
EXT = 32
FIELDS = 21
EDGES = 36
FORCES = 9
X_TILES = FIELDS + EDGES + FORCES
VMEM_LIMIT = 16 * 1024 * 1024
F32 = jnp.float32


def lane_index(shape):
    return lax.broadcasted_iota(jnp.int32, shape, len(shape) - 1)


def roll(values, shift, axis):
    size = values.shape[axis]
    shift = shift % size
    return values if shift == 0 else pltpu.roll(values, shift, axis)


def parities():
    return lax.axis_index("core"), lax.rem(lax.axis_index("x"), 2)


def each(count, body):
    def step(index, carry):
        body(index)
        return carry

    lax.fori_loop(0, count, step, 0)


def x_place(refs, index):
    state, switch, edges, forcing = refs
    if index < 18:
        return lambda rows: state[index, rows, :]
    index -= 18
    if index < 3:
        return lambda rows: switch[index, rows, :].astype(F32)
    index -= 3
    if index < EDGES:
        return lambda rows: edges[index, rows, :]
    index -= EDGES
    return lambda rows: forcing[index, rows, :]


def first_kernel(
    state_in, switch_in, edges_in, forcing_in,
    pair_out, odd_out, state, switch, edges, forcing, arrived,
):
    refs = (state, switch, edges, forcing)
    copies = [
        pltpu.make_async_copy(source, target, arrived.at[k])
        for k, (source, target) in enumerate(
            zip((state_in, switch_in, edges_in, forcing_in), refs, strict=True)
        )
    ]
    for copy in copies:
        copy.start()
    odd, _ = parities()
    near = pl.multiple_of(8 * (1 - odd), 8)
    far = pl.multiple_of(8 * odd, 8)
    for k in (0, 1, 3):
        copies[k].wait()
    peak = None
    total = None
    for plane in range(3):
        fields = [state[3 * k + plane] for k in range(6)]
        density = fields[0]
        inverse = 1.0 / density
        kinetic = 0.5 * inverse * (fields[1] ** 2 + fields[2] ** 2 + fields[3] ** 2)
        heat = jnp.where(switch[plane] == 1, fields[5], fields[4] - kinetic)
        sound = jnp.sqrt(ADIABATIC * (ADIABATIC - 1.0) * heat * inverse)
        speed = (
            jnp.abs(fields[1]) + jnp.abs(fields[2]) + jnp.abs(fields[3])
        ) * inverse + 3.0 * sound
        drive = [forcing[3 * k + plane] for k in range(3)]
        power = density * (drive[0] ** 2 + drive[1] ** 2 + drive[2] ** 2)
        peak = speed if peak is None else jnp.maximum(peak, speed)
        total = power if total is None else total + power
    row = lax.broadcasted_iota(jnp.int32, (8, LANES), 0)
    pair_out[X_TILES] = jnp.where(row == 0, jnp.max(peak), jnp.sum(total))
    copies[2].wait()
    for index in range(X_TILES):
        tile = x_place(refs, index)
        pair_out[index] = tile(pl.ds(near, 8))
        odd_out[index] = tile(pl.ds(far, 8))


def spread_kernel(rows, after, out):
    peak = jnp.max(rows[:, 0, :], axis=0, keepdims=True)
    total = jnp.sum(rows[:, 1, :], axis=0, keepdims=True)
    joined = jnp.concatenate([peak, total], axis=0)
    out[...] = jnp.broadcast_to(joined[None], out.shape)


def rows_around(odd_x, pair_in, odd_in, index, block):
    from_pair = pair_in[1 - odd_x, index]
    from_odd = odd_in[index]
    below = jnp.where(odd_x == 0, from_odd, from_pair)
    above = jnp.where(odd_x == 0, from_pair, from_odd)
    return jnp.concatenate([below, block, above], axis=0)


def turned(values, shift):
    return pltpu.roll(values, lax.rem(shift + LANES, LANES), 1)


def second_kernel(state, switch, edges, forcing, pair_in, odd_in, even_out, odd_out):
    odd_x, odd_y = parities()
    lane = lane_index((EXT, LANES))
    high = jnp.zeros((EXT, LANES), F32)
    low = jnp.zeros((EXT, LANES), F32)
    for index in range(FIELDS):
        block = x_place((state, switch, edges, forcing), index)(slice(0, ROWS))
        column = rows_around(odd_x, pair_in, odd_in, index, block)
        mine = (lane >= 6 * index) & (lane < 6 * index + 6)
        high = jnp.where(mine, roll(column, 6 * index - 122, 1), high)
        low = jnp.where(mine, roll(column, 6 * index, 1), low)
    even_out[0:EXT] = jnp.where(odd_y == 0, high, low)
    odd_out[0:EXT] = jnp.where(odd_y == 0, low, high)
    lane = lane[0:ROWS]
    for source, count, row in ((edges, EDGES, EXT), (forcing, FORCES, EXT + ROWS)):
        high = jnp.zeros((ROWS, LANES), F32)
        low = jnp.zeros((ROWS, LANES), F32)
        for index in range(count):
            mine = (lane >= 3 * index) & (lane < 3 * index + 3)
            high = jnp.where(mine, roll(source[index], 3 * index - 125, 1), high)
            low = jnp.where(mine, roll(source[index], 3 * index, 1), low)
        even_out[row : row + ROWS] = jnp.where(odd_y == 0, high, low)
        odd_out[row : row + ROWS] = jnp.where(odd_y == 0, low, high)


def median(one, two, three):
    return jnp.maximum(jnp.minimum(one, two), jnp.minimum(jnp.maximum(one, two), three))


def face_above(before, here, after, beyond):
    value = (7.0 / 12.0) * (here + after) - (1.0 / 12.0) * (before + beyond)
    return median(here, after, value)


def limited(here, face_low, face_high):
    thrice = 3.0 * here
    return (
        median(here, face_low, thrice - (face_high + face_high)),
        median(here, face_high, thrice - (face_low + face_low)),
    )


def sound_of(state):
    push = ADIABATIC * state[4]
    return push * lax.rsqrt(push * state[0])


def face_flux(left, right, normal):
    left_u, right_u = left[1 + normal], right[1 + normal]
    left_sound, right_sound = sound_of(left), sound_of(right)
    slow = jnp.minimum(jnp.minimum(left_u - left_sound, right_u - right_sound), 0.0)
    fast = jnp.maximum(jnp.maximum(left_u + left_sound, right_u + right_sound), 0.0)
    share = 1.0 / (fast - slow)
    left_part = fast * share
    right_part = -slow * share
    left_lead = left_u - slow
    right_lead = right_u - fast
    left_mass = left_part * left_lead * left[0]
    right_mass = right_part * right_lead * right[0]
    left_square = left[1] * left[1] + left[2] * left[2] + left[3] * left[3]
    right_square = right[1] * right[1] + right[2] * right[2] + right[3] * right[3]
    flux = [left_mass + right_mass]
    for k in (1, 2, 3):
        flux.append(left_mass * left[k] + right_mass * right[k])
    left_push = left_part * left[4]
    right_push = right_part * right[4]
    flux[1 + normal] = flux[1 + normal] + (left_push + right_push)
    flux.append(
        0.5 * (left_mass * left_square + right_mass * right_square)
        + left_push * (1.5 * left_lead + left_u)
        + right_push * (1.5 * right_lead + right_u)
    )
    flux.append(left_mass * left[5] + right_mass * right[5])
    return flux


def z_fluxes(planes):
    lower, upper = [], []
    for k in range(6):
        column = [planes[j][k] for j in range(9)]
        faces = [face_above(*column[j : j + 4]) for j in range(6)]
        cells = [limited(column[j + 2], faces[j], faces[j + 1]) for j in range(5)]
        lower.append([cells[j][1] for j in range(4)])
        upper.append([cells[j + 1][0] for j in range(4)])
    return [
        face_flux([lower[k][j] for k in range(6)], [upper[k][j] for k in range(6)], 2)
        for j in range(4)
    ]


def edge_primitives(fields):
    density = fields[0]
    inverse = 1.0 / density
    kinetic = 0.5 * inverse * (fields[1] ** 2 + fields[2] ** 2 + fields[3] ** 2)
    return [
        density,
        fields[1] * inverse,
        fields[2] * inverse,
        fields[3] * inverse,
        (ADIABATIC - 1.0) * (fields[4] - kinetic),
        fields[5] * inverse,
    ]


def shift_pair(main, rim, step):
    lane = lane_index(main.shape)
    main_rolled = roll(main, -step, 1)
    rim_rolled = roll(rim, -step, 1)
    inside = lane < LANES - step if step > 0 else lane >= -step
    return (
        jnp.where(inside, main_rolled, rim_rolled),
        jnp.where(inside, rim_rolled, main_rolled),
    )


def y_differences(main, rim):
    lows, highs = ([], []), ([], [])
    spread = None
    for k in range(6):
        here = (main[k], rim[k])
        before = shift_pair(*here, -1)
        after = shift_pair(*here, 1)
        beyond = shift_pair(*here, 2)
        faces = [face_above(before[j], here[j], after[j], beyond[j]) for j in range(2)]
        below = shift_pair(*faces, -1)
        cells = [limited(here[j], below[j], faces[j]) for j in range(2)]
        nexts = shift_pair(cells[0][0], cells[1][0], 1)
        for j in range(2):
            lows[j].append(cells[j][1])
            highs[j].append(nexts[j])
        if k == 2:
            spread = [0.5 * (after[j] - before[j]) for j in range(2)]
    fluxes = [face_flux(lows[j], highs[j], 1) for j in range(2)]
    differences = ([], [])
    for k in range(6):
        below = shift_pair(fluxes[0][k], fluxes[1][k], -1)
        for j in range(2):
            differences[j].append(fluxes[j][k] - below[j])
    return differences, spread


CHUNKS = (4, 12, 20)


def x_sweep(prims, low_ref, high_ref, face_ref, flux_ref):
    for row in CHUNKS:
        for k in range(6):
            before, here, after, beyond = [
                prims[k, pl.ds(row + s, 8), :] for s in (-1, 0, 1, 2)
            ]
            if row == CHUNKS[0]:
                below = face_above(prims[k, pl.ds(row - 2, 8), :], before, here, after)
            above = face_above(before, here, after, beyond)
            face_ref[k, pl.ds(row, 8), :] = above
            if row != CHUNKS[0]:
                below = face_ref[k, pl.ds(row - 1, 8), :]
            low_ref[k, pl.ds(row, 8), :], high_ref[k, pl.ds(row, 8), :] = limited(
                here, below, above
            )
    for row in CHUNKS:
        left = [high_ref[k, pl.ds(row, 8), :] for k in range(6)]
        right = [low_ref[k, pl.ds(row + 1, 8), :] for k in range(6)]
        flux = face_flux(left, right, 0)
        for k in range(6):
            flux_ref[k, pl.ds(row, 8), :] = flux[k]


def clear_ends(low_ref, flux_ref):
    for k in range(6):
        low_ref[k, pl.ds(28, 4), :] = jnp.ones((4, LANES), F32)
        flux_ref[k, pl.ds(0, 4), :] = jnp.zeros((4, LANES), F32)


def third_kernel(
    state, switch, edges, forcing, pair_in, odd_in, even_in, odd_y_in,
    fields, force, tend, outer, prims, planes, low_ref, high_ref, face_ref, flux_ref, strip_ref,
):
    odd_x, odd_y = parities()
    strip_ref[0] = jnp.where(odd_y == 0, even_in[...], odd_y_in[...])
    strip_ref[1] = jnp.where(odd_y == 0, odd_y_in[...], even_in[...])
    clear_ends(low_ref, flux_ref)
    lane = lane_index((EXT, LANES))
    edge_lane = lane[0:ROWS]

    def field_tiles(index, block):
        fields[0, index] = rows_around(odd_x, pair_in, odd_in, index, block)
        fields[1, index] = jnp.where(
            lane < 64,
            turned(strip_ref[0, 0:EXT], -6 * index),
            turned(strip_ref[1, 0:EXT], 122 - 6 * index),
        )

    def rim_tile(row, index):
        return jnp.where(
            edge_lane < 64,
            turned(strip_ref[0, row : row + ROWS], -3 * index),
            turned(strip_ref[1, row : row + ROWS], 125 - 3 * index),
        )

    @functools.partial(each, 6)
    def _(field):
        for plane in range(3):
            index = 3 * field + plane
            field_tiles(index, state[index])

    for plane in range(3):
        field_tiles(18 + plane, switch[plane].astype(F32))

    @functools.partial(each, 3)
    def _(part):
        for k in range(3):
            index = 3 * part + k
            force[0, index] = rows_around(
                odd_x, pair_in, odd_in, FIELDS + EDGES + index, forcing[index]
            )
            force[1, index, 0:8] = jnp.zeros((8, LANES), F32)
            force[1, index, 8:24] = rim_tile(EXT + ROWS, index)
            force[1, index, 24:32] = jnp.zeros((8, LANES), F32)

    @functools.partial(each, 6)
    def _(step):
        tile, plane = step // 3, step % 3
        values = [fields[tile, 3 * k + plane] for k in range(7)]
        density = values[0]
        inverse = 1.0 / density
        kinetic = 0.5 * inverse * (values[1] ** 2 + values[2] ** 2 + values[3] ** 2)
        heat = jnp.where(values[6] == 1.0, values[5], values[4] - kinetic)
        prims[tile, plane, 0] = density
        for k in (1, 2, 3):
            prims[tile, plane, k] = values[k] * inverse
        prims[tile, plane, 4] = (ADIABATIC - 1.0) * heat
        prims[tile, plane, 5] = values[5] * inverse

    @functools.partial(each, 6)
    def _(step):
        first = 18 * (step // 3) + step % 3
        places = [first + 3 * k for k in range(6)]
        values = edge_primitives(
            [rows_around(odd_x, pair_in, odd_in, FIELDS + k, edges[k]) for k in places]
        )
        for k in range(6):
            planes[0, step, k] = values[k]
            outer[step, k] = values[k][8:24]
        values = edge_primitives([rim_tile(EXT, k) for k in places])
        for k in range(6):
            planes[1, step, k, 0:8] = jnp.ones((8, LANES), F32)
            planes[1, step, k, 8:24] = values[k]
            planes[1, step, k, 24:32] = jnp.ones((8, LANES), F32)

    @functools.partial(each, 3)
    def _(plane):
        for row in CHUNKS:
            rows = pl.ds(row, 8)
            both = [[prims[tile, plane, k, rows, :] for k in range(6)] for tile in range(2)]
            differences, spread = y_differences(*both)
            for tile in range(2):
                for k in range(5):
                    tend[tile, 3 * k + plane, rows, :] = -differences[tile][k]
                tend[tile, 15 + plane, rows, :] = (
                    -differences[tile][5] - both[tile][4] * spread[tile]
                )

    @functools.partial(each, 6)
    def _(step):
        tile, plane = step // 3, step % 3
        x_sweep(prims.at[tile, plane], low_ref, high_ref, face_ref, flux_ref)
        for row in CHUNKS:
            rows = pl.ds(row, 8)
            for k in range(6):
                difference = flux_ref[k, rows, :] - flux_ref[k, pl.ds(row - 1, 8), :]
                if k == 5:
                    before = prims[tile, plane, 1, pl.ds(row - 1, 8), :]
                    after = prims[tile, plane, 1, pl.ds(row + 1, 8), :]
                    spread = 0.5 * (after - before)
                    difference = difference + prims[tile, plane, 4, rows, :] * spread
                tend[tile, 3 * k + plane, rows, :] -= difference

    @functools.partial(each, 2)
    def _(tile):
        for row in CHUNKS:
            rows = pl.ds(row, 8)
            column = (
                [[planes[tile, p, k, rows, :] for k in range(6)] for p in range(3)]
                + [[prims[tile, p, k, rows, :] for k in range(6)] for p in range(3)]
                + [[planes[tile, 3 + p, k, rows, :] for k in range(6)] for p in range(3)]
            )
            flux = z_fluxes(column)
            for plane in range(3):
                for k in range(6):
                    difference = flux[plane + 1][k] - flux[plane][k]
                    if k == 5:
                        spread = 0.5 * (column[plane + 4][3] - column[plane + 2][3])
                        difference = difference + column[plane + 3][4] * spread
                    tend[tile, 3 * k + plane, rows, :] -= difference


def fourth_kernel(
    cells, totals, fields, force, tend, outer_prims, out,
    updated, section, prims, low_ref, high_ref, face_ref, flux_ref, sent,
):
    peak = jnp.max(totals[:, 0, :], axis=0, keepdims=True)
    power = jnp.sum(totals[:, 1, :], axis=0, keepdims=True)
    time_step = CFL_NUMBER / peak
    scale = jnp.sqrt(INJECTION / (0.5 * time_step * (power / cells + 1e-06)))
    clear_ends(low_ref, flux_ref)

    def forced(values, drive, tendency):
        result = list(tendency)
        for k in (1, 2, 3):
            result[k] = result[k] + scale * values[0] * drive[k - 1]
        result[4] = result[4] + scale * (
            values[1] * drive[0] + values[2] * drive[1] + values[3] * drive[2]
        )
        return result

    def settle(values, switch, inverse):
        kinetic = 0.5 * inverse * (values[1] ** 2 + values[2] ** 2 + values[3] ** 2)
        values[5] = jnp.where(switch == 0.0, values[4] - kinetic, values[5])

    @functools.partial(each, 6)
    def _(step):
        tile, plane = step // 3, step % 3
        for row in CHUNKS:
            rows = pl.ds(row, 8)
            values = [fields[tile, 3 * k + plane, rows, :] for k in range(7)]
            drive = [force[tile, 3 * k + plane, rows, :] for k in range(3)]
            rate = forced(values, drive, [tend[tile, 3 * k + plane, rows, :] for k in range(6)])
            stage = [values[k] + time_step * rate[k] for k in range(6)]
            inverse = 1.0 / stage[0]
            settle(stage, values[6], inverse)
            for k in range(6):
                section[tile, plane, k, rows, :] = stage[k]
            prims[tile, plane, 0, rows, :] = stage[0]
            for k in (1, 2, 3):
                prims[tile, plane, k, rows, :] = stage[k] * inverse
            prims[tile, plane, 4, rows, :] = (ADIABATIC - 1.0) * stage[5]
            prims[tile, plane, 5, rows, :] = stage[5] * inverse

    @functools.partial(each, 2)
    def _(step):
        inner = pl.ds(pl.multiple_of(8 * step, 8), 8)
        rows = pl.ds(pl.multiple_of(8 * step + 8, 8), 8)
        outer = [[outer_prims[p, k, inner, :] for k in range(6)] for p in range(6)]
        column = (
            outer[0:3] + [[prims[0, p, k, rows, :] for k in range(6)] for p in range(3)] + outer[3:6]
        )
        flux = z_fluxes(column)
        for plane in range(3):
            for k in range(6):
                difference = flux[plane + 1][k] - flux[plane][k]
                if k == 5:
                    spread = 0.5 * (column[plane + 4][3] - column[plane + 2][3])
                    difference = difference + column[plane + 3][4] * spread
                updated[k, plane, inner, :] = -difference

    @functools.partial(each, 3)
    def _(plane):
        x_sweep(prims.at[0, plane], low_ref, high_ref, face_ref, flux_ref)
        for row in (8, 16):
            rows = pl.ds(row, 8)
            inner = pl.ds(row - 8, 8)
            both = [[prims[tile, plane, k, rows, :] for k in range(6)] for tile in range(2)]
            differences, spread = y_differences(*both)
            before = prims[0, plane, 1, pl.ds(row - 1, 8), :]
            after = prims[0, plane, 1, pl.ds(row + 1, 8), :]
            spread = spread[0] + 0.5 * (after - before)
            rate = []
            for k in range(6):
                across = flux_ref[k, rows, :] - flux_ref[k, pl.ds(row - 1, 8), :]
                rate.append(updated[k, plane, inner, :] - differences[0][k] - across)
            rate[5] = rate[5] - both[0][4] * spread
            stage = [section[0, plane, k, rows, :] for k in range(6)]
            drive = [force[0, 3 * k + plane, rows, :] for k in range(3)]
            rate = forced(stage, drive, rate)
            values = [fields[0, 3 * k + plane, rows, :] for k in range(7)]
            result = [
                0.5 * values[k] + 0.5 * (stage[k] + time_step * rate[k]) for k in range(6)
            ]
            settle(result, values[6], 1.0 / result[0])
            for k in range(6):
                updated[k, plane, inner, :] = result[k]
        pltpu.make_async_copy(updated.at[:, plane], out.at[:, plane], sent.at[plane]).start()

    for plane in range(3):
        pltpu.make_async_copy(updated.at[:, plane], out.at[:, plane], sent.at[plane]).wait()


def shape(*sizes):
    return jax.ShapeDtypeStruct(sizes, F32)


def vmem_specs(count):
    return [pl.BlockSpec(memory_space=pltpu.VMEM)] * count


def call(kernel, name, outs, arrays, scratch=(), cost=0, out_space=pltpu.VMEM):
    single = not isinstance(outs, tuple)
    out_spec = pl.BlockSpec(memory_space=out_space)
    return pl.pallas_call(
        kernel,
        out_shape=outs,
        in_specs=vmem_specs(len(arrays)),
        out_specs=out_spec if single else (out_spec,) * len(outs),
        scratch_shapes=list(scratch),
        compiler_params=pltpu.CompilerParams(vmem_limit_bytes=VMEM_LIMIT),
        cost_estimate=pl.CostEstimate(flops=cost, bytes_accessed=cost, transcendentals=0),
        name=name,
    )(*arrays)


def pairs(count, begin):
    table = []
    for first in range(begin, begin + count, 2):
        low, high = first % count, (first + 1) % count
        table += [(low, high), (high, low)]
    return table


def spread_over(rows, after, axes):
    return pl.pallas_call(
        spread_kernel,
        out_shape=shape(lax.axis_size(axes), 2, LANES),
        in_specs=[*vmem_specs(1), pl.BlockSpec(memory_space=pl.ANY)],
        out_specs=vmem_specs(1)[0],
        compiler_params=pltpu.CompilerParams(vmem_limit_bytes=VMEM_LIMIT),
        name="spread",
    )(rows, after)


def exchanged(spread, axes):
    return lax.all_to_all(spread, axes, 0, 0, tiled=True)


GX = ("zl", "core")
GY = ("y", "zh", "x")


def local(fluid_state, switch, z_edges, forcing):
    count_x = lax.axis_size(GX)
    count_y = lax.axis_size(GY)
    cells = 3.0 * ROWS * LANES * count_x * count_y
    tile = (8, LANES)
    block = (ROWS, LANES)
    inputs = (
        fluid_state.reshape(18, *block),
        switch,
        z_edges.reshape(EDGES, *block),
        forcing.reshape(FORCES, *block),
    )
    pair_out, odd_out, *arrays = pl.pallas_call(
        first_kernel,
        out_shape=(
            shape(X_TILES + 1, *tile),
            shape(X_TILES, *tile),
            *(jax.ShapeDtypeStruct(values.shape, values.dtype) for values in inputs),
        ),
        in_specs=[
            *([pl.BlockSpec(memory_space=pltpu.HBM)] * 4),
        ],
        out_specs=tuple(vmem_specs(6)),
        scratch_shapes=[pltpu.SemaphoreType.DMA((4,))],
        compiler_params=pltpu.CompilerParams(vmem_limit_bytes=VMEM_LIMIT),
        name="first",
    )(*(pltpu.with_memory_space_constraint(values, pltpu.HBM) for values in inputs))
    pair_in = lax.all_gather(pair_out, "core")
    rows = pair_in[:, X_TILES, 0:2]
    spread = spread_over(rows, rows, ("y", "x"))
    odd_out, spread = lax.optimization_barrier((odd_out, spread))
    odd_in = lax.ppermute(odd_out, GX, pairs(count_x, 1))
    totals = exchanged(spread, ("y", "x"))
    strips = call(
        second_kernel,
        "second",
        (shape(EXT + 2 * ROWS, LANES), shape(EXT + 2 * ROWS, LANES)),
        (*arrays, pair_in, odd_in),
        cost=4_000_000,
    )
    even_in = lax.ppermute(strips[0], GY, pairs(count_y, 0))
    odd_y_in = lax.ppermute(strips[1], GY, pairs(count_y, 1))
    totals = exchanged(spread_over(totals, even_in, ("zh", "zl")), ("zh", "zl"))
    extended = (EXT, LANES)
    work = [pltpu.VMEM((6, *extended), F32) for _ in range(4)]
    fields, force, tend, outer = call(
        third_kernel,
        "third",
        (
            shape(2, FIELDS, *extended),
            shape(2, FORCES, *extended),
            shape(2, 18, *extended),
            shape(6, 6, ROWS, LANES),
        ),
        (*arrays, pair_in, odd_in, even_in, odd_y_in),
        [
            pltpu.VMEM((2, 3, 6, *extended), F32),
            pltpu.VMEM((2, 6, 6, *extended), F32),
            *work,
            pltpu.VMEM((2, EXT + 2 * ROWS, LANES), F32),
        ],
        cost=60_000_000,
    )
    return call(
        functools.partial(fourth_kernel, cells),
        "fourth",
        shape(6, 3, ROWS, LANES),
        (totals, fields, force, tend, outer),
        [
            pltpu.VMEM((6, 3, ROWS, LANES), F32),
            pltpu.VMEM((2, 3, 6, *extended), F32),
            pltpu.VMEM((2, 3, 6, *extended), F32),
            *work,
            pltpu.SemaphoreType.DMA((3,)),
        ],
        cost=8_000_000,
        out_space=pltpu.HBM,
    )


def solution(mesh):
    count_x, count_y = mesh.devices.shape
    count_z = 2 if count_y % 8 == 0 else 1
    parts = (count_x // 2, 2, count_y // (4 * count_z), count_z, 4)
    split = Mesh(mesh.devices.reshape(parts), (*GX, *GY))
    return jax.shard_map(
        local,
        mesh=split,
        in_specs=(
            P(None, None, GX, GY),
            P(None, GX, GY),
            P(None, None, None, GX, GY),
            P(None, None, GX, GY),
        ),
        out_specs=P(None, None, GX, GY),
        check_vma=False,
    )
```

```python
import functools

import jax
import jax.numpy as jnp
from jax import lax
from jax.experimental import pallas as pl
from jax.experimental.pallas import tpu as pltpu
from jax.sharding import Mesh
from jax.sharding import PartitionSpec as P

ADIABATIC = 5.0 / 3.0
CFL_NUMBER = 0.4
INJECTION = 0.04
LANES = 128
ROWS = 16
EXT = 32
FIELDS = 21
EDGES = 36
FORCES = 9
X_TILES = FIELDS + EDGES + FORCES
VMEM_LIMIT = 16 * 1024 * 1024
F32 = jnp.float32


def lane_index(shape):
    return lax.broadcasted_iota(jnp.int32, shape, len(shape) - 1)


def roll(values, shift, axis):
    size = values.shape[axis]
    shift = shift % size
    return values if shift == 0 else pltpu.roll(values, shift, axis)


def parities():
    return lax.axis_index("core"), lax.rem(lax.axis_index("x"), 2)


def each(count, body):
    def step(index, carry):
        body(index)
        return carry

    lax.fori_loop(0, count, step, 0)


def x_place(refs, index):
    state, switch, edges, forcing = refs
    if index < 18:
        return lambda rows: state[index, rows, :]
    index -= 18
    if index < 3:
        return lambda rows: switch[index, rows, :].astype(F32)
    index -= 3
    if index < EDGES:
        return lambda rows: edges[index, rows, :]
    index -= EDGES
    return lambda rows: forcing[index, rows, :]


def first_kernel(
    state_in, switch_in, edges_in, forcing_in,
    pair_out, odd_out, state, switch, edges, forcing, arrived,
):
    refs = (state, switch, edges, forcing)
    copies = [
        pltpu.make_async_copy(source, target, arrived.at[k])
        for k, (source, target) in enumerate(
            zip((state_in, switch_in, edges_in, forcing_in), refs, strict=True)
        )
    ]
    for k in (2, 0, 3, 1):
        copies[k].start()
    odd, _ = parities()
    near = pl.multiple_of(8 * (1 - odd), 8)
    far = pl.multiple_of(8 * odd, 8)
    for k in (0, 1, 3):
        copies[k].wait()
    peak = None
    total = None
    for plane in range(3):
        fields = [state[3 * k + plane] for k in range(6)]
        density = fields[0]
        inverse = 1.0 / density
        kinetic = 0.5 * inverse * (fields[1] ** 2 + fields[2] ** 2 + fields[3] ** 2)
        heat = jnp.where(switch[plane] == 1, fields[5], fields[4] - kinetic)
        sound = jnp.sqrt(ADIABATIC * (ADIABATIC - 1.0) * heat * inverse)
        speed = (
            jnp.abs(fields[1]) + jnp.abs(fields[2]) + jnp.abs(fields[3])
        ) * inverse + 3.0 * sound
        drive = [forcing[3 * k + plane] for k in range(3)]
        power = density * (drive[0] ** 2 + drive[1] ** 2 + drive[2] ** 2)
        peak = speed if peak is None else jnp.maximum(peak, speed)
        total = power if total is None else total + power
    row = lax.broadcasted_iota(jnp.int32, (8, LANES), 0)
    pair_out[X_TILES] = jnp.where(row == 0, jnp.max(peak), jnp.sum(total))
    copies[2].wait()
    for index in range(X_TILES):
        tile = x_place(refs, index)
        pair_out[index] = tile(pl.ds(near, 8))
        odd_out[index] = tile(pl.ds(far, 8))


def spread_kernel(rows, after, out):
    peak = jnp.max(rows[:, 0, :], axis=0, keepdims=True)
    total = jnp.sum(rows[:, 1, :], axis=0, keepdims=True)
    joined = jnp.concatenate([peak, total], axis=0)
    out[...] = jnp.broadcast_to(joined[None], out.shape)


def rows_around(odd_x, pair_in, odd_in, index, block):
    from_pair = pair_in[1 - odd_x, index]
    from_odd = odd_in[index]
    below = jnp.where(odd_x == 0, from_odd, from_pair)
    above = jnp.where(odd_x == 0, from_pair, from_odd)
    return jnp.concatenate([below, block, above], axis=0)


def turned(values, shift):
    return pltpu.roll(values, lax.rem(shift + LANES, LANES), 1)


def second_kernel(state, switch, edges, forcing, pair_in, odd_in, even_out, odd_out):
    odd_x, odd_y = parities()
    lane = lane_index((EXT, LANES))
    high = jnp.zeros((EXT, LANES), F32)
    low = jnp.zeros((EXT, LANES), F32)
    for index in range(FIELDS):
        block = x_place((state, switch, edges, forcing), index)(slice(0, ROWS))
        column = rows_around(odd_x, pair_in, odd_in, index, block)
        mine = (lane >= 6 * index) & (lane < 6 * index + 6)
        high = jnp.where(mine, roll(column, 6 * index - 122, 1), high)
        low = jnp.where(mine, roll(column, 6 * index, 1), low)
    even_out[0:EXT] = jnp.where(odd_y == 0, high, low)
    odd_out[0:EXT] = jnp.where(odd_y == 0, low, high)
    lane = lane[0:ROWS]
    for source, count, row in ((edges, EDGES, EXT), (forcing, FORCES, EXT + ROWS)):
        high = jnp.zeros((ROWS, LANES), F32)
        low = jnp.zeros((ROWS, LANES), F32)
        for index in range(count):
            mine = (lane >= 3 * index) & (lane < 3 * index + 3)
            high = jnp.where(mine, roll(source[index], 3 * index - 125, 1), high)
            low = jnp.where(mine, roll(source[index], 3 * index, 1), low)
        even_out[row : row + ROWS] = jnp.where(odd_y == 0, high, low)
        odd_out[row : row + ROWS] = jnp.where(odd_y == 0, low, high)


def median(one, two, three):
    return jnp.maximum(jnp.minimum(one, two), jnp.minimum(jnp.maximum(one, two), three))


def face_above(before, here, after, beyond):
    value = (7.0 / 12.0) * (here + after) - (1.0 / 12.0) * (before + beyond)
    return median(here, after, value)


def limited(here, face_low, face_high):
    thrice = 3.0 * here
    return (
        median(here, face_low, thrice - (face_high + face_high)),
        median(here, face_high, thrice - (face_low + face_low)),
    )


def sound_of(state):
    push = ADIABATIC * state[4]
    return push * lax.rsqrt(push * state[0])


def face_flux(left, right, normal):
    left_u, right_u = left[1 + normal], right[1 + normal]
    left_sound, right_sound = sound_of(left), sound_of(right)
    slow = jnp.minimum(jnp.minimum(left_u - left_sound, right_u - right_sound), 0.0)
    fast = jnp.maximum(jnp.maximum(left_u + left_sound, right_u + right_sound), 0.0)
    share = 1.0 / (fast - slow)
    left_part = fast * share
    right_part = -slow * share
    left_lead = left_u - slow
    right_lead = right_u - fast
    left_mass = left_part * left_lead * left[0]
    right_mass = right_part * right_lead * right[0]
    left_square = left[1] * left[1] + left[2] * left[2] + left[3] * left[3]
    right_square = right[1] * right[1] + right[2] * right[2] + right[3] * right[3]
    flux = [left_mass + right_mass]
    for k in (1, 2, 3):
        flux.append(left_mass * left[k] + right_mass * right[k])
    left_push = left_part * left[4]
    right_push = right_part * right[4]
    flux[1 + normal] = flux[1 + normal] + (left_push + right_push)
    flux.append(
        0.5 * (left_mass * left_square + right_mass * right_square)
        + left_push * (1.5 * left_lead + left_u)
        + right_push * (1.5 * right_lead + right_u)
    )
    flux.append(left_mass * left[5] + right_mass * right[5])
    return flux


def z_fluxes(planes):
    lower, upper = [], []
    for k in range(6):
        column = [planes[j][k] for j in range(9)]
        faces = [face_above(*column[j : j + 4]) for j in range(6)]
        cells = [limited(column[j + 2], faces[j], faces[j + 1]) for j in range(5)]
        lower.append([cells[j][1] for j in range(4)])
        upper.append([cells[j + 1][0] for j in range(4)])
    return [
        face_flux([lower[k][j] for k in range(6)], [upper[k][j] for k in range(6)], 2)
        for j in range(4)
    ]


def edge_primitives(fields):
    density = fields[0]
    inverse = 1.0 / density
    kinetic = 0.5 * inverse * (fields[1] ** 2 + fields[2] ** 2 + fields[3] ** 2)
    return [
        density,
        fields[1] * inverse,
        fields[2] * inverse,
        fields[3] * inverse,
        (ADIABATIC - 1.0) * (fields[4] - kinetic),
        fields[5] * inverse,
    ]


def shift_pair(main, rim, step):
    lane = lane_index(main.shape)
    main_rolled = roll(main, -step, 1)
    rim_rolled = roll(rim, -step, 1)
    inside = lane < LANES - step if step > 0 else lane >= -step
    return (
        jnp.where(inside, main_rolled, rim_rolled),
        jnp.where(inside, rim_rolled, main_rolled),
    )


def y_differences(main, rim):
    lows, highs = ([], []), ([], [])
    spread = None
    for k in range(6):
        here = (main[k], rim[k])
        before = shift_pair(*here, -1)
        after = shift_pair(*here, 1)
        beyond = shift_pair(*here, 2)
        faces = [face_above(before[j], here[j], after[j], beyond[j]) for j in range(2)]
        below = shift_pair(*faces, -1)
        cells = [limited(here[j], below[j], faces[j]) for j in range(2)]
        nexts = shift_pair(cells[0][0], cells[1][0], 1)
        for j in range(2):
            lows[j].append(cells[j][1])
            highs[j].append(nexts[j])
        if k == 2:
            spread = [0.5 * (after[j] - before[j]) for j in range(2)]
    fluxes = [face_flux(lows[j], highs[j], 1) for j in range(2)]
    differences = ([], [])
    for k in range(6):
        below = shift_pair(fluxes[0][k], fluxes[1][k], -1)
        for j in range(2):
            differences[j].append(fluxes[j][k] - below[j])
    return differences, spread


CHUNKS = (4, 12, 20)


def x_sweep(prims, low_ref, high_ref, face_ref, flux_ref):
    for row in CHUNKS:
        for k in range(6):
            before, here, after, beyond = [
                prims[k, pl.ds(row + s, 8), :] for s in (-1, 0, 1, 2)
            ]
            if row == CHUNKS[0]:
                below = face_above(prims[k, pl.ds(row - 2, 8), :], before, here, after)
            above = face_above(before, here, after, beyond)
            face_ref[k, pl.ds(row, 8), :] = above
            if row != CHUNKS[0]:
                below = face_ref[k, pl.ds(row - 1, 8), :]
            low_ref[k, pl.ds(row, 8), :], high_ref[k, pl.ds(row, 8), :] = limited(
                here, below, above
            )
    for row in CHUNKS:
        left = [high_ref[k, pl.ds(row, 8), :] for k in range(6)]
        right = [low_ref[k, pl.ds(row + 1, 8), :] for k in range(6)]
        flux = face_flux(left, right, 0)
        for k in range(6):
            flux_ref[k, pl.ds(row, 8), :] = flux[k]


def clear_ends(low_ref, flux_ref):
    for k in range(6):
        low_ref[k, pl.ds(28, 4), :] = jnp.ones((4, LANES), F32)
        flux_ref[k, pl.ds(0, 4), :] = jnp.zeros((4, LANES), F32)


def third_kernel(
    state, switch, edges, forcing, pair_in, odd_in, even_in, odd_y_in,
    fields, force, tend, outer, prims, planes, low_ref, high_ref, face_ref, flux_ref, strip_ref,
):
    odd_x, odd_y = parities()
    strip_ref[0] = jnp.where(odd_y == 0, even_in[...], odd_y_in[...])
    strip_ref[1] = jnp.where(odd_y == 0, odd_y_in[...], even_in[...])
    clear_ends(low_ref, flux_ref)
    lane = lane_index((EXT, LANES))
    edge_lane = lane[0:ROWS]

    def field_tiles(index, block):
        fields[0, index] = rows_around(odd_x, pair_in, odd_in, index, block)
        fields[1, index] = jnp.where(
            lane < 64,
            turned(strip_ref[0, 0:EXT], -6 * index),
            turned(strip_ref[1, 0:EXT], 122 - 6 * index),
        )

    def rim_tile(row, index):
        return jnp.where(
            edge_lane < 64,
            turned(strip_ref[0, row : row + ROWS], -3 * index),
            turned(strip_ref[1, row : row + ROWS], 125 - 3 * index),
        )

    @functools.partial(each, 6)
    def _(field):
        for plane in range(3):
            index = 3 * field + plane
            field_tiles(index, state[index])

    for plane in range(3):
        field_tiles(18 + plane, switch[plane].astype(F32))

    @functools.partial(each, 3)
    def _(part):
        for k in range(3):
            index = 3 * part + k
            force[0, index] = rows_around(
                odd_x, pair_in, odd_in, FIELDS + EDGES + index, forcing[index]
            )
            force[1, index, 0:8] = jnp.zeros((8, LANES), F32)
            force[1, index, 8:24] = rim_tile(EXT + ROWS, index)
            force[1, index, 24:32] = jnp.zeros((8, LANES), F32)

    @functools.partial(each, 6)
    def _(step):
        tile, plane = step // 3, step % 3
        values = [fields[tile, 3 * k + plane] for k in range(7)]
        density = values[0]
        inverse = 1.0 / density
        kinetic = 0.5 * inverse * (values[1] ** 2 + values[2] ** 2 + values[3] ** 2)
        heat = jnp.where(values[6] == 1.0, values[5], values[4] - kinetic)
        prims[tile, plane, 0] = density
        for k in (1, 2, 3):
            prims[tile, plane, k] = values[k] * inverse
        prims[tile, plane, 4] = (ADIABATIC - 1.0) * heat
        prims[tile, plane, 5] = values[5] * inverse

    @functools.partial(each, 6)
    def _(step):
        first = 18 * (step // 3) + step % 3
        places = [first + 3 * k for k in range(6)]
        values = edge_primitives(
            [rows_around(odd_x, pair_in, odd_in, FIELDS + k, edges[k]) for k in places]
        )
        for k in range(6):
            planes[0, step, k] = values[k]
            outer[step, k] = values[k][8:24]
        values = edge_primitives([rim_tile(EXT, k) for k in places])
        for k in range(6):
            planes[1, step, k, 0:8] = jnp.ones((8, LANES), F32)
            planes[1, step, k, 8:24] = values[k]
            planes[1, step, k, 24:32] = jnp.ones((8, LANES), F32)

    @functools.partial(each, 3)
    def _(plane):
        for row in CHUNKS:
            rows = pl.ds(row, 8)
            both = [[prims[tile, plane, k, rows, :] for k in range(6)] for tile in range(2)]
            differences, spread = y_differences(*both)
            for tile in range(2):
                for k in range(5):
                    tend[tile, 3 * k + plane, rows, :] = -differences[tile][k]
                tend[tile, 15 + plane, rows, :] = (
                    -differences[tile][5] - both[tile][4] * spread[tile]
                )

    @functools.partial(each, 6)
    def _(step):
        tile, plane = step // 3, step % 3
        x_sweep(prims.at[tile, plane], low_ref, high_ref, face_ref, flux_ref)
        for row in CHUNKS:
            rows = pl.ds(row, 8)
            for k in range(6):
                difference = flux_ref[k, rows, :] - flux_ref[k, pl.ds(row - 1, 8), :]
                if k == 5:
                    before = prims[tile, plane, 1, pl.ds(row - 1, 8), :]
                    after = prims[tile, plane, 1, pl.ds(row + 1, 8), :]
                    spread = 0.5 * (after - before)
                    difference = difference + prims[tile, plane, 4, rows, :] * spread
                tend[tile, 3 * k + plane, rows, :] -= difference

    @functools.partial(each, 2)
    def _(tile):
        for row in CHUNKS:
            rows = pl.ds(row, 8)
            column = (
                [[planes[tile, p, k, rows, :] for k in range(6)] for p in range(3)]
                + [[prims[tile, p, k, rows, :] for k in range(6)] for p in range(3)]
                + [[planes[tile, 3 + p, k, rows, :] for k in range(6)] for p in range(3)]
            )
            flux = z_fluxes(column)
            for plane in range(3):
                for k in range(6):
                    difference = flux[plane + 1][k] - flux[plane][k]
                    if k == 5:
                        spread = 0.5 * (column[plane + 4][3] - column[plane + 2][3])
                        difference = difference + column[plane + 3][4] * spread
                    tend[tile, 3 * k + plane, rows, :] -= difference


def fourth_kernel(
    cells, totals, fields, force, tend, outer_prims, out,
    updated, section, prims, low_ref, high_ref, face_ref, flux_ref, sent,
):
    peak = jnp.max(totals[:, 0, :], axis=0, keepdims=True)
    power = jnp.sum(totals[:, 1, :], axis=0, keepdims=True)
    time_step = CFL_NUMBER / peak
    scale = jnp.sqrt(INJECTION / (0.5 * time_step * (power / cells + 1e-06)))
    clear_ends(low_ref, flux_ref)

    def forced(values, drive, tendency):
        result = list(tendency)
        for k in (1, 2, 3):
            result[k] = result[k] + scale * values[0] * drive[k - 1]
        result[4] = result[4] + scale * (
            values[1] * drive[0] + values[2] * drive[1] + values[3] * drive[2]
        )
        return result

    def settle(values, switch, inverse):
        kinetic = 0.5 * inverse * (values[1] ** 2 + values[2] ** 2 + values[3] ** 2)
        values[5] = jnp.where(switch == 0.0, values[4] - kinetic, values[5])

    def advance(tile, plane, chunks):
        for row in chunks:
            rows = pl.ds(row, 8)
            values = [fields[tile, 3 * k + plane, rows, :] for k in range(7)]
            drive = [force[tile, 3 * k + plane, rows, :] for k in range(3)]
            rate = forced(values, drive, [tend[tile, 3 * k + plane, rows, :] for k in range(6)])
            stage = [values[k] + time_step * rate[k] for k in range(6)]
            inverse = 1.0 / stage[0]
            settle(stage, values[6], inverse)
            if tile == 0:
                for k in range(6):
                    section[plane, k, rows, :] = stage[k]
            prims[tile, plane, 0, rows, :] = stage[0]
            for k in (1, 2, 3):
                prims[tile, plane, k, rows, :] = stage[k] * inverse
            prims[tile, plane, 4, rows, :] = (ADIABATIC - 1.0) * stage[5]
            prims[tile, plane, 5, rows, :] = stage[5] * inverse

    @functools.partial(each, 3)
    def _(plane):
        advance(0, plane, CHUNKS)
        advance(1, plane, (8, 16))

    @functools.partial(each, 2)
    def _(step):
        inner = pl.ds(pl.multiple_of(8 * step, 8), 8)
        rows = pl.ds(pl.multiple_of(8 * step + 8, 8), 8)
        outer = [[outer_prims[p, k, inner, :] for k in range(6)] for p in range(6)]
        column = (
            outer[0:3] + [[prims[0, p, k, rows, :] for k in range(6)] for p in range(3)] + outer[3:6]
        )
        flux = z_fluxes(column)
        for plane in range(3):
            for k in range(6):
                difference = flux[plane + 1][k] - flux[plane][k]
                if k == 5:
                    spread = 0.5 * (column[plane + 4][3] - column[plane + 2][3])
                    difference = difference + column[plane + 3][4] * spread
                updated[k, plane, inner, :] = -difference

    @functools.partial(each, 3)
    def _(plane):
        x_sweep(prims.at[0, plane], low_ref, high_ref, face_ref, flux_ref)
        for row in (8, 16):
            rows = pl.ds(row, 8)
            inner = pl.ds(row - 8, 8)
            both = [[prims[tile, plane, k, rows, :] for k in range(6)] for tile in range(2)]
            differences, spread = y_differences(*both)
            before = prims[0, plane, 1, pl.ds(row - 1, 8), :]
            after = prims[0, plane, 1, pl.ds(row + 1, 8), :]
            spread = spread[0] + 0.5 * (after - before)
            rate = []
            for k in range(6):
                across = flux_ref[k, rows, :] - flux_ref[k, pl.ds(row - 1, 8), :]
                rate.append(updated[k, plane, inner, :] - differences[0][k] - across)
            rate[5] = rate[5] - both[0][4] * spread
            stage = [section[plane, k, rows, :] for k in range(6)]
            drive = [force[0, 3 * k + plane, rows, :] for k in range(3)]
            rate = forced(stage, drive, rate)
            values = [fields[0, 3 * k + plane, rows, :] for k in range(7)]
            result = [
                0.5 * values[k] + 0.5 * (stage[k] + time_step * rate[k]) for k in range(6)
            ]
            settle(result, values[6], 1.0 / result[0])
            for k in range(6):
                updated[k, plane, inner, :] = result[k]
        pltpu.make_async_copy(updated.at[:, plane], out.at[:, plane], sent.at[plane]).start()

    for plane in range(3):
        pltpu.make_async_copy(updated.at[:, plane], out.at[:, plane], sent.at[plane]).wait()


def shape(*sizes):
    return jax.ShapeDtypeStruct(sizes, F32)


def vmem_specs(count):
    return [pl.BlockSpec(memory_space=pltpu.VMEM)] * count


def call(kernel, name, outs, arrays, scratch=(), cost=0, out_space=pltpu.VMEM):
    single = not isinstance(outs, tuple)
    out_spec = pl.BlockSpec(memory_space=out_space)
    return pl.pallas_call(
        kernel,
        out_shape=outs,
        in_specs=vmem_specs(len(arrays)),
        out_specs=out_spec if single else (out_spec,) * len(outs),
        scratch_shapes=list(scratch),
        compiler_params=pltpu.CompilerParams(vmem_limit_bytes=VMEM_LIMIT),
        cost_estimate=pl.CostEstimate(flops=cost, bytes_accessed=cost, transcendentals=0),
        name=name,
    )(*arrays)


def pairs(count, begin):
    table = []
    for first in range(begin, begin + count, 2):
        low, high = first % count, (first + 1) % count
        table += [(low, high), (high, low)]
    return table


def spread_over(rows, after, axes):
    return pl.pallas_call(
        spread_kernel,
        out_shape=shape(lax.axis_size(axes), 2, LANES),
        in_specs=[*vmem_specs(1), pl.BlockSpec(memory_space=pl.ANY)],
        out_specs=vmem_specs(1)[0],
        compiler_params=pltpu.CompilerParams(vmem_limit_bytes=VMEM_LIMIT),
        name="spread",
    )(rows, after)


def exchanged(spread, axes):
    return lax.all_to_all(spread, axes, 0, 0, tiled=True)


GX = ("zl", "core")
GY = ("y", "zh", "x")


def local(fluid_state, switch, z_edges, forcing):
    count_x = lax.axis_size(GX)
    count_y = lax.axis_size(GY)
    cells = 3.0 * ROWS * LANES * count_x * count_y
    tile = (8, LANES)
    block = (ROWS, LANES)
    inputs = (
        fluid_state.reshape(18, *block),
        switch,
        z_edges.reshape(EDGES, *block),
        forcing.reshape(FORCES, *block),
    )
    pair_out, odd_out, *arrays = pl.pallas_call(
        first_kernel,
        out_shape=(
            shape(X_TILES + 1, *tile),
            shape(X_TILES, *tile),
            *(jax.ShapeDtypeStruct(values.shape, values.dtype) for values in inputs),
        ),
        in_specs=[
            *([pl.BlockSpec(memory_space=pltpu.HBM)] * 4),
        ],
        out_specs=tuple(vmem_specs(6)),
        scratch_shapes=[pltpu.SemaphoreType.DMA((4,))],
        compiler_params=pltpu.CompilerParams(vmem_limit_bytes=VMEM_LIMIT),
        name="first",
    )(*(pltpu.with_memory_space_constraint(values, pltpu.HBM) for values in inputs))
    pair_in = lax.all_gather(pair_out, "core")
    rows = pair_in[:, X_TILES, 0:2]
    spread = spread_over(rows, rows, ("y", "x"))
    odd_out, spread = lax.optimization_barrier((odd_out, spread))
    odd_in = lax.ppermute(odd_out, GX, pairs(count_x, 1))
    totals = exchanged(spread, ("y", "x"))
    strips = call(
        second_kernel,
        "second",
        (shape(EXT + 2 * ROWS, LANES), shape(EXT + 2 * ROWS, LANES)),
        (*arrays, pair_in, odd_in),
        cost=4_000_000,
    )
    even_in = lax.ppermute(strips[0], GY, pairs(count_y, 0))
    odd_y_in = lax.ppermute(strips[1], GY, pairs(count_y, 1))
    totals = exchanged(spread_over(totals, even_in, ("zh", "zl")), ("zh", "zl"))
    extended = (EXT, LANES)
    work = [pltpu.VMEM((6, *extended), F32) for _ in range(4)]
    fields, force, tend, outer = call(
        third_kernel,
        "third",
        (
            shape(2, FIELDS, *extended),
            shape(2, FORCES, *extended),
            shape(2, 18, *extended),
            shape(6, 6, ROWS, LANES),
        ),
        (*arrays, pair_in, odd_in, even_in, odd_y_in),
        [
            pltpu.VMEM((2, 3, 6, *extended), F32),
            pltpu.VMEM((2, 6, 6, *extended), F32),
            *work,
            pltpu.VMEM((2, EXT + 2 * ROWS, LANES), F32),
        ],
        cost=60_000_000,
    )
    return call(
        functools.partial(fourth_kernel, cells),
        "fourth",
        shape(6, 3, ROWS, LANES),
        (totals, fields, force, tend, outer),
        [
            pltpu.VMEM((6, 3, ROWS, LANES), F32),
            pltpu.VMEM((3, 6, *extended), F32),
            pltpu.VMEM((2, 3, 6, *extended), F32),
            *work,
            pltpu.SemaphoreType.DMA((3,)),
        ],
        cost=8_000_000,
        out_space=pltpu.HBM,
    )


def solution(mesh):
    count_x, count_y = mesh.devices.shape
    count_z = 2 if count_y % 8 == 0 else 1
    parts = (count_x // 2, 2, count_y // (4 * count_z), count_z, 4)
    split = Mesh(mesh.devices.reshape(parts), (*GX, *GY))
    return jax.shard_map(
        local,
        mesh=split,
        in_specs=(
            P(None, None, GX, GY),
            P(None, GX, GY),
            P(None, None, None, GX, GY),
            P(None, None, GX, GY),
        ),
        out_specs=P(None, None, GX, GY),
        check_vma=False,
    )
```

```python
import functools

import jax
import jax.numpy as jnp
from jax import lax
from jax.experimental import pallas as pl
from jax.experimental.pallas import tpu as pltpu
from jax.sharding import Mesh
from jax.sharding import PartitionSpec as P

ADIABATIC = 5.0 / 3.0
CFL_NUMBER = 0.4
INJECTION = 0.04
LANES = 128
ROWS = 16
EXT = 32
FIELDS = 21
EDGES = 36
FORCES = 9
HALVES = 23
PAYLOAD = FIELDS + HALVES
VMEM_LIMIT = 16 * 1024 * 1024
F32 = jnp.float32


def lane_index(shape):
    return lax.broadcasted_iota(jnp.int32, shape, len(shape) - 1)


def roll(values, shift, axis):
    size = values.shape[axis]
    shift = shift % size
    return values if shift == 0 else pltpu.roll(values, shift, axis)


def parities():
    return lax.axis_index("core"), lax.rem(lax.axis_index("x"), 2)


def each(count, body):
    def step(index, carry):
        body(index)
        return carry

    lax.fori_loop(0, count, step, 0)


def x_place(refs, index):
    state, switch, edges, forcing = refs
    if index < 18:
        return lambda rows: state[index, rows, :]
    index -= 18
    if index < 3:
        return lambda rows: switch[index, rows, :].astype(F32)
    index -= 3
    if index < EDGES:
        return lambda rows: edges[index, rows, :]
    index -= EDGES
    return lambda rows: forcing[index, rows, :]


def first_kernel(
    state_in, switch_in, edges_in, forcing_in,
    pair_out, odd_out, state, switch, edges, forcing, arrived,
):
    refs = (state, switch, edges, forcing)
    copies = [
        pltpu.make_async_copy(source, target, arrived.at[k])
        for k, (source, target) in enumerate(
            zip((state_in, switch_in, edges_in, forcing_in), refs, strict=True)
        )
    ]
    for k in (2, 0, 3, 1):
        copies[k].start()
    odd, _ = parities()
    near = pl.multiple_of(8 * (1 - odd), 8)
    far = pl.multiple_of(8 * odd, 8)
    for k in (0, 1, 3):
        copies[k].wait()
    peak = None
    total = None
    for plane in range(3):
        fields = [state[3 * k + plane] for k in range(6)]
        density = fields[0]
        inverse = 1.0 / density
        kinetic = 0.5 * inverse * (fields[1] ** 2 + fields[2] ** 2 + fields[3] ** 2)
        heat = jnp.where(switch[plane] == 1, fields[5], fields[4] - kinetic)
        sound = jnp.sqrt(ADIABATIC * (ADIABATIC - 1.0) * heat * inverse)
        speed = (
            jnp.abs(fields[1]) + jnp.abs(fields[2]) + jnp.abs(fields[3])
        ) * inverse + 3.0 * sound
        drive = [forcing[3 * k + plane] for k in range(3)]
        power = density * (drive[0] ** 2 + drive[1] ** 2 + drive[2] ** 2)
        peak = speed if peak is None else jnp.maximum(peak, speed)
        total = power if total is None else total + power
    row = lax.broadcasted_iota(jnp.int32, (8, LANES), 0)
    pair_out[PAYLOAD] = jnp.where(row == 0, jnp.max(peak), jnp.sum(total))
    copies[2].wait()
    upper = lax.broadcasted_iota(jnp.int32, (8, LANES), 0) // 4
    for out, start, keep in (
        (pair_out, near, upper == 1 - odd),
        (odd_out, far, upper == odd),
    ):
        rows = pl.ds(start, 8)
        for index in range(PAYLOAD):
            tile = x_place(refs, index)(rows)
            if index >= FIELDS and index + HALVES < FIELDS + EDGES + FORCES:
                other = x_place(refs, index + HALVES)(rows)
                tile = jnp.where(keep, tile, roll(other, 4, 0))
            out[index] = tile


def spread_kernel(rows, after, out):
    peak = jnp.max(rows[:, 0, :], axis=0, keepdims=True)
    total = jnp.sum(rows[:, 1, :], axis=0, keepdims=True)
    joined = jnp.concatenate([peak, total], axis=0)
    out[...] = jnp.broadcast_to(joined[None], out.shape)


def rows_around(odd_x, pair_in, odd_in, index, block):
    from_pair = pair_in[1 - odd_x, index]
    from_odd = odd_in[index]
    below = jnp.where(odd_x == 0, from_odd, from_pair)
    above = jnp.where(odd_x == 0, from_pair, from_odd)
    return jnp.concatenate([below, block, above], axis=0)


def rows_around_half(odd_x, pair_in, odd_in, index, block):
    second = index >= HALVES
    slot = FIELDS + jnp.where(second, index - HALVES, index)
    column = rows_around(odd_x, pair_in, odd_in, slot, block)
    below, above = column[0:8], column[ROWS + 8 :]
    return jnp.concatenate(
        [
            jnp.where(second, roll(below, 4, 0), below),
            block,
            jnp.where(second, roll(above, 4, 0), above),
        ],
        axis=0,
    )


def turned(values, shift):
    return pltpu.roll(values, lax.rem(shift + LANES, LANES), 1)


def second_kernel(state, switch, edges, forcing, pair_in, odd_in, even_out, odd_out):
    odd_x, odd_y = parities()
    lane = lane_index((EXT, LANES))
    high = jnp.zeros((EXT, LANES), F32)
    low = jnp.zeros((EXT, LANES), F32)
    for index in range(FIELDS):
        block = x_place((state, switch, edges, forcing), index)(slice(0, ROWS))
        column = rows_around(odd_x, pair_in, odd_in, index, block)
        mine = (lane >= 6 * index) & (lane < 6 * index + 6)
        high = jnp.where(mine, roll(column, 6 * index - 122, 1), high)
        low = jnp.where(mine, roll(column, 6 * index, 1), low)
    even_out[0:EXT] = jnp.where(odd_y == 0, high, low)
    odd_out[0:EXT] = jnp.where(odd_y == 0, low, high)
    lane = lane[0:ROWS]
    for source, count, row in ((edges, EDGES, EXT), (forcing, FORCES, EXT + ROWS)):
        high = jnp.zeros((ROWS, LANES), F32)
        low = jnp.zeros((ROWS, LANES), F32)
        for index in range(count):
            mine = (lane >= 3 * index) & (lane < 3 * index + 3)
            high = jnp.where(mine, roll(source[index], 3 * index - 125, 1), high)
            low = jnp.where(mine, roll(source[index], 3 * index, 1), low)
        even_out[row : row + ROWS] = jnp.where(odd_y == 0, high, low)
        odd_out[row : row + ROWS] = jnp.where(odd_y == 0, low, high)


def median(one, two, three):
    return jnp.maximum(jnp.minimum(one, two), jnp.minimum(jnp.maximum(one, two), three))


def face_above(before, here, after, beyond):
    value = (7.0 / 12.0) * (here + after) - (1.0 / 12.0) * (before + beyond)
    return median(here, after, value)


def limited(here, face_low, face_high):
    thrice = 3.0 * here
    return (
        median(here, face_low, thrice - (face_high + face_high)),
        median(here, face_high, thrice - (face_low + face_low)),
    )


def sound_of(state):
    push = ADIABATIC * state[4]
    return push * lax.rsqrt(push * state[0])


def face_flux(left, right, normal):
    left_u, right_u = left[1 + normal], right[1 + normal]
    left_sound, right_sound = sound_of(left), sound_of(right)
    slow = jnp.minimum(jnp.minimum(left_u - left_sound, right_u - right_sound), 0.0)
    fast = jnp.maximum(jnp.maximum(left_u + left_sound, right_u + right_sound), 0.0)
    share = 1.0 / (fast - slow)
    left_part = fast * share
    right_part = -slow * share
    left_lead = left_u - slow
    right_lead = right_u - fast
    left_mass = left_part * left_lead * left[0]
    right_mass = right_part * right_lead * right[0]
    left_square = left[1] * left[1] + left[2] * left[2] + left[3] * left[3]
    right_square = right[1] * right[1] + right[2] * right[2] + right[3] * right[3]
    flux = [left_mass + right_mass]
    for k in (1, 2, 3):
        flux.append(left_mass * left[k] + right_mass * right[k])
    left_push = left_part * left[4]
    right_push = right_part * right[4]
    flux[1 + normal] = flux[1 + normal] + (left_push + right_push)
    flux.append(
        0.5 * (left_mass * left_square + right_mass * right_square)
        + left_push * (1.5 * left_lead + left_u)
        + right_push * (1.5 * right_lead + right_u)
    )
    flux.append(left_mass * left[5] + right_mass * right[5])
    return flux


def z_fluxes(planes):
    lower, upper = [], []
    for k in range(6):
        column = [planes[j][k] for j in range(9)]
        faces = [face_above(*column[j : j + 4]) for j in range(6)]
        cells = [limited(column[j + 2], faces[j], faces[j + 1]) for j in range(5)]
        lower.append([cells[j][1] for j in range(4)])
        upper.append([cells[j + 1][0] for j in range(4)])
    return [
        face_flux([lower[k][j] for k in range(6)], [upper[k][j] for k in range(6)], 2)
        for j in range(4)
    ]


def edge_primitives(fields):
    density = fields[0]
    inverse = 1.0 / density
    kinetic = 0.5 * inverse * (fields[1] ** 2 + fields[2] ** 2 + fields[3] ** 2)
    return [
        density,
        fields[1] * inverse,
        fields[2] * inverse,
        fields[3] * inverse,
        (ADIABATIC - 1.0) * (fields[4] - kinetic),
        fields[5] * inverse,
    ]


def shift_pair(main, rim, step):
    lane = lane_index(main.shape)
    main_rolled = roll(main, -step, 1)
    rim_rolled = roll(rim, -step, 1)
    inside = lane < LANES - step if step > 0 else lane >= -step
    return (
        jnp.where(inside, main_rolled, rim_rolled),
        jnp.where(inside, rim_rolled, main_rolled),
    )


def y_differences(main, rim):
    lows, highs = ([], []), ([], [])
    spread = None
    for k in range(6):
        here = (main[k], rim[k])
        before = shift_pair(*here, -1)
        after = shift_pair(*here, 1)
        beyond = shift_pair(*here, 2)
        faces = [face_above(before[j], here[j], after[j], beyond[j]) for j in range(2)]
        below = shift_pair(*faces, -1)
        cells = [limited(here[j], below[j], faces[j]) for j in range(2)]
        nexts = shift_pair(cells[0][0], cells[1][0], 1)
        for j in range(2):
            lows[j].append(cells[j][1])
            highs[j].append(nexts[j])
        if k == 2:
            spread = [0.5 * (after[j] - before[j]) for j in range(2)]
    fluxes = [face_flux(lows[j], highs[j], 1) for j in range(2)]
    differences = ([], [])
    for k in range(6):
        below = shift_pair(fluxes[0][k], fluxes[1][k], -1)
        for j in range(2):
            differences[j].append(fluxes[j][k] - below[j])
    return differences, spread


CHUNKS = (4, 12, 20)


def x_sweep(prims, low_ref, high_ref, face_ref, flux_ref):
    for row in CHUNKS:
        for k in range(6):
            before, here, after, beyond = [
                prims[k, pl.ds(row + s, 8), :] for s in (-1, 0, 1, 2)
            ]
            if row == CHUNKS[0]:
                below = face_above(prims[k, pl.ds(row - 2, 8), :], before, here, after)
            above = face_above(before, here, after, beyond)
            face_ref[k, pl.ds(row, 8), :] = above
            if row != CHUNKS[0]:
                below = face_ref[k, pl.ds(row - 1, 8), :]
            low_ref[k, pl.ds(row, 8), :], high_ref[k, pl.ds(row, 8), :] = limited(
                here, below, above
            )
    for row in CHUNKS:
        left = [high_ref[k, pl.ds(row, 8), :] for k in range(6)]
        right = [low_ref[k, pl.ds(row + 1, 8), :] for k in range(6)]
        flux = face_flux(left, right, 0)
        for k in range(6):
            flux_ref[k, pl.ds(row, 8), :] = flux[k]


def clear_ends(low_ref, flux_ref):
    for k in range(6):
        low_ref[k, pl.ds(28, 4), :] = jnp.ones((4, LANES), F32)
        flux_ref[k, pl.ds(0, 4), :] = jnp.zeros((4, LANES), F32)


def third_kernel(
    state, switch, edges, forcing, pair_in, odd_in, even_in, odd_y_in,
    fields, force, tend, outer, prims, planes, low_ref, high_ref, face_ref, flux_ref, strip_ref,
):
    odd_x, odd_y = parities()
    strip_ref[0] = jnp.where(odd_y == 0, even_in[...], odd_y_in[...])
    strip_ref[1] = jnp.where(odd_y == 0, odd_y_in[...], even_in[...])
    clear_ends(low_ref, flux_ref)
    lane = lane_index((EXT, LANES))
    edge_lane = lane[0:ROWS]

    def field_tiles(index, block):
        fields[0, index] = rows_around(odd_x, pair_in, odd_in, index, block)
        fields[1, index] = jnp.where(
            lane < 64,
            turned(strip_ref[0, 0:EXT], -6 * index),
            turned(strip_ref[1, 0:EXT], 122 - 6 * index),
        )

    def rim_tile(row, index):
        return jnp.where(
            edge_lane < 64,
            turned(strip_ref[0, row : row + ROWS], -3 * index),
            turned(strip_ref[1, row : row + ROWS], 125 - 3 * index),
        )

    @functools.partial(each, 6)
    def _(field):
        for plane in range(3):
            index = 3 * field + plane
            field_tiles(index, state[index])

    for plane in range(3):
        field_tiles(18 + plane, switch[plane].astype(F32))

    @functools.partial(each, 3)
    def _(part):
        for k in range(3):
            index = 3 * part + k
            force[0, index] = rows_around_half(
                odd_x, pair_in, odd_in, EDGES + index, forcing[index]
            )
            force[1, index, 0:8] = jnp.zeros((8, LANES), F32)
            force[1, index, 8:24] = rim_tile(EXT + ROWS, index)
            force[1, index, 24:32] = jnp.zeros((8, LANES), F32)

    @functools.partial(each, 6)
    def _(step):
        tile, plane = step // 3, step % 3
        values = [fields[tile, 3 * k + plane] for k in range(7)]
        density = values[0]
        inverse = 1.0 / density
        kinetic = 0.5 * inverse * (values[1] ** 2 + values[2] ** 2 + values[3] ** 2)
        heat = jnp.where(values[6] == 1.0, values[5], values[4] - kinetic)
        prims[tile, plane, 0] = density
        for k in (1, 2, 3):
            prims[tile, plane, k] = values[k] * inverse
        prims[tile, plane, 4] = (ADIABATIC - 1.0) * heat
        prims[tile, plane, 5] = values[5] * inverse

    @functools.partial(each, 6)
    def _(step):
        first = 18 * (step // 3) + step % 3
        places = [first + 3 * k for k in range(6)]
        values = edge_primitives(
            [rows_around_half(odd_x, pair_in, odd_in, k, edges[k]) for k in places]
        )
        for k in range(6):
            planes[0, step, k] = values[k]
            outer[step, k] = values[k][8:24]
        values = edge_primitives([rim_tile(EXT, k) for k in places])
        for k in range(6):
            planes[1, step, k, 0:8] = jnp.ones((8, LANES), F32)
            planes[1, step, k, 8:24] = values[k]
            planes[1, step, k, 24:32] = jnp.ones((8, LANES), F32)

    @functools.partial(each, 3)
    def _(plane):
        for row in CHUNKS:
            rows = pl.ds(row, 8)
            both = [[prims[tile, plane, k, rows, :] for k in range(6)] for tile in range(2)]
            differences, spread = y_differences(*both)
            for tile in range(2):
                for k in range(5):
                    tend[tile, 3 * k + plane, rows, :] = -differences[tile][k]
                tend[tile, 15 + plane, rows, :] = (
                    -differences[tile][5] - both[tile][4] * spread[tile]
                )

    @functools.partial(each, 6)
    def _(step):
        tile, plane = step // 3, step % 3
        x_sweep(prims.at[tile, plane], low_ref, high_ref, face_ref, flux_ref)
        for row in CHUNKS:
            rows = pl.ds(row, 8)
            for k in range(6):
                difference = flux_ref[k, rows, :] - flux_ref[k, pl.ds(row - 1, 8), :]
                if k == 5:
                    before = prims[tile, plane, 1, pl.ds(row - 1, 8), :]
                    after = prims[tile, plane, 1, pl.ds(row + 1, 8), :]
                    spread = 0.5 * (after - before)
                    difference = difference + prims[tile, plane, 4, rows, :] * spread
                tend[tile, 3 * k + plane, rows, :] -= difference

    @functools.partial(each, 2)
    def _(tile):
        for row in CHUNKS:
            rows = pl.ds(row, 8)
            column = (
                [[planes[tile, p, k, rows, :] for k in range(6)] for p in range(3)]
                + [[prims[tile, p, k, rows, :] for k in range(6)] for p in range(3)]
                + [[planes[tile, 3 + p, k, rows, :] for k in range(6)] for p in range(3)]
            )
            flux = z_fluxes(column)
            for plane in range(3):
                for k in range(6):
                    difference = flux[plane + 1][k] - flux[plane][k]
                    if k == 5:
                        spread = 0.5 * (column[plane + 4][3] - column[plane + 2][3])
                        difference = difference + column[plane + 3][4] * spread
                    tend[tile, 3 * k + plane, rows, :] -= difference


def fourth_kernel(
    cells, totals, fields, force, tend, outer_prims, out,
    updated, section, prims, low_ref, high_ref, face_ref, flux_ref, sent,
):
    peak = jnp.max(totals[:, 0, :], axis=0, keepdims=True)
    power = jnp.sum(totals[:, 1, :], axis=0, keepdims=True)
    time_step = CFL_NUMBER / peak
    scale = jnp.sqrt(INJECTION / (0.5 * time_step * (power / cells + 1e-06)))
    clear_ends(low_ref, flux_ref)

    def forced(values, drive, tendency):
        result = list(tendency)
        for k in (1, 2, 3):
            result[k] = result[k] + scale * values[0] * drive[k - 1]
        result[4] = result[4] + scale * (
            values[1] * drive[0] + values[2] * drive[1] + values[3] * drive[2]
        )
        return result

    def settle(values, switch, inverse):
        kinetic = 0.5 * inverse * (values[1] ** 2 + values[2] ** 2 + values[3] ** 2)
        values[5] = jnp.where(switch == 0.0, values[4] - kinetic, values[5])

    def advance(tile, plane, chunks):
        for row in chunks:
            rows = pl.ds(row, 8)
            values = [fields[tile, 3 * k + plane, rows, :] for k in range(7)]
            drive = [force[tile, 3 * k + plane, rows, :] for k in range(3)]
            rate = forced(values, drive, [tend[tile, 3 * k + plane, rows, :] for k in range(6)])
            stage = [values[k] + time_step * rate[k] for k in range(6)]
            inverse = 1.0 / stage[0]
            settle(stage, values[6], inverse)
            if tile == 0:
                for k in range(6):
                    section[plane, k, rows, :] = stage[k]
            prims[tile, plane, 0, rows, :] = stage[0]
            for k in (1, 2, 3):
                prims[tile, plane, k, rows, :] = stage[k] * inverse
            prims[tile, plane, 4, rows, :] = (ADIABATIC - 1.0) * stage[5]
            prims[tile, plane, 5, rows, :] = stage[5] * inverse

    @functools.partial(each, 3)
    def _(plane):
        advance(0, plane, CHUNKS)
        advance(1, plane, (8, 16))

    @functools.partial(each, 2)
    def _(step):
        inner = pl.ds(pl.multiple_of(8 * step, 8), 8)
        rows = pl.ds(pl.multiple_of(8 * step + 8, 8), 8)
        outer = [[outer_prims[p, k, inner, :] for k in range(6)] for p in range(6)]
        column = (
            outer[0:3] + [[prims[0, p, k, rows, :] for k in range(6)] for p in range(3)] + outer[3:6]
        )
        flux = z_fluxes(column)
        for plane in range(3):
            for k in range(6):
                difference = flux[plane + 1][k] - flux[plane][k]
                if k == 5:
                    spread = 0.5 * (column[plane + 4][3] - column[plane + 2][3])
                    difference = difference + column[plane + 3][4] * spread
                updated[k, plane, inner, :] = -difference

    @functools.partial(each, 3)
    def _(plane):
        x_sweep(prims.at[0, plane], low_ref, high_ref, face_ref, flux_ref)
        for row in (8, 16):
            rows = pl.ds(row, 8)
            inner = pl.ds(row - 8, 8)
            both = [[prims[tile, plane, k, rows, :] for k in range(6)] for tile in range(2)]
            differences, spread = y_differences(*both)
            before = prims[0, plane, 1, pl.ds(row - 1, 8), :]
            after = prims[0, plane, 1, pl.ds(row + 1, 8), :]
            spread = spread[0] + 0.5 * (after - before)
            rate = []
            for k in range(6):
                across = flux_ref[k, rows, :] - flux_ref[k, pl.ds(row - 1, 8), :]
                rate.append(updated[k, plane, inner, :] - differences[0][k] - across)
            rate[5] = rate[5] - both[0][4] * spread
            stage = [section[plane, k, rows, :] for k in range(6)]
            drive = [force[0, 3 * k + plane, rows, :] for k in range(3)]
            rate = forced(stage, drive, rate)
            values = [fields[0, 3 * k + plane, rows, :] for k in range(7)]
            result = [
                0.5 * values[k] + 0.5 * (stage[k] + time_step * rate[k]) for k in range(6)
            ]
            settle(result, values[6], 1.0 / result[0])
            for k in range(6):
                updated[k, plane, inner, :] = result[k]
        pltpu.make_async_copy(updated.at[:, plane], out.at[:, plane], sent.at[plane]).start()

    for plane in range(3):
        pltpu.make_async_copy(updated.at[:, plane], out.at[:, plane], sent.at[plane]).wait()


def shape(*sizes):
    return jax.ShapeDtypeStruct(sizes, F32)


def vmem_specs(count):
    return [pl.BlockSpec(memory_space=pltpu.VMEM)] * count


def call(kernel, name, outs, arrays, scratch=(), cost=0, out_space=pltpu.VMEM):
    single = not isinstance(outs, tuple)
    out_spec = pl.BlockSpec(memory_space=out_space)
    return pl.pallas_call(
        kernel,
        out_shape=outs,
        in_specs=vmem_specs(len(arrays)),
        out_specs=out_spec if single else (out_spec,) * len(outs),
        scratch_shapes=list(scratch),
        compiler_params=pltpu.CompilerParams(vmem_limit_bytes=VMEM_LIMIT),
        cost_estimate=pl.CostEstimate(flops=cost, bytes_accessed=cost, transcendentals=0),
        name=name,
    )(*arrays)


def pairs(count, begin):
    table = []
    for first in range(begin, begin + count, 2):
        low, high = first % count, (first + 1) % count
        table += [(low, high), (high, low)]
    return table


def spread_over(rows, after, axes):
    return pl.pallas_call(
        spread_kernel,
        out_shape=shape(lax.axis_size(axes), 2, LANES),
        in_specs=[*vmem_specs(1), pl.BlockSpec(memory_space=pl.ANY)],
        out_specs=vmem_specs(1)[0],
        compiler_params=pltpu.CompilerParams(vmem_limit_bytes=VMEM_LIMIT),
        name="spread",
    )(rows, after)


def exchanged(spread, axes):
    return lax.all_to_all(spread, axes, 0, 0, tiled=True)


GX = ("zl", "core")
GY = ("y", "zh", "x")


def local(fluid_state, switch, z_edges, forcing):
    count_x = lax.axis_size(GX)
    count_y = lax.axis_size(GY)
    cells = 3.0 * ROWS * LANES * count_x * count_y
    tile = (8, LANES)
    block = (ROWS, LANES)
    inputs = (
        fluid_state.reshape(18, *block),
        switch,
        z_edges.reshape(EDGES, *block),
        forcing.reshape(FORCES, *block),
    )
    pair_out, odd_out, *arrays = pl.pallas_call(
        first_kernel,
        out_shape=(
            shape(PAYLOAD + 1, *tile),
            shape(PAYLOAD, *tile),
            *(jax.ShapeDtypeStruct(values.shape, values.dtype) for values in inputs),
        ),
        in_specs=[
            *([pl.BlockSpec(memory_space=pltpu.HBM)] * 4),
        ],
        out_specs=tuple(vmem_specs(6)),
        scratch_shapes=[pltpu.SemaphoreType.DMA((4,))],
        compiler_params=pltpu.CompilerParams(vmem_limit_bytes=VMEM_LIMIT),
        name="first",
    )(*(pltpu.with_memory_space_constraint(values, pltpu.HBM) for values in inputs))
    pair_in = lax.all_gather(pair_out, "core")
    rows = pair_in[:, PAYLOAD, 0:2]
    spread = spread_over(rows, rows, ("y", "x"))
    odd_out, spread = lax.optimization_barrier((odd_out, spread))
    odd_in = lax.ppermute(odd_out, GX, pairs(count_x, 1))
    totals = exchanged(spread, ("y", "x"))
    strips = call(
        second_kernel,
        "second",
        (shape(EXT + 2 * ROWS, LANES), shape(EXT + 2 * ROWS, LANES)),
        (*arrays, pair_in, odd_in),
        cost=4_000_000,
    )
    even_in = lax.ppermute(strips[0], GY, pairs(count_y, 0))
    odd_y_in = lax.ppermute(strips[1], GY, pairs(count_y, 1))
    totals = exchanged(spread_over(totals, even_in, ("zh", "zl")), ("zh", "zl"))
    extended = (EXT, LANES)
    work = [pltpu.VMEM((6, *extended), F32) for _ in range(4)]
    fields, force, tend, outer = call(
        third_kernel,
        "third",
        (
            shape(2, FIELDS, *extended),
            shape(2, FORCES, *extended),
            shape(2, 18, *extended),
            shape(6, 6, ROWS, LANES),
        ),
        (*arrays, pair_in, odd_in, even_in, odd_y_in),
        [
            pltpu.VMEM((2, 3, 6, *extended), F32),
            pltpu.VMEM((2, 6, 6, *extended), F32),
            *work,
            pltpu.VMEM((2, EXT + 2 * ROWS, LANES), F32),
        ],
        cost=60_000_000,
    )
    return call(
        functools.partial(fourth_kernel, cells),
        "fourth",
        shape(6, 3, ROWS, LANES),
        (totals, fields, force, tend, outer),
        [
            pltpu.VMEM((6, 3, ROWS, LANES), F32),
            pltpu.VMEM((3, 6, *extended), F32),
            pltpu.VMEM((2, 3, 6, *extended), F32),
            *work,
            pltpu.SemaphoreType.DMA((3,)),
        ],
        cost=8_000_000,
        out_space=pltpu.HBM,
    )


def solution(mesh):
    count_x, count_y = mesh.devices.shape
    count_z = 2 if count_y % 8 == 0 else 1
    parts = (count_x // 2, 2, count_y // (4 * count_z), count_z, 4)
    split = Mesh(mesh.devices.reshape(parts), (*GX, *GY))
    return jax.shard_map(
        local,
        mesh=split,
        in_specs=(
            P(None, None, GX, GY),
            P(None, GX, GY),
            P(None, None, None, GX, GY),
            P(None, None, GX, GY),
        ),
        out_specs=P(None, None, GX, GY),
        check_vma=False,
    )
```

```python
import functools

import jax
import jax.numpy as jnp
from jax import lax
from jax.experimental import pallas as pl
from jax.experimental.pallas import tpu as pltpu
from jax.sharding import Mesh
from jax.sharding import PartitionSpec as P

ADIABATIC = 5.0 / 3.0
CFL_NUMBER = 0.4
INJECTION = 0.04
LANES = 128
ROWS = 16
EXT = 32
FIELDS = 21
EDGES = 36
FORCES = 9
X_TILES = FIELDS + EDGES + FORCES
VMEM_LIMIT = 16 * 1024 * 1024
F32 = jnp.float32


def lane_index(shape):
    return lax.broadcasted_iota(jnp.int32, shape, len(shape) - 1)


def roll(values, shift, axis):
    size = values.shape[axis]
    shift = shift % size
    return values if shift == 0 else pltpu.roll(values, shift, axis)


def parities():
    return lax.axis_index("core"), lax.rem(lax.axis_index("x"), 2)


def each(count, body):
    def step(index, carry):
        body(index)
        return carry

    lax.fori_loop(0, count, step, 0)


def x_place(refs, index):
    state, switch, edges, forcing = refs
    if index < 18:
        return lambda rows: state[index, rows, :]
    index -= 18
    if index < 3:
        return lambda rows: switch[index, rows, :].astype(F32)
    index -= 3
    if index < EDGES:
        return lambda rows: edges[index, rows, :]
    index -= EDGES
    return lambda rows: forcing[index, rows, :]


def first_kernel(
    state_in, switch_in, edges_in, forcing_in,
    pair_out, odd_out, state, switch, edges, forcing, arrived,
):
    refs = (state, switch, edges, forcing)
    copies = [
        pltpu.make_async_copy(source, target, arrived.at[k])
        for k, (source, target) in enumerate(
            zip((state_in, switch_in, edges_in, forcing_in), refs, strict=True)
        )
    ]
    for k in (2, 0, 3, 1):
        copies[k].start()
    odd, _ = parities()
    near = pl.multiple_of(8 * (1 - odd), 8)
    far = pl.multiple_of(8 * odd, 8)
    for k in (0, 1, 3):
        copies[k].wait()
    peak = None
    total = None
    for plane in range(3):
        fields = [state[3 * k + plane] for k in range(6)]
        density = fields[0]
        inverse = 1.0 / density
        kinetic = 0.5 * inverse * (fields[1] ** 2 + fields[2] ** 2 + fields[3] ** 2)
        heat = jnp.where(switch[plane] == 1, fields[5], fields[4] - kinetic)
        sound = jnp.sqrt(ADIABATIC * (ADIABATIC - 1.0) * heat * inverse)
        speed = (
            jnp.abs(fields[1]) + jnp.abs(fields[2]) + jnp.abs(fields[3])
        ) * inverse + 3.0 * sound
        drive = [forcing[3 * k + plane] for k in range(3)]
        power = density * (drive[0] ** 2 + drive[1] ** 2 + drive[2] ** 2)
        peak = speed if peak is None else jnp.maximum(peak, speed)
        total = power if total is None else total + power
    row = lax.broadcasted_iota(jnp.int32, (8, LANES), 0)
    pair_out[X_TILES] = jnp.where(row == 0, jnp.max(peak), jnp.sum(total))
    copies[2].wait()
    for index in range(X_TILES):
        tile = x_place(refs, index)
        pair_out[index] = tile(pl.ds(near, 8))
        odd_out[index] = tile(pl.ds(far, 8))


def spread_kernel(rows, after, out):
    peak = jnp.max(rows[:, 0, :], axis=0, keepdims=True)
    total = jnp.sum(rows[:, 1, :], axis=0, keepdims=True)
    joined = jnp.concatenate([peak, total], axis=0)
    out[...] = jnp.broadcast_to(joined[None], out.shape)


def rows_around(odd_x, pair_in, odd_in, index, block):
    from_pair = pair_in[1 - odd_x, index]
    from_odd = odd_in[index]
    below = jnp.where(odd_x == 0, from_odd, from_pair)
    above = jnp.where(odd_x == 0, from_pair, from_odd)
    return jnp.concatenate([below, block, above], axis=0)


def turned(values, shift):
    return pltpu.roll(values, lax.rem(shift + LANES, LANES), 1)


def second_kernel(state, switch, edges, forcing, pair_in, odd_in, even_out, odd_out):
    odd_x, odd_y = parities()
    lane = lane_index((EXT, LANES))
    high = jnp.zeros((EXT, LANES), F32)
    low = jnp.zeros((EXT, LANES), F32)
    for index in range(FIELDS):
        block = x_place((state, switch, edges, forcing), index)(slice(0, ROWS))
        column = rows_around(odd_x, pair_in, odd_in, index, block)
        mine = (lane >= 6 * index) & (lane < 6 * index + 6)
        high = jnp.where(mine, roll(column, 6 * index - 122, 1), high)
        low = jnp.where(mine, roll(column, 6 * index, 1), low)
    even_out[0:EXT] = jnp.where(odd_y == 0, high, low)
    odd_out[0:EXT] = jnp.where(odd_y == 0, low, high)
    lane = lane[0:ROWS]
    for source, count, row in ((edges, EDGES, EXT), (forcing, FORCES, EXT + ROWS)):
        high = jnp.zeros((ROWS, LANES), F32)
        low = jnp.zeros((ROWS, LANES), F32)
        for index in range(count):
            mine = (lane >= 3 * index) & (lane < 3 * index + 3)
            high = jnp.where(mine, roll(source[index], 3 * index - 125, 1), high)
            low = jnp.where(mine, roll(source[index], 3 * index, 1), low)
        even_out[row : row + ROWS] = jnp.where(odd_y == 0, high, low)
        odd_out[row : row + ROWS] = jnp.where(odd_y == 0, low, high)


def median(one, two, three):
    return jnp.maximum(jnp.minimum(one, two), jnp.minimum(jnp.maximum(one, two), three))


def face_above(before, here, after, beyond):
    value = (7.0 / 12.0) * (here + after) - (1.0 / 12.0) * (before + beyond)
    return median(here, after, value)


def limited(here, face_low, face_high):
    thrice = 3.0 * here
    return (
        median(here, face_low, thrice - (face_high + face_high)),
        median(here, face_high, thrice - (face_low + face_low)),
    )


def sound_of(state):
    push = ADIABATIC * state[4]
    return push * lax.rsqrt(push * state[0])


def face_flux(left, right, normal):
    left_u, right_u = left[1 + normal], right[1 + normal]
    left_sound, right_sound = sound_of(left), sound_of(right)
    slow = jnp.minimum(jnp.minimum(left_u - left_sound, right_u - right_sound), 0.0)
    fast = jnp.maximum(jnp.maximum(left_u + left_sound, right_u + right_sound), 0.0)
    share = 1.0 / (fast - slow)
    left_part = fast * share
    right_part = -slow * share
    left_lead = left_u - slow
    right_lead = right_u - fast
    left_mass = left_part * left_lead * left[0]
    right_mass = right_part * right_lead * right[0]
    left_square = left[1] * left[1] + left[2] * left[2] + left[3] * left[3]
    right_square = right[1] * right[1] + right[2] * right[2] + right[3] * right[3]
    flux = [left_mass + right_mass]
    for k in (1, 2, 3):
        flux.append(left_mass * left[k] + right_mass * right[k])
    left_push = left_part * left[4]
    right_push = right_part * right[4]
    flux[1 + normal] = flux[1 + normal] + (left_push + right_push)
    flux.append(
        0.5 * (left_mass * left_square + right_mass * right_square)
        + left_push * (1.5 * left_lead + left_u)
        + right_push * (1.5 * right_lead + right_u)
    )
    flux.append(left_mass * left[5] + right_mass * right[5])
    return flux


def z_fluxes(planes):
    lower, upper = [], []
    for k in range(6):
        column = [planes[j][k] for j in range(9)]
        faces = [face_above(*column[j : j + 4]) for j in range(6)]
        cells = [limited(column[j + 2], faces[j], faces[j + 1]) for j in range(5)]
        lower.append([cells[j][1] for j in range(4)])
        upper.append([cells[j + 1][0] for j in range(4)])
    return [
        face_flux([lower[k][j] for k in range(6)], [upper[k][j] for k in range(6)], 2)
        for j in range(4)
    ]


def edge_primitives(fields):
    density = fields[0]
    inverse = 1.0 / density
    kinetic = 0.5 * inverse * (fields[1] ** 2 + fields[2] ** 2 + fields[3] ** 2)
    return [
        density,
        fields[1] * inverse,
        fields[2] * inverse,
        fields[3] * inverse,
        (ADIABATIC - 1.0) * (fields[4] - kinetic),
        fields[5] * inverse,
    ]


def shift_pair(main, rim, step):
    lane = lane_index(main.shape)
    main_rolled = roll(main, -step, 1)
    rim_rolled = roll(rim, -step, 1)
    inside = lane < LANES - step if step > 0 else lane >= -step
    return (
        jnp.where(inside, main_rolled, rim_rolled),
        jnp.where(inside, rim_rolled, main_rolled),
    )


def y_differences(main, rim):
    lows, highs = ([], []), ([], [])
    spread = None
    for k in range(6):
        here = (main[k], rim[k])
        before = shift_pair(*here, -1)
        after = shift_pair(*here, 1)
        beyond = shift_pair(*here, 2)
        faces = [face_above(before[j], here[j], after[j], beyond[j]) for j in range(2)]
        below = shift_pair(*faces, -1)
        cells = [limited(here[j], below[j], faces[j]) for j in range(2)]
        nexts = shift_pair(cells[0][0], cells[1][0], 1)
        for j in range(2):
            lows[j].append(cells[j][1])
            highs[j].append(nexts[j])
        if k == 2:
            spread = [0.5 * (after[j] - before[j]) for j in range(2)]
    fluxes = [face_flux(lows[j], highs[j], 1) for j in range(2)]
    differences = ([], [])
    for k in range(6):
        below = shift_pair(fluxes[0][k], fluxes[1][k], -1)
        for j in range(2):
            differences[j].append(fluxes[j][k] - below[j])
    return differences, spread


CHUNKS = (4, 12, 20)


def x_sweep(prims, low_ref, high_ref, face_ref, flux_ref):
    for row in CHUNKS:
        for k in range(6):
            before, here, after, beyond = [
                prims[k, pl.ds(row + s, 8), :] for s in (-1, 0, 1, 2)
            ]
            if row == CHUNKS[0]:
                below = face_above(prims[k, pl.ds(row - 2, 8), :], before, here, after)
            above = face_above(before, here, after, beyond)
            face_ref[k, pl.ds(row, 8), :] = above
            if row != CHUNKS[0]:
                below = face_ref[k, pl.ds(row - 1, 8), :]
            low_ref[k, pl.ds(row, 8), :], high_ref[k, pl.ds(row, 8), :] = limited(
                here, below, above
            )
    for row in CHUNKS:
        left = [high_ref[k, pl.ds(row, 8), :] for k in range(6)]
        right = [low_ref[k, pl.ds(row + 1, 8), :] for k in range(6)]
        flux = face_flux(left, right, 0)
        for k in range(6):
            flux_ref[k, pl.ds(row, 8), :] = flux[k]


def clear_ends(low_ref, flux_ref):
    for k in range(6):
        low_ref[k, pl.ds(28, 4), :] = jnp.ones((4, LANES), F32)
        flux_ref[k, pl.ds(0, 4), :] = jnp.zeros((4, LANES), F32)


def third_kernel(
    state, switch, edges, forcing, pair_in, odd_in, even_in, odd_y_in,
    fields, force, push, tend, outer, prims, planes, low_ref, high_ref, face_ref, flux_ref, strip_ref,
):
    odd_x, odd_y = parities()
    strip_ref[0] = jnp.where(odd_y == 0, even_in[...], odd_y_in[...])
    strip_ref[1] = jnp.where(odd_y == 0, odd_y_in[...], even_in[...])
    clear_ends(low_ref, flux_ref)
    lane = lane_index((EXT, LANES))
    edge_lane = lane[0:ROWS]

    def field_tiles(index, block):
        fields[0, index] = rows_around(odd_x, pair_in, odd_in, index, block)
        fields[1, index] = jnp.where(
            lane < 64,
            turned(strip_ref[0, 0:EXT], -6 * index),
            turned(strip_ref[1, 0:EXT], 122 - 6 * index),
        )

    def rim_tile(row, index):
        return jnp.where(
            edge_lane < 64,
            turned(strip_ref[0, row : row + ROWS], -3 * index),
            turned(strip_ref[1, row : row + ROWS], 125 - 3 * index),
        )

    @functools.partial(each, 6)
    def _(field):
        for plane in range(3):
            index = 3 * field + plane
            field_tiles(index, state[index])

    for plane in range(3):
        field_tiles(18 + plane, switch[plane].astype(F32))

    @functools.partial(each, 3)
    def _(part):
        for k in range(3):
            index = 3 * part + k
            force[0, index] = rows_around(
                odd_x, pair_in, odd_in, FIELDS + EDGES + index, forcing[index]
            )
            force[1, index, 0:8] = jnp.zeros((8, LANES), F32)
            force[1, index, 8:24] = rim_tile(EXT + ROWS, index)
            force[1, index, 24:32] = jnp.zeros((8, LANES), F32)

    @functools.partial(each, 6)
    def _(step):
        tile, plane = step // 3, step % 3
        values = [fields[tile, 3 * k + plane] for k in range(7)]
        density = values[0]
        inverse = 1.0 / density
        kinetic = 0.5 * inverse * (values[1] ** 2 + values[2] ** 2 + values[3] ** 2)
        heat = jnp.where(values[6] == 1.0, values[5], values[4] - kinetic)
        prims[tile, plane, 0] = density
        for k in (1, 2, 3):
            prims[tile, plane, k] = values[k] * inverse
        drive = [force[tile, 3 * k + plane] for k in range(3)]
        for k in range(3):
            push[tile, 3 * k + plane] = density * drive[k]
        push[tile, 9 + plane] = (
            values[1] * drive[0] + values[2] * drive[1] + values[3] * drive[2]
        )
        prims[tile, plane, 4] = (ADIABATIC - 1.0) * heat
        prims[tile, plane, 5] = values[5] * inverse

    @functools.partial(each, 6)
    def _(step):
        first = 18 * (step // 3) + step % 3
        places = [first + 3 * k for k in range(6)]
        values = edge_primitives(
            [rows_around(odd_x, pair_in, odd_in, FIELDS + k, edges[k]) for k in places]
        )
        for k in range(6):
            planes[0, step, k] = values[k]
            outer[step, k] = values[k][8:24]
        values = edge_primitives([rim_tile(EXT, k) for k in places])
        for k in range(6):
            planes[1, step, k, 0:8] = jnp.ones((8, LANES), F32)
            planes[1, step, k, 8:24] = values[k]
            planes[1, step, k, 24:32] = jnp.ones((8, LANES), F32)

    @functools.partial(each, 3)
    def _(plane):
        for row in CHUNKS:
            rows = pl.ds(row, 8)
            both = [[prims[tile, plane, k, rows, :] for k in range(6)] for tile in range(2)]
            differences, spread = y_differences(*both)
            for tile in range(2):
                for k in range(5):
                    tend[tile, 3 * k + plane, rows, :] = -differences[tile][k]
                tend[tile, 15 + plane, rows, :] = (
                    -differences[tile][5] - both[tile][4] * spread[tile]
                )

    @functools.partial(each, 6)
    def _(step):
        tile, plane = step // 3, step % 3
        x_sweep(prims.at[tile, plane], low_ref, high_ref, face_ref, flux_ref)
        for row in CHUNKS:
            rows = pl.ds(row, 8)
            for k in range(6):
                difference = flux_ref[k, rows, :] - flux_ref[k, pl.ds(row - 1, 8), :]
                if k == 5:
                    before = prims[tile, plane, 1, pl.ds(row - 1, 8), :]
                    after = prims[tile, plane, 1, pl.ds(row + 1, 8), :]
                    spread = 0.5 * (after - before)
                    difference = difference + prims[tile, plane, 4, rows, :] * spread
                tend[tile, 3 * k + plane, rows, :] -= difference

    @functools.partial(each, 2)
    def _(tile):
        for row in CHUNKS:
            rows = pl.ds(row, 8)
            column = (
                [[planes[tile, p, k, rows, :] for k in range(6)] for p in range(3)]
                + [[prims[tile, p, k, rows, :] for k in range(6)] for p in range(3)]
                + [[planes[tile, 3 + p, k, rows, :] for k in range(6)] for p in range(3)]
            )
            flux = z_fluxes(column)
            for plane in range(3):
                for k in range(6):
                    difference = flux[plane + 1][k] - flux[plane][k]
                    if k == 5:
                        spread = 0.5 * (column[plane + 4][3] - column[plane + 2][3])
                        difference = difference + column[plane + 3][4] * spread
                    tend[tile, 3 * k + plane, rows, :] -= difference


def fourth_kernel(
    cells, totals, fields, force, push, tend, outer_prims, out,
    updated, section, prims, low_ref, high_ref, face_ref, flux_ref, sent,
):
    peak = jnp.max(totals[:, 0, :], axis=0, keepdims=True)
    power = jnp.sum(totals[:, 1, :], axis=0, keepdims=True)
    time_step = CFL_NUMBER / peak
    scale = jnp.sqrt(INJECTION / (0.5 * time_step * (power / cells + 1e-06)))
    clear_ends(low_ref, flux_ref)

    def forced(values, drive, tendency):
        result = list(tendency)
        for k in (1, 2, 3):
            result[k] = result[k] + scale * values[0] * drive[k - 1]
        result[4] = result[4] + scale * (
            values[1] * drive[0] + values[2] * drive[1] + values[3] * drive[2]
        )
        return result

    def settle(values, switch, inverse):
        kinetic = 0.5 * inverse * (values[1] ** 2 + values[2] ** 2 + values[3] ** 2)
        values[5] = jnp.where(switch == 0.0, values[4] - kinetic, values[5])

    def advance(tile, plane, chunks):
        for row in chunks:
            rows = pl.ds(row, 8)
            values = [fields[tile, 3 * k + plane, rows, :] for k in range(7)]
            rate = [tend[tile, 3 * k + plane, rows, :] for k in range(6)]
            for k in range(4):
                rate[1 + k] = rate[1 + k] + scale * push[tile, 3 * k + plane, rows, :]
            stage = [values[k] + time_step * rate[k] for k in range(6)]
            inverse = 1.0 / stage[0]
            settle(stage, values[6], inverse)
            if tile == 0:
                for k in range(6):
                    section[plane, k, rows, :] = stage[k]
            prims[tile, plane, 0, rows, :] = stage[0]
            for k in (1, 2, 3):
                prims[tile, plane, k, rows, :] = stage[k] * inverse
            prims[tile, plane, 4, rows, :] = (ADIABATIC - 1.0) * stage[5]
            prims[tile, plane, 5, rows, :] = stage[5] * inverse

    @functools.partial(each, 3)
    def _(plane):
        advance(0, plane, CHUNKS)
        advance(1, plane, (8, 16))

    @functools.partial(each, 2)
    def _(step):
        inner = pl.ds(pl.multiple_of(8 * step, 8), 8)
        rows = pl.ds(pl.multiple_of(8 * step + 8, 8), 8)
        outer = [[outer_prims[p, k, inner, :] for k in range(6)] for p in range(6)]
        column = (
            outer[0:3] + [[prims[0, p, k, rows, :] for k in range(6)] for p in range(3)] + outer[3:6]
        )
        flux = z_fluxes(column)
        for plane in range(3):
            for k in range(6):
                difference = flux[plane + 1][k] - flux[plane][k]
                if k == 5:
                    spread = 0.5 * (column[plane + 4][3] - column[plane + 2][3])
                    difference = difference + column[plane + 3][4] * spread
                updated[k, plane, inner, :] = -difference

    @functools.partial(each, 3)
    def _(plane):
        x_sweep(prims.at[0, plane], low_ref, high_ref, face_ref, flux_ref)
        for row in (8, 16):
            rows = pl.ds(row, 8)
            inner = pl.ds(row - 8, 8)
            both = [[prims[tile, plane, k, rows, :] for k in range(6)] for tile in range(2)]
            differences, spread = y_differences(*both)
            before = prims[0, plane, 1, pl.ds(row - 1, 8), :]
            after = prims[0, plane, 1, pl.ds(row + 1, 8), :]
            spread = spread[0] + 0.5 * (after - before)
            rate = []
            for k in range(6):
                across = flux_ref[k, rows, :] - flux_ref[k, pl.ds(row - 1, 8), :]
                rate.append(updated[k, plane, inner, :] - differences[0][k] - across)
            rate[5] = rate[5] - both[0][4] * spread
            stage = [section[plane, k, rows, :] for k in range(6)]
            drive = [force[0, 3 * k + plane, rows, :] for k in range(3)]
            rate = forced(stage, drive, rate)
            values = [fields[0, 3 * k + plane, rows, :] for k in range(7)]
            result = [
                0.5 * values[k] + 0.5 * (stage[k] + time_step * rate[k]) for k in range(6)
            ]
            settle(result, values[6], 1.0 / result[0])
            for k in range(6):
                updated[k, plane, inner, :] = result[k]
        pltpu.make_async_copy(updated.at[:, plane], out.at[:, plane], sent.at[plane]).start()

    for plane in range(3):
        pltpu.make_async_copy(updated.at[:, plane], out.at[:, plane], sent.at[plane]).wait()


def shape(*sizes):
    return jax.ShapeDtypeStruct(sizes, F32)


def vmem_specs(count):
    return [pl.BlockSpec(memory_space=pltpu.VMEM)] * count


def call(kernel, name, outs, arrays, scratch=(), cost=0, out_space=pltpu.VMEM):
    single = not isinstance(outs, tuple)
    out_spec = pl.BlockSpec(memory_space=out_space)
    return pl.pallas_call(
        kernel,
        out_shape=outs,
        in_specs=vmem_specs(len(arrays)),
        out_specs=out_spec if single else (out_spec,) * len(outs),
        scratch_shapes=list(scratch),
        compiler_params=pltpu.CompilerParams(vmem_limit_bytes=VMEM_LIMIT),
        cost_estimate=pl.CostEstimate(flops=cost, bytes_accessed=cost, transcendentals=0),
        name=name,
    )(*arrays)


def pairs(count, begin):
    table = []
    for first in range(begin, begin + count, 2):
        low, high = first % count, (first + 1) % count
        table += [(low, high), (high, low)]
    return table


def spread_over(rows, after, axes):
    return pl.pallas_call(
        spread_kernel,
        out_shape=shape(lax.axis_size(axes), 2, LANES),
        in_specs=[*vmem_specs(1), pl.BlockSpec(memory_space=pl.ANY)],
        out_specs=vmem_specs(1)[0],
        compiler_params=pltpu.CompilerParams(vmem_limit_bytes=VMEM_LIMIT),
        name="spread",
    )(rows, after)


def exchanged(spread, axes):
    return lax.all_to_all(spread, axes, 0, 0, tiled=True)


GX = ("zl", "core")
GY = ("y", "zh", "x")


def local(fluid_state, switch, z_edges, forcing):
    count_x = lax.axis_size(GX)
    count_y = lax.axis_size(GY)
    cells = 3.0 * ROWS * LANES * count_x * count_y
    tile = (8, LANES)
    block = (ROWS, LANES)
    inputs = (
        fluid_state.reshape(18, *block),
        switch,
        z_edges.reshape(EDGES, *block),
        forcing.reshape(FORCES, *block),
    )
    pair_out, odd_out, *arrays = pl.pallas_call(
        first_kernel,
        out_shape=(
            shape(X_TILES + 1, *tile),
            shape(X_TILES, *tile),
            *(jax.ShapeDtypeStruct(values.shape, values.dtype) for values in inputs),
        ),
        in_specs=[
            *([pl.BlockSpec(memory_space=pltpu.HBM)] * 4),
        ],
        out_specs=tuple(vmem_specs(6)),
        scratch_shapes=[pltpu.SemaphoreType.DMA((4,))],
        compiler_params=pltpu.CompilerParams(vmem_limit_bytes=VMEM_LIMIT),
        name="first",
    )(*(pltpu.with_memory_space_constraint(values, pltpu.HBM) for values in inputs))
    pair_in = lax.all_gather(pair_out, "core")
    rows = pair_in[:, X_TILES, 0:2]
    spread = spread_over(rows, rows, ("y", "x"))
    odd_out, spread = lax.optimization_barrier((odd_out, spread))
    odd_in = lax.ppermute(odd_out, GX, pairs(count_x, 1))
    totals = exchanged(spread, ("y", "x"))
    strips = call(
        second_kernel,
        "second",
        (shape(EXT + 2 * ROWS, LANES), shape(EXT + 2 * ROWS, LANES)),
        (*arrays, pair_in, odd_in),
        cost=4_000_000,
    )
    even_in = lax.ppermute(strips[0], GY, pairs(count_y, 0))
    odd_y_in = lax.ppermute(strips[1], GY, pairs(count_y, 1))
    totals = exchanged(spread_over(totals, even_in, ("zh", "zl")), ("zh", "zl"))
    extended = (EXT, LANES)
    work = [pltpu.VMEM((6, *extended), F32) for _ in range(4)]
    fields, force, push, tend, outer = call(
        third_kernel,
        "third",
        (
            shape(2, FIELDS, *extended),
            shape(2, FORCES, *extended),
            shape(2, 12, *extended),
            shape(2, 18, *extended),
            shape(6, 6, ROWS, LANES),
        ),
        (*arrays, pair_in, odd_in, even_in, odd_y_in),
        [
            pltpu.VMEM((2, 3, 6, *extended), F32),
            pltpu.VMEM((2, 6, 6, *extended), F32),
            *work,
            pltpu.VMEM((2, EXT + 2 * ROWS, LANES), F32),
        ],
        cost=60_000_000,
    )
    return call(
        functools.partial(fourth_kernel, cells),
        "fourth",
        shape(6, 3, ROWS, LANES),
        (totals, fields, force, push, tend, outer),
        [
            pltpu.VMEM((6, 3, ROWS, LANES), F32),
            pltpu.VMEM((3, 6, *extended), F32),
            pltpu.VMEM((2, 3, 6, *extended), F32),
            *work,
            pltpu.SemaphoreType.DMA((3,)),
        ],
        cost=8_000_000,
        out_space=pltpu.HBM,
    )


def solution(mesh):
    count_x, count_y = mesh.devices.shape
    count_z = 2 if count_y % 8 == 0 else 1
    parts = (count_x // 2, 2, count_y // (4 * count_z), count_z, 4)
    split = Mesh(mesh.devices.reshape(parts), (*GX, *GY))
    return jax.shard_map(
        local,
        mesh=split,
        in_specs=(
            P(None, None, GX, GY),
            P(None, GX, GY),
            P(None, None, None, GX, GY),
            P(None, None, GX, GY),
        ),
        out_specs=P(None, None, GX, GY),
        check_vma=False,
    )
```

```python
import functools

import jax
import jax.numpy as jnp
from jax import lax
from jax.experimental import pallas as pl
from jax.experimental.pallas import tpu as pltpu
from jax.sharding import Mesh
from jax.sharding import PartitionSpec as P

ADIABATIC = 5.0 / 3.0
CFL_NUMBER = 0.4
INJECTION = 0.04
LANES = 128
ROWS = 16
EXT = 32
FIELDS = 21
EDGES = 36
FORCES = 9
X_TILES = FIELDS + EDGES + FORCES
VMEM_LIMIT = 16 * 1024 * 1024
F32 = jnp.float32


def lane_index(shape):
    return lax.broadcasted_iota(jnp.int32, shape, len(shape) - 1)


def roll(values, shift, axis):
    size = values.shape[axis]
    shift = shift % size
    return values if shift == 0 else pltpu.roll(values, shift, axis)


def parities():
    return lax.axis_index("core"), lax.rem(lax.axis_index("x"), 2)


def each(count, body):
    def step(index, carry):
        body(index)
        return carry

    lax.fori_loop(0, count, step, 0)


def x_place(refs, index):
    state, switch, edges, forcing = refs
    if index < 18:
        return lambda rows: state[index, rows, :]
    index -= 18
    if index < 3:
        return lambda rows: switch[index, rows, :].astype(F32)
    index -= 3
    if index < EDGES:
        return lambda rows: edges[index, rows, :]
    index -= EDGES
    return lambda rows: forcing[index, rows, :]


def first_kernel(
    state_in, switch_in, edges_in, forcing_in,
    pair_out, odd_out, state, switch, edges, forcing, arrived,
):
    refs = (state, switch, edges, forcing)
    copies = [
        pltpu.make_async_copy(source, target, arrived.at[k])
        for k, (source, target) in enumerate(
            zip((state_in, switch_in, edges_in, forcing_in), refs, strict=True)
        )
    ]
    for k in (2, 0, 3, 1):
        copies[k].start()
    odd, _ = parities()
    near = pl.multiple_of(8 * (1 - odd), 8)
    far = pl.multiple_of(8 * odd, 8)
    for k in (0, 1, 3):
        copies[k].wait()
    peak = None
    total = None
    for plane in range(3):
        fields = [state[3 * k + plane] for k in range(6)]
        density = fields[0]
        inverse = 1.0 / density
        kinetic = 0.5 * inverse * (fields[1] ** 2 + fields[2] ** 2 + fields[3] ** 2)
        heat = jnp.where(switch[plane] == 1, fields[5], fields[4] - kinetic)
        sound = jnp.sqrt(ADIABATIC * (ADIABATIC - 1.0) * heat * inverse)
        speed = (
            jnp.abs(fields[1]) + jnp.abs(fields[2]) + jnp.abs(fields[3])
        ) * inverse + 3.0 * sound
        drive = [forcing[3 * k + plane] for k in range(3)]
        power = density * (drive[0] ** 2 + drive[1] ** 2 + drive[2] ** 2)
        peak = speed if peak is None else jnp.maximum(peak, speed)
        total = power if total is None else total + power
    row = lax.broadcasted_iota(jnp.int32, (8, LANES), 0)
    pair_out[X_TILES] = jnp.where(row == 0, jnp.max(peak), jnp.sum(total))
    copies[2].wait()
    for index in range(X_TILES):
        tile = x_place(refs, index)
        pair_out[index] = tile(pl.ds(near, 8))
        odd_out[index] = tile(pl.ds(far, 8))


def spread_kernel(rows, after, out):
    peak = jnp.max(rows[:, 0, :], axis=0, keepdims=True)
    total = jnp.sum(rows[:, 1, :], axis=0, keepdims=True)
    joined = jnp.concatenate([peak, total], axis=0)
    out[...] = jnp.broadcast_to(joined[None], out.shape)


def rows_around(odd_x, pair_in, odd_in, index, block):
    from_pair = pair_in[1 - odd_x, index]
    from_odd = odd_in[index]
    below = jnp.where(odd_x == 0, from_odd, from_pair)
    above = jnp.where(odd_x == 0, from_pair, from_odd)
    return jnp.concatenate([below, block, above], axis=0)


def turned(values, shift):
    return pltpu.roll(values, lax.rem(shift + LANES, LANES), 1)


def second_kernel(state, switch, edges, forcing, pair_in, odd_in, even_out, odd_out):
    odd_x, odd_y = parities()
    lane = lane_index((EXT, LANES))
    high = jnp.zeros((EXT, LANES), F32)
    low = jnp.zeros((EXT, LANES), F32)
    for index in range(FIELDS):
        block = x_place((state, switch, edges, forcing), index)(slice(0, ROWS))
        column = rows_around(odd_x, pair_in, odd_in, index, block)
        mine = (lane >= 6 * index) & (lane < 6 * index + 6)
        high = jnp.where(mine, roll(column, 6 * index - 122, 1), high)
        low = jnp.where(mine, roll(column, 6 * index, 1), low)
    even_out[0:EXT] = jnp.where(odd_y == 0, high, low)
    odd_out[0:EXT] = jnp.where(odd_y == 0, low, high)
    lane = lane[0:ROWS]
    for source, count, row in ((edges, EDGES, EXT), (forcing, FORCES, EXT + ROWS)):
        high = jnp.zeros((ROWS, LANES), F32)
        low = jnp.zeros((ROWS, LANES), F32)
        for index in range(count):
            mine = (lane >= 3 * index) & (lane < 3 * index + 3)
            high = jnp.where(mine, roll(source[index], 3 * index - 125, 1), high)
            low = jnp.where(mine, roll(source[index], 3 * index, 1), low)
        even_out[row : row + ROWS] = jnp.where(odd_y == 0, high, low)
        odd_out[row : row + ROWS] = jnp.where(odd_y == 0, low, high)


def median(one, two, three):
    return jnp.maximum(jnp.minimum(one, two), jnp.minimum(jnp.maximum(one, two), three))


def face_above(before, here, after, beyond):
    value = (7.0 / 12.0) * (here + after) - (1.0 / 12.0) * (before + beyond)
    return median(here, after, value)


def limited(here, face_low, face_high):
    thrice = 3.0 * here
    return (
        median(here, face_low, thrice - (face_high + face_high)),
        median(here, face_high, thrice - (face_low + face_low)),
    )


def sound_of(state):
    push = ADIABATIC * state[4]
    return push * lax.rsqrt(push * state[0])


def face_flux(left, right, normal):
    left_u, right_u = left[1 + normal], right[1 + normal]
    left_sound, right_sound = sound_of(left), sound_of(right)
    slow = jnp.minimum(jnp.minimum(left_u - left_sound, right_u - right_sound), 0.0)
    fast = jnp.maximum(jnp.maximum(left_u + left_sound, right_u + right_sound), 0.0)
    share = 1.0 / (fast - slow)
    left_part = fast * share
    right_part = -slow * share
    left_lead = left_u - slow
    right_lead = right_u - fast
    left_mass = left_part * left_lead * left[0]
    right_mass = right_part * right_lead * right[0]
    left_square = left[1] * left[1] + left[2] * left[2] + left[3] * left[3]
    right_square = right[1] * right[1] + right[2] * right[2] + right[3] * right[3]
    flux = [left_mass + right_mass]
    for k in (1, 2, 3):
        flux.append(left_mass * left[k] + right_mass * right[k])
    left_push = left_part * left[4]
    right_push = right_part * right[4]
    flux[1 + normal] = flux[1 + normal] + (left_push + right_push)
    flux.append(
        0.5 * (left_mass * left_square + right_mass * right_square)
        + left_push * (1.5 * left_lead + left_u)
        + right_push * (1.5 * right_lead + right_u)
    )
    flux.append(left_mass * left[5] + right_mass * right[5])
    return flux


def z_fluxes(planes):
    lower, upper = [], []
    for k in range(6):
        column = [planes[j][k] for j in range(9)]
        faces = [face_above(*column[j : j + 4]) for j in range(6)]
        cells = [limited(column[j + 2], faces[j], faces[j + 1]) for j in range(5)]
        lower.append([cells[j][1] for j in range(4)])
        upper.append([cells[j + 1][0] for j in range(4)])
    return [
        face_flux([lower[k][j] for k in range(6)], [upper[k][j] for k in range(6)], 2)
        for j in range(4)
    ]


def edge_primitives(fields):
    density = fields[0]
    inverse = 1.0 / density
    kinetic = 0.5 * inverse * (fields[1] ** 2 + fields[2] ** 2 + fields[3] ** 2)
    return [
        density,
        fields[1] * inverse,
        fields[2] * inverse,
        fields[3] * inverse,
        (ADIABATIC - 1.0) * (fields[4] - kinetic),
        fields[5] * inverse,
    ]


def shift_pair(main, rim, step):
    lane = lane_index(main.shape)
    main_rolled = roll(main, -step, 1)
    rim_rolled = roll(rim, -step, 1)
    inside = lane < LANES - step if step > 0 else lane >= -step
    return (
        jnp.where(inside, main_rolled, rim_rolled),
        jnp.where(inside, rim_rolled, main_rolled),
    )


def y_differences(main, rim):
    lows, highs = ([], []), ([], [])
    spread = None
    for k in range(6):
        here = (main[k], rim[k])
        before = shift_pair(*here, -1)
        after = shift_pair(*here, 1)
        beyond = shift_pair(*here, 2)
        faces = [face_above(before[j], here[j], after[j], beyond[j]) for j in range(2)]
        below = shift_pair(*faces, -1)
        cells = [limited(here[j], below[j], faces[j]) for j in range(2)]
        nexts = shift_pair(cells[0][0], cells[1][0], 1)
        for j in range(2):
            lows[j].append(cells[j][1])
            highs[j].append(nexts[j])
        if k == 2:
            spread = [0.5 * (after[j] - before[j]) for j in range(2)]
    fluxes = [face_flux(lows[j], highs[j], 1) for j in range(2)]
    differences = ([], [])
    for k in range(6):
        below = shift_pair(fluxes[0][k], fluxes[1][k], -1)
        for j in range(2):
            differences[j].append(fluxes[j][k] - below[j])
    return differences, spread


CHUNKS = (4, 12, 20)


def x_sweep(prims, low_ref, high_ref, face_ref, flux_ref):
    for row in CHUNKS:
        for k in range(6):
            before, here, after, beyond = [
                prims[k, pl.ds(row + s, 8), :] for s in (-1, 0, 1, 2)
            ]
            if row == CHUNKS[0]:
                below = face_above(prims[k, pl.ds(row - 2, 8), :], before, here, after)
            above = face_above(before, here, after, beyond)
            face_ref[k, pl.ds(row, 8), :] = above
            if row != CHUNKS[0]:
                below = face_ref[k, pl.ds(row - 1, 8), :]
            low_ref[k, pl.ds(row, 8), :], high_ref[k, pl.ds(row, 8), :] = limited(
                here, below, above
            )
    for row in CHUNKS:
        left = [high_ref[k, pl.ds(row, 8), :] for k in range(6)]
        right = [low_ref[k, pl.ds(row + 1, 8), :] for k in range(6)]
        flux = face_flux(left, right, 0)
        for k in range(6):
            flux_ref[k, pl.ds(row, 8), :] = flux[k]


def clear_ends(low_ref, flux_ref):
    for k in range(6):
        low_ref[k, pl.ds(28, 4), :] = jnp.ones((4, LANES), F32)
        flux_ref[k, pl.ds(0, 4), :] = jnp.zeros((4, LANES), F32)


def third_kernel(
    state, switch, edges, forcing, pair_in, odd_in, even_in, odd_y_in,
    fields, force, tend, outer, prims, planes, low_ref, high_ref, face_ref, flux_ref, strip_ref,
):
    odd_x, odd_y = parities()
    strip_ref[0] = jnp.where(odd_y == 0, even_in[...], odd_y_in[...])
    strip_ref[1] = jnp.where(odd_y == 0, odd_y_in[...], even_in[...])
    clear_ends(low_ref, flux_ref)
    lane = lane_index((EXT, LANES))
    edge_lane = lane[0:ROWS]

    def field_tiles(index, block):
        fields[0, index] = rows_around(odd_x, pair_in, odd_in, index, block)
        fields[1, index] = jnp.where(
            lane < 64,
            turned(strip_ref[0, 0:EXT], -6 * index),
            turned(strip_ref[1, 0:EXT], 122 - 6 * index),
        )

    def rim_tile(row, index):
        return jnp.where(
            edge_lane < 64,
            turned(strip_ref[0, row : row + ROWS], -3 * index),
            turned(strip_ref[1, row : row + ROWS], 125 - 3 * index),
        )

    @functools.partial(each, 6)
    def _(field):
        for plane in range(3):
            index = 3 * field + plane
            field_tiles(index, state[index])

    for plane in range(3):
        field_tiles(18 + plane, switch[plane].astype(F32))

    @functools.partial(each, 3)
    def _(part):
        for k in range(3):
            index = 3 * part + k
            force[0, index] = rows_around(
                odd_x, pair_in, odd_in, FIELDS + EDGES + index, forcing[index]
            )
            force[1, index, 0:8] = jnp.zeros((8, LANES), F32)
            force[1, index, 8:24] = rim_tile(EXT + ROWS, index)
            force[1, index, 24:32] = jnp.zeros((8, LANES), F32)

    @functools.partial(each, 6)
    def _(step):
        tile, plane = step // 3, step % 3
        values = [fields[tile, 3 * k + plane] for k in range(7)]
        density = values[0]
        inverse = 1.0 / density
        kinetic = 0.5 * inverse * (values[1] ** 2 + values[2] ** 2 + values[3] ** 2)
        heat = jnp.where(values[6] == 1.0, values[5], values[4] - kinetic)
        prims[tile, plane, 0] = density
        for k in (1, 2, 3):
            prims[tile, plane, k] = values[k] * inverse
        prims[tile, plane, 4] = (ADIABATIC - 1.0) * heat
        prims[tile, plane, 5] = values[5] * inverse

    @functools.partial(each, 6)
    def _(step):
        first = 18 * (step // 3) + step % 3
        places = [first + 3 * k for k in range(6)]
        values = edge_primitives(
            [rows_around(odd_x, pair_in, odd_in, FIELDS + k, edges[k]) for k in places]
        )
        for k in range(6):
            planes[0, step, k] = values[k]
            outer[step, k] = values[k][8:24]
        values = edge_primitives([rim_tile(EXT, k) for k in places])
        for k in range(6):
            planes[1, step, k, 0:8] = jnp.ones((8, LANES), F32)
            planes[1, step, k, 8:24] = values[k]
            planes[1, step, k, 24:32] = jnp.ones((8, LANES), F32)

    @functools.partial(each, 3)
    def _(plane):
        for row in CHUNKS:
            rows = pl.ds(row, 8)
            both = [[prims[tile, plane, k, rows, :] for k in range(6)] for tile in range(2)]
            differences, spread = y_differences(*both)
            for tile in range(2):
                for k in range(5):
                    tend[tile, 3 * k + plane, rows, :] = -differences[tile][k]
                tend[tile, 15 + plane, rows, :] = (
                    -differences[tile][5] - both[tile][4] * spread[tile]
                )

    @functools.partial(each, 6)
    def _(step):
        tile, plane = step // 3, step % 3
        x_sweep(prims.at[tile, plane], low_ref, high_ref, face_ref, flux_ref)
        for row in CHUNKS:
            rows = pl.ds(row, 8)
            for k in range(6):
                difference = flux_ref[k, rows, :] - flux_ref[k, pl.ds(row - 1, 8), :]
                if k == 5:
                    before = prims[tile, plane, 1, pl.ds(row - 1, 8), :]
                    after = prims[tile, plane, 1, pl.ds(row + 1, 8), :]
                    spread = 0.5 * (after - before)
                    difference = difference + prims[tile, plane, 4, rows, :] * spread
                tend[tile, 3 * k + plane, rows, :] -= difference

    @functools.partial(each, 2)
    def _(tile):
        for row in CHUNKS:
            rows = pl.ds(row, 8)
            column = (
                [[planes[tile, p, k, rows, :] for k in range(6)] for p in range(3)]
                + [[prims[tile, p, k, rows, :] for k in range(6)] for p in range(3)]
                + [[planes[tile, 3 + p, k, rows, :] for k in range(6)] for p in range(3)]
            )
            flux = z_fluxes(column)
            for plane in range(3):
                for k in range(6):
                    difference = flux[plane + 1][k] - flux[plane][k]
                    if k == 5:
                        spread = 0.5 * (column[plane + 4][3] - column[plane + 2][3])
                        difference = difference + column[plane + 3][4] * spread
                    tend[tile, 3 * k + plane, rows, :] -= difference


def fourth_kernel(
    cells, totals, fields, force, tend, outer_prims, out,
    updated, section, prims, low_ref, high_ref, face_ref, flux_ref, sent,
):
    peak = jnp.max(totals[:, 0, :], axis=0, keepdims=True)
    power = jnp.sum(totals[:, 1, :], axis=0, keepdims=True)
    time_step = CFL_NUMBER / peak
    scale = jnp.sqrt(INJECTION / (0.5 * time_step * (power / cells + 1e-06)))
    clear_ends(low_ref, flux_ref)

    def forced(values, drive, tendency):
        result = list(tendency)
        for k in (1, 2, 3):
            result[k] = result[k] + scale * values[0] * drive[k - 1]
        result[4] = result[4] + scale * (
            values[1] * drive[0] + values[2] * drive[1] + values[3] * drive[2]
        )
        return result

    def settle(values, switch, inverse):
        kinetic = 0.5 * inverse * (values[1] ** 2 + values[2] ** 2 + values[3] ** 2)
        values[5] = jnp.where(switch == 0.0, values[4] - kinetic, values[5])

    def advance(tile, plane, chunks):
        for row in chunks:
            rows = pl.ds(row, 8)
            values = [fields[tile, 3 * k + plane, rows, :] for k in range(7)]
            drive = [force[tile, 3 * k + plane, rows, :] for k in range(3)]
            rate = forced(values, drive, [tend[tile, 3 * k + plane, rows, :] for k in range(6)])
            stage = [values[k] + time_step * rate[k] for k in range(6)]
            inverse = 1.0 / stage[0]
            settle(stage, values[6], inverse)
            if tile == 0:
                for k in range(6):
                    section[plane, k, rows, :] = stage[k]
            prims[tile, plane, 0, rows, :] = stage[0]
            for k in (1, 2, 3):
                prims[tile, plane, k, rows, :] = stage[k] * inverse
            prims[tile, plane, 4, rows, :] = (ADIABATIC - 1.0) * stage[5]
            prims[tile, plane, 5, rows, :] = stage[5] * inverse

    @functools.partial(each, 3)
    def _(plane):
        advance(0, plane, CHUNKS)
        advance(1, plane, (8, 16))

    @functools.partial(each, 2)
    def _(step):
        inner = pl.ds(pl.multiple_of(8 * step, 8), 8)
        rows = pl.ds(pl.multiple_of(8 * step + 8, 8), 8)
        outer = [[outer_prims[p, k, inner, :] for k in range(6)] for p in range(6)]
        column = (
            outer[0:3] + [[prims[0, p, k, rows, :] for k in range(6)] for p in range(3)] + outer[3:6]
        )
        flux = z_fluxes(column)
        for plane in range(3):
            for k in range(6):
                difference = flux[plane + 1][k] - flux[plane][k]
                if k == 5:
                    spread = 0.5 * (column[plane + 4][3] - column[plane + 2][3])
                    difference = difference + column[plane + 3][4] * spread
                updated[k, plane, inner, :] = -difference

    @functools.partial(each, 3)
    def _(plane):
        x_sweep(prims.at[0, plane], low_ref, high_ref, face_ref, flux_ref)
        for row in (8, 16):
            rows = pl.ds(row, 8)
            inner = pl.ds(row - 8, 8)
            both = [[prims[tile, plane, k, rows, :] for k in range(6)] for tile in range(2)]
            differences, spread = y_differences(*both)
            before = prims[0, plane, 1, pl.ds(row - 1, 8), :]
            after = prims[0, plane, 1, pl.ds(row + 1, 8), :]
            spread = spread[0] + 0.5 * (after - before)
            rate = []
            for k in range(6):
                across = flux_ref[k, rows, :] - flux_ref[k, pl.ds(row - 1, 8), :]
                rate.append(updated[k, plane, inner, :] - differences[0][k] - across)
            rate[5] = rate[5] - both[0][4] * spread
            stage = [section[plane, k, rows, :] for k in range(6)]
            drive = [force[0, 3 * k + plane, rows, :] for k in range(3)]
            rate = forced(stage, drive, rate)
            values = [fields[0, 3 * k + plane, rows, :] for k in range(7)]
            result = [
                0.5 * values[k] + 0.5 * (stage[k] + time_step * rate[k]) for k in range(6)
            ]
            settle(result, values[6], 1.0 / result[0])
            for k in range(6):
                updated[k, plane, inner, :] = result[k]
        pltpu.make_async_copy(updated.at[:, plane], out.at[:, plane], sent.at[plane]).start()

    for plane in range(3):
        pltpu.make_async_copy(updated.at[:, plane], out.at[:, plane], sent.at[plane]).wait()


def shape(*sizes):
    return jax.ShapeDtypeStruct(sizes, F32)


def vmem_specs(count):
    return [pl.BlockSpec(memory_space=pltpu.VMEM)] * count


def call(kernel, name, outs, arrays, scratch=(), cost=0, out_space=pltpu.VMEM):
    single = not isinstance(outs, tuple)
    out_spec = pl.BlockSpec(memory_space=out_space)
    return pl.pallas_call(
        kernel,
        out_shape=outs,
        in_specs=vmem_specs(len(arrays)),
        out_specs=out_spec if single else (out_spec,) * len(outs),
        scratch_shapes=list(scratch),
        compiler_params=pltpu.CompilerParams(vmem_limit_bytes=VMEM_LIMIT),
        cost_estimate=pl.CostEstimate(flops=cost, bytes_accessed=cost, transcendentals=0),
        name=name,
    )(*arrays)


def pairs(count, begin):
    table = []
    for first in range(begin, begin + count, 2):
        low, high = first % count, (first + 1) % count
        table += [(low, high), (high, low)]
    return table


def spread_over(rows, after, axes):
    return pl.pallas_call(
        spread_kernel,
        out_shape=shape(lax.axis_size(axes), 2, LANES),
        in_specs=[*vmem_specs(1), pl.BlockSpec(memory_space=pl.ANY)],
        out_specs=vmem_specs(1)[0],
        compiler_params=pltpu.CompilerParams(vmem_limit_bytes=VMEM_LIMIT),
        name="spread",
    )(rows, after)


def exchanged(spread, axes):
    return lax.all_to_all(spread, axes, 0, 0, tiled=True)


GX = ("zl", "core")
GY = ("y", "zh", "x")


def local(fluid_state, switch, z_edges, forcing):
    count_x = lax.axis_size(GX)
    count_y = lax.axis_size(GY)
    cells = 3.0 * ROWS * LANES * count_x * count_y
    tile = (8, LANES)
    block = (ROWS, LANES)
    inputs = (
        fluid_state.reshape(18, *block),
        switch,
        z_edges.reshape(EDGES, *block),
        forcing.reshape(FORCES, *block),
    )
    pair_out, odd_out, *arrays = pl.pallas_call(
        first_kernel,
        out_shape=(
            shape(X_TILES + 1, *tile),
            shape(X_TILES, *tile),
            *(jax.ShapeDtypeStruct(values.shape, values.dtype) for values in inputs),
        ),
        in_specs=[
            *([pl.BlockSpec(memory_space=pltpu.HBM)] * 4),
        ],
        out_specs=tuple(vmem_specs(6)),
        scratch_shapes=[pltpu.SemaphoreType.DMA((4,))],
        compiler_params=pltpu.CompilerParams(vmem_limit_bytes=VMEM_LIMIT),
        name="first",
    )(*(pltpu.with_memory_space_constraint(values, pltpu.HBM) for values in inputs))
    pair_in = lax.all_gather(pair_out, "core")
    odd_out, pair_in = lax.optimization_barrier((odd_out, pair_in))
    odd_in = lax.ppermute(odd_out, GX, pairs(count_x, 1))
    rows = pair_in[:, X_TILES, 0:2]
    spread = spread_over(rows, rows, ("y", "x"))
    totals = exchanged(spread, ("y", "x"))
    strips = call(
        second_kernel,
        "second",
        (shape(EXT + 2 * ROWS, LANES), shape(EXT + 2 * ROWS, LANES)),
        (*arrays, pair_in, odd_in),
        cost=4_000_000,
    )
    even_in = lax.ppermute(strips[0], GY, pairs(count_y, 0))
    odd_y_in = lax.ppermute(strips[1], GY, pairs(count_y, 1))
    totals = exchanged(spread_over(totals, even_in, ("zh", "zl")), ("zh", "zl"))
    extended = (EXT, LANES)
    work = [pltpu.VMEM((6, *extended), F32) for _ in range(4)]
    fields, force, tend, outer = call(
        third_kernel,
        "third",
        (
            shape(2, FIELDS, *extended),
            shape(2, FORCES, *extended),
            shape(2, 18, *extended),
            shape(6, 6, ROWS, LANES),
        ),
        (*arrays, pair_in, odd_in, even_in, odd_y_in),
        [
            pltpu.VMEM((2, 3, 6, *extended), F32),
            pltpu.VMEM((2, 6, 6, *extended), F32),
            *work,
            pltpu.VMEM((2, EXT + 2 * ROWS, LANES), F32),
        ],
        cost=60_000_000,
    )
    return call(
        functools.partial(fourth_kernel, cells),
        "fourth",
        shape(6, 3, ROWS, LANES),
        (totals, fields, force, tend, outer),
        [
            pltpu.VMEM((6, 3, ROWS, LANES), F32),
            pltpu.VMEM((3, 6, *extended), F32),
            pltpu.VMEM((2, 3, 6, *extended), F32),
            *work,
            pltpu.SemaphoreType.DMA((3,)),
        ],
        cost=8_000_000,
        out_space=pltpu.HBM,
    )


def solution(mesh):
    count_x, count_y = mesh.devices.shape
    count_z = 2 if count_y % 8 == 0 else 1
    parts = (count_x // 2, 2, count_y // (4 * count_z), count_z, 4)
    split = Mesh(mesh.devices.reshape(parts), (*GX, *GY))
    return jax.shard_map(
        local,
        mesh=split,
        in_specs=(
            P(None, None, GX, GY),
            P(None, GX, GY),
            P(None, None, None, GX, GY),
            P(None, None, GX, GY),
        ),
        out_specs=P(None, None, GX, GY),
        check_vma=False,
    )
```
